32 devices in a mesh: dom: 16 (over z, y, x), slab: 2 (over core).
Axes of the slice: x: 2, y: 2, z: 4, core: 2. Of those that a mesh axis runs over, the one named last changes fastest.
Arguments:
- positions: float32 [32768, 3], P(('dom', 'slab')), may hold values from 0 to 20
- species: int32 [32768], P(('dom', 'slab')), may hold values from 0 to 9
- send_pick: int32 [512, 64], P(('dom', 'slab')), may hold values from -1 to 1023, as said below
- ghost_pick: int32 [128, 384], P(('dom', 'slab')), may hold values from 0 to 1023
- near_tiles: int32 [512, 4], P(('dom', 'slab')), may hold values from 0 to 39
- embedding: bfloat16 [10, 128], replicated, may hold values from -6 to 6
- radial_weight: bfloat16 [2, 8, 128], replicated, may hold values from -6 to 6
- update_weight: bfloat16 [2, 512, 128], replicated, may hold values from -0.25 to 0.25
- force_weight: bfloat16 [128, 128], replicated, may hold values from -0.5 to 0.5
Outputs:
- features: bfloat16 [32768, 128], P(('dom', 'slab'))
- forces: float32 [3, 32768], P(None, ('dom', 'slab'))
The draws below stay inside these ranges and needn't reach their ends.
Inputs may be any that keep to these rules, and one draw needn't show every extreme that they name: `send_pick`: for each domain, a block of 16 x 64; each old row appears at most once in its domain's block; live slots of a destination come first; in every domain some destination is full, and for each slab index one destination along dom receives full slots from every source. `ghost_pick`: ghost rows may repeat. `near_tiles`: tiles index the pool of 64-row tiles and may repeat.
All inputs are finite; a program needn't handle non-finite values.
Results may differ from the reference program's by a relative error of at most 0.0062.
Values may be sent and summed in bfloat16 or wider, within the bound.
No kernel may reach another device: no remote copies, remote signals or barrier semaphores. Data moves between devices by JAX's collectives and lax.ppermute only.
A program may use at most 64 MiB of HBM per device.

```python
import jax
import jax.numpy as jnp
from jax import lax

CHANNELS = 128
NBASIS = 8
NSPECIES = 10
LAYERS = 2
TILE = 64
NEAR = 4
ATOM_DEV = 1024
GHOST = 384
CAP = 64
LOCAL_TILES = 16
POOL_TILES = 40
TOTAL = 32768
N_DOM = 16
N_SLAB = 2


def draw_send_pick(key, part):
    first, second, third, fourth = jax.random.split(key, 4)
    devices = N_DOM * N_SLAB
    orders = jax.vmap(lambda sub: jax.random.permutation(sub, ATOM_DEV))(jax.random.split(first, devices))
    orders = orders.reshape(N_DOM, N_SLAB, N_DOM, CAP).astype(jnp.int32)
    counts = jax.random.randint(second, (N_DOM, N_SLAB, N_DOM), CAP // 4, CAP + 1)
    target = jnp.arange(N_DOM)
    full_one = jax.random.randint(third, (N_DOM, N_SLAB), 0, N_DOM)
    counts = jnp.where(target[None, None, :] == full_one[:, :, None], CAP, counts)
    hotter = jax.random.randint(fourth, (N_SLAB,), 0, N_DOM)
    counts = jnp.where(target[None, None, :] == hotter[None, :, None], CAP, counts)
    slots = jnp.arange(CAP)
    living = slots[None, None, None, :] < counts[..., None]
    return jnp.where(living, orders, -1).reshape(N_DOM * N_SLAB * N_DOM, CAP).astype(jnp.int32)


def with_ends(entries, rng, least, high):
    longest = entries.shape.index(max(entries.shape))
    spots = []
    for shift in (0, 1):
        where = [jax.random.randint(jax.random.fold_in(rng, axis), (), 0, length) for axis, length in enumerate(entries.shape)]
        where[longest] = (where[longest] + shift) % entries.shape[longest]
        spots.append(tuple(where))
    return entries.at[spots[0]].set(least).at[spots[1]].set(high)


def shard_levels(stream_key, dims, cuts, least, high):
    level, own = 1.0, jax.random.fold_in(stream_key, 6)
    for dim, shards_of in cuts:
        draws = jnp.exp(jax.random.uniform(jax.random.fold_in(own, dim), (shards_of,), jnp.float32, least / len(cuts), high / len(cuts)))
        level = level * jnp.repeat(draws, dims[dim] // shards_of).reshape([-1 if axis == dim else 1 for axis in range(len(dims))])
    return level


def centred(key, extent, scale, bound, held_as=jnp.bfloat16):
    values = scale * jax.random.normal(key, extent, jnp.float32)
    return jnp.clip(values, min=-bound, max=bound).astype(held_as)


def setup_inputs(seed: int = 0) -> dict:
    keys = jax.random.split(jax.random.key(seed), 10)
    positions = jnp.clip(20.0 * jax.random.uniform(keys[0], (TOTAL, 3), jnp.float32) ** shard_levels(keys[0], (TOTAL, 3), ((0, 32),), -0.2, 0.2), 0.0, 20.0)
    species = with_ends(jax.random.randint(keys[1], (TOTAL,), 0, NSPECIES), jax.random.fold_in(keys[1], 1), 0, NSPECIES - 1).astype(jnp.int32)
    send_pick = draw_send_pick(jax.random.fold_in(keys[9], 71), 0)
    ghost_pick = with_ends(jax.random.randint(keys[3], (N_DOM * N_SLAB * 4, GHOST), 0, ATOM_DEV), jax.random.fold_in(keys[3], 1), 0, ATOM_DEV - 1).astype(jnp.int32)
    near_tiles = with_ends(jax.random.randint(keys[4], (N_DOM * N_SLAB * LOCAL_TILES, NEAR), 0, POOL_TILES), jax.random.fold_in(keys[4], 1), 0, POOL_TILES - 1).astype(jnp.int32)
    embedding = centred(keys[5], (NSPECIES, CHANNELS), 1.0, 6.0)
    radial_weight = centred(keys[6], (LAYERS, NBASIS, CHANNELS), 1.0, 6.0)
    update_weight = centred(keys[7], (LAYERS, 4 * CHANNELS, CHANNELS), (4 * CHANNELS) ** -0.5, 0.25)
    force_weight = centred(keys[8], (CHANNELS, CHANNELS), CHANNELS ** -0.5, 0.5)
    return dict(positions=positions, species=species, send_pick=send_pick, ghost_pick=ghost_pick, near_tiles=near_tiles, embedding=embedding, radial_weight=radial_weight, update_weight=update_weight, force_weight=force_weight)


cutoff = 6.0
softening = 0.25

def geometry(pos_t, live, rows_i, rows_j):
    offset = pos_t[:, rows_j][:, None, :] - pos_t[:, rows_i][:, :, None]
    distance = jnp.sqrt(lax.optimization_barrier(jnp.sum(offset * offset, axis=0)) + softening)
    ratio = distance / cutoff
    envelope = jnp.where(ratio < 1.0, (1.0 - ratio * ratio) ** 2, 0.0)
    keep = live[rows_i][:, None] * live[rows_j][None, :] * (rows_i[:, None] != rows_j[None, :]).astype(live.dtype)
    return (offset, distance, envelope * keep)

def edge_terms(offset, distance, weight):
    unit = offset / distance[None]
    along_x, along_y, along_z = (unit[0], unit[1], unit[2])
    harmonic = jnp.stack([jnp.ones_like(along_x), along_x, along_y, along_z, along_x * along_y, along_y * along_z, along_z * along_x, along_x * along_x - along_y * along_y, 3.0 * along_z * along_z - 1.0])
    orders = jnp.arange(1, NBASIS + 1).astype(distance.dtype)
    radial = jnp.sin(orders[:, None, None] * (jnp.pi / cutoff) * distance[None]) / distance[None] * weight[None]
    return (harmonic[:, None] * radial[None]).astype(jnp.bfloat16)

def layer_device(pos_t, live, h_pool, near, radial_w, update_w):
    weighted = (h_pool.astype(jnp.float32)[None] * radial_w.astype(jnp.float32)[:, None, :]).astype(jnp.bfloat16)
    span = jnp.arange(TILE).astype(jnp.int32)
    scale = 1.0 / TILE ** 0.5

    def one(index):
        rows_i = index * TILE + span
        rows_j = (near[index][:, None] * TILE + span[None]).reshape(-1)
        offset, distance, weight = geometry(pos_t, live, rows_i, rows_j)
        edges = edge_terms(offset, distance, weight)
        gathered = weighted[:, rows_j]
        agg = jnp.einsum('lnij,njc->ilc', edges.astype(jnp.float32), gathered.astype(jnp.float32)) * scale
        square = agg * agg
        query = jnp.concatenate([agg[:, 0], square[:, 0], lax.optimization_barrier(jnp.sum(square[:, 1:4], axis=1)), lax.optimization_barrier(jnp.sum(square[:, 4:9], axis=1))], axis=1).astype(jnp.bfloat16)
        update = jnp.dot(query, update_w, preferred_element_type=jnp.float32)
        before = h_pool[rows_i].astype(jnp.float32)
        return ((before + jax.nn.silu(update)) * live[rows_i][:, None]).astype(jnp.bfloat16)
    return lax.map(one, jnp.arange(LOCAL_TILES).astype(jnp.int32)).reshape(ATOM_DEV, CHANNELS)

def force_device(pos_t, live, g_pool, near):
    span = jnp.arange(TILE).astype(jnp.int32)
    scale = 1.0 / CHANNELS ** 0.5

    def step(total, index):
        rows_i = index * TILE + span
        rows_j = (near[index][:, None] * TILE + span[None]).reshape(-1)
        offset, distance, weight = geometry(pos_t, live, rows_i, rows_j)
        inner = jnp.dot(g_pool[rows_i], g_pool[rows_j].T, preferred_element_type=jnp.float32)
        strength = weight / distance * inner * scale
        pair = strength[None] * offset
        total = total.at[:, rows_j].add(-lax.optimization_barrier(jnp.sum(pair, axis=1)))
        return (total, lax.optimization_barrier(jnp.sum(pair, axis=2)))
    start = jnp.zeros((3, g_pool.shape[0]), jnp.float32)
    total, own = lax.scan(step, start, jnp.arange(LOCAL_TILES).astype(jnp.int32))
    local = own.transpose(1, 0, 2).reshape(3, ATOM_DEV) + total[:, :ATOM_DEV]
    return (local, total[:, ATOM_DEV:])

def reference(positions, species, send_pick, ghost_pick, near_tiles, embedding, radial_weight, update_weight, force_weight):
    state = jnp.concatenate([positions, jnp.ones((TOTAL, 1), positions.dtype), species.astype(positions.dtype)[:, None]], axis=1).reshape(N_DOM, N_SLAB, ATOM_DEV, 5)
    pick = send_pick.reshape(N_DOM, N_SLAB, N_DOM, CAP)
    taken = jax.vmap(jax.vmap(lambda rows, idx: rows[jnp.maximum(idx, 0)]))(state, pick)
    sent = taken * (pick >= 0).astype(positions.dtype)[..., None]
    moved = sent.transpose(2, 1, 0, 3, 4).reshape(N_DOM, N_SLAB, ATOM_DEV, 5)
    gpick = ghost_pick.reshape(N_DOM, N_SLAB, 4, GHOST)

    def ghosts(rows):
        out = jax.vmap(jax.vmap(lambda arr, idx: arr[idx]))(rows, gpick)
        blocks = [jnp.roll(out[:, :, 0], 1, 0), jnp.roll(out[:, :, 1], -1, 0), jnp.roll(out[:, :, 2], 1, 1), jnp.roll(out[:, :, 3], -1, 1)]
        extra = jnp.stack(blocks, 2).reshape((N_DOM, N_SLAB, 4 * GHOST) + rows.shape[3:])
        return jnp.concatenate([rows, extra], axis=2)
    pool = ghosts(moved)
    devices = N_DOM * N_SLAB
    pool_rows = ATOM_DEV + 4 * GHOST
    pos_t = pool[..., :3].reshape(devices, pool_rows, 3).transpose(0, 2, 1)
    live = pool[..., 3].reshape(devices, pool_rows)
    kinds = moved[..., 4].astype(jnp.int32)
    hidden = embedding[kinds]
    near = near_tiles.reshape(devices, LOCAL_TILES, NEAR)
    for level in range(LAYERS):
        h_pool = ghosts(hidden).reshape(devices, pool_rows, CHANNELS)
        fresh = lax.map(lambda item: layer_device(item[0], item[1], item[2], item[3], radial_weight[level], update_weight[level]), (pos_t, live, h_pool, near))
        hidden = fresh.reshape(N_DOM, N_SLAB, ATOM_DEV, CHANNELS)
    projected = jnp.dot(hidden.reshape(TOTAL, CHANNELS), force_weight, preferred_element_type=jnp.float32).astype(jnp.bfloat16)
    g_pool = ghosts(projected.reshape(N_DOM, N_SLAB, ATOM_DEV, CHANNELS)).reshape(devices, pool_rows, CHANNELS)
    local, outer = lax.map(lambda item: force_device(item[0], item[1], item[2], item[3]), (pos_t, live, g_pool, near))
    local = local.reshape(N_DOM, N_SLAB, 3, ATOM_DEV)
    outer = outer.reshape(N_DOM, N_SLAB, 3, 4, GHOST)
    backs = [jnp.roll(outer[:, :, :, 0], -1, 0), jnp.roll(outer[:, :, :, 1], 1, 0), jnp.roll(outer[:, :, :, 2], -1, 1), jnp.roll(outer[:, :, :, 3], 1, 1)]
    for face in range(4):
        local = jax.vmap(jax.vmap(lambda acc, idx, val: acc.at[:, idx].add(val)))(local, gpick[:, :, face], backs[face])
    forces = local.transpose(2, 0, 1, 3).reshape(3, TOTAL)
    return (hidden.reshape(TOTAL, CHANNELS), forces)
```

```python
import functools

import jax
import jax.numpy as jnp
from jax import lax
from jax.experimental import pallas as pl
from jax.experimental.pallas import tpu as pltpu
from jax.sharding import PartitionSpec as P

LAYERS = 2
TILE = 64
LANES = 128
FACES = 4
NHARM = 9
AWAY = 1000.0
CUTOFF = 6.0
SOFTENING = 0.25
F32 = jnp.float32
BF16 = jnp.bfloat16

COS_TERMS = (1.0, -4.934802200544679, 4.058712126416768, -1.3352627688545893, 0.2353306303588935, -0.02580689139001406)
SIN_TERMS = (3.141592653589793, -5.16771278004997, 2.550164039877345, -0.5992645293207921, 0.08214588661112823, -0.00737043094571435)

VMEM = pl.BlockSpec(memory_space=pltpu.VMEM)
SMEM = pl.BlockSpec(memory_space=pltpu.SMEM)


def params():
    return pltpu.CompilerParams(vmem_limit_bytes=40 * 1024 * 1024)


def pieces(value):
    top = value.astype(BF16)
    rest = value - top.astype(F32)
    middle = rest.astype(BF16)
    low = (rest - middle.astype(F32)).astype(BF16)
    return top, middle, low


def series(terms, square):
    total = jnp.full_like(square, terms[-1])
    for term in reversed(terms[:-1]):
        total = total * square + term
    return total


def iota(shape, dim):
    return lax.broadcasted_iota(jnp.int32, shape, dim)


def send_kernel(n_dom, n_slab, pos_ref, kind_ref, pick_ref, ghost_ref, out_ref, picked_ref):
    rows = pos_ref.shape[1]
    cap = pick_ref.shape[1]
    ghost_rows = ghost_ref.shape[1]
    blocks = rows // LANES
    state = jnp.concatenate([pos_ref[...], kind_ref[...].astype(F32) + 1.0], axis=0)
    top, middle, low = (part.astype(F32) for part in pieces(state))
    table = jnp.concatenate([top, middle, low, jnp.zeros_like(low)], axis=0).astype(BF16)
    table = jnp.concatenate([table[:, m * LANES : (m + 1) * LANES] for m in range(blocks)], axis=0)
    shift = LANES.bit_length() - 1
    for dest in range(n_dom):
        pick = pick_ref[dest : dest + 1, :]
        onehot = (iota((LANES, cap), 0) == (pick & (LANES - 1))).astype(F32).astype(BF16)
        found = jnp.dot(table, onehot, preferred_element_type=F32)
        high = pick >> shift
        total = jnp.zeros((16, cap), F32)
        for m in range(blocks):
            total = total + jnp.where(high == m, found[m * 16 : (m + 1) * 16], 0.0)
        total = total[:8] + total[8:]
        picked_ref[dest] = total + pltpu.roll(total, 4, 0)
    upper = iota((8, cap), 0) < 4
    for dest in range(n_dom):
        left = jnp.where(upper, picked_ref[dest], picked_ref[(dest + 1) % n_dom])
        right = picked_ref[(dest - 1) % n_dom]
        if cap < TILE:
            gap = jnp.zeros((8, TILE - cap), F32)
            block = jnp.concatenate([left, gap, right, gap], axis=1)
        else:
            block = jnp.concatenate([left, right], axis=1)
        for slab in range(n_slab):
            out_ref[dest * n_slab + slab, 0:8, :] = block
    me_dom, me_slab = lax.axis_index("dom"), lax.axis_index("slab")
    ghosts = ghost_ref[...].astype(F32)
    targets = (
        lax.rem(me_dom + 1, n_dom) * n_slab + me_slab,
        lax.rem(me_dom + n_dom - 1, n_dom) * n_slab + me_slab,
        me_dom * n_slab + lax.rem(me_slab + 1, n_slab),
        me_dom * n_slab + lax.rem(me_slab + n_slab - 1, n_slab),
    )
    per = ghost_rows // LANES
    for face, target in enumerate(targets):
        start = 8 + (face % 2) * per
        for m in range(per):
            out_ref[target, start + m : start + m + 1, :] = ghosts[face : face + 1, m * LANES : (m + 1) * LANES]


def payload_rows(ghost_rows):
    return -(-(8 + 2 * (ghost_rows // LANES)) // 8) * 8


def send_states(n_dom, n_slab, positions, species, send_pick, ghost_pick):
    cap = send_pick.shape[1]
    depth = payload_rows(ghost_pick.shape[1])
    return pl.pallas_call(
        functools.partial(send_kernel, n_dom, n_slab),
        out_shape=jax.ShapeDtypeStruct((n_dom * n_slab, depth, LANES), F32),
        in_specs=[VMEM] * 4,
        out_specs=VMEM,
        scratch_shapes=[pltpu.VMEM((n_dom, 8, cap), F32)],
        compiler_params=params(),
        name="send_states",
    )(positions.T, species.reshape(1, -1), send_pick, ghost_pick)


def store_tile(doubled, tile, pool_ref):
    live = doubled[3:4] > 0.5
    for word in range(3):
        pool_ref[tile, word] = jnp.broadcast_to(jnp.where(live, doubled[word : word + 1], AWAY), (8, LANES))


def build_pool(n_dom, n_slab, cap, ghost_rows, recv_ref, emb_ref, pool_ref, column_ref, h_ref, kind_ref):
    me_dom, me_slab = lax.axis_index("dom"), lax.axis_index("slab")
    atom_rows = column_ref.shape[0]
    local_tiles = atom_rows // TILE
    before, after = lax.rem(me_slab + n_slab - 1, n_slab), lax.rem(me_slab + 1, n_slab)
    per = TILE // cap
    half = iota((1, LANES), 1) < TILE
    for pair in range(local_tiles // 2):
        kinds = []
        for tile in (2 * pair, 2 * pair + 1):
            parts = [recv_ref[(tile * per + p) * n_slab + me_slab, 0:8, :][:, :cap] for p in range(per)]
            doubled = jnp.concatenate(parts * 2, axis=1)
            store_tile(doubled, tile, pool_ref)
            column = doubled.T[:TILE]
            live = column[:, 3:4] > 0.5
            spot = iota((TILE, 8), 1)
            column_ref[tile * TILE : (tile + 1) * TILE, :] = jnp.where((spot >= 3) | live, column, -AWAY)
            kinds.append(doubled[3:4])
        kind_ref[0:1, pair * LANES : (pair + 1) * LANES] = jnp.where(half, kinds[0], kinds[1])

    def rows_of(slab):
        return jnp.concatenate([recv_ref[e * n_slab + slab, 0:8, :] for e in range(n_dom)], axis=0)

    own = pieces(rows_of(me_slab))
    below = pieces(rows_of(before))
    above = below if n_slab == 2 else pieces(rows_of(after))
    own_at = me_dom * n_slab
    width = ghost_rows // LANES
    sources = (
        (lax.rem(me_dom + n_dom - 1, n_dom) * n_slab + me_slab, 0, own, TILE, 0),
        (lax.rem(me_dom + 1, n_dom) * n_slab + me_slab, 1, own, 0, 4),
        (own_at + before, 0, below, 0, 0),
        (own_at + after, 1, above, 0, 0),
    )
    shift = cap.bit_length() - 1
    for face, (origin, place, tables, lane_start, row_start) in enumerate(sources):
        for m in range(width):
            at = 8 + place * width + m
            pick = recv_ref[origin, at : at + 1, :].astype(jnp.int32)
            onehot = (iota((LANES, LANES), 0) == (pick & (cap - 1)) + lane_start).astype(F32).astype(BF16)
            found = sum(jnp.dot(table, onehot, preferred_element_type=F32) for table in (tables[0], tables[2], tables[1]))
            high = pick >> shift
            total = jnp.zeros((8, LANES), F32)
            for e in range(n_dom):
                total = total + jnp.where(high == e, found[e * 8 : (e + 1) * 8], 0.0)
            if row_start:
                total = pltpu.roll(total, 4, 0)
            swapped = pltpu.roll(total, TILE, 1)
            tile = local_tiles + (face * ghost_rows) // TILE + 2 * m
            store_tile(jnp.where(half, total, swapped), tile, pool_ref)
            store_tile(jnp.where(half, swapped, total), tile + 1, pool_ref)
            spot = tile * TILE
            kind_ref[0:1, spot : spot + LANES] = total[3:4]
    nspecies, width = emb_ref.shape
    table = jnp.concatenate([emb_ref[...].astype(F32), jnp.zeros((16 - nspecies, width), F32)], axis=0).astype(BF16)
    step = 512
    for start in range(0, h_ref.shape[0], step):
        kinds = kind_ref[0:1, start : start + step].astype(jnp.int32)
        onehot = (iota((16, step), 0) == kinds - 1).astype(F32).astype(BF16)
        h_ref[start : start + step, :] = lax.dot_general(onehot, table, (((0,), (0,)), ((), ())), preferred_element_type=F32).astype(BF16)


def half_rows(near_ref, pool_ref, tile, side):
    first, second = near_ref[2 * side, tile], near_ref[2 * side + 1, tile]
    lane = iota((8, LANES), 1)
    left = lane < TILE
    xyz = [jnp.where(left, pool_ref[first, w], pool_ref[second, w]) for w in range(3)]
    rows = jnp.where(left, first * TILE, second * TILE) + (lane & (TILE - 1))
    return first, second, xyz, rows


def tall(value, count):
    return jnp.concatenate([value] * count, axis=0) if count > 1 else value


def geometry(column_ref, start, count, xyz, rows):
    column = column_ref[pl.ds(start, count), :]
    offset = [tall(xyz[w], count // 8) - column[:, w : w + 1] for w in range(3)]
    square = offset[0] * offset[0] + offset[1] * offset[1] + offset[2] * offset[2] + SOFTENING
    inverse = lax.rsqrt(square)
    ratio = jnp.minimum(square * inverse * (1.0 / CUTOFF), 1.0)
    same = tall(rows, count // 8) == iota((count, LANES), 0) + start
    ratio = jnp.where(same, 1.0, ratio)
    fade = 1.0 - ratio * ratio
    return offset, inverse, ratio, fade * fade


def edges_of(column_ref, start, count, xyz, rows):
    offset, inverse, ratio, envelope = geometry(column_ref, start, count, xyz, rows)
    x, y, z = (part * inverse for part in offset)
    harmonic = [x, y, z, x * y, y * z, z * x, (x - y) * (x + y), 3.0 * (z * z) - 1.0]
    shifted = ratio - 0.5
    square = shifted * shifted
    sine = series(COS_TERMS, square)
    cosine = -shifted * series(SIN_TERMS, square)
    twice = cosine + cosine
    radial = [sine * (envelope * inverse)]
    radial.append(twice * radial[0])
    while len(radial) < 8:
        radial.append(twice * radial[-1] - radial[-2])
    return [part.astype(BF16) for part in harmonic], [part.astype(BF16) for part in radial]


def make_edges(near_ref, pool_ref, column_ref, h_ref, radial_ref, tile, edge_ref, weight_ref):
    nbasis = radial_ref.shape[0]
    near = pool_ref.shape[0] * 0 + 4
    span = near * TILE
    chunk = 16
    for side in range(2):
        first, second, xyz, rows = half_rows(near_ref, pool_ref, tile, side)
        for place, other in enumerate((first, second)):
            h = h_ref[pl.ds(pl.multiple_of(other * TILE, TILE), TILE), :]
            for n in range(nbasis):
                spot = n * span + side * LANES + place * TILE
                weight_ref[spot : spot + TILE, :] = h * radial_ref[n : n + 1, :]
        for part in range(TILE // chunk):
            start = pl.multiple_of(tile * TILE + part * chunk, chunk)
            harmonic, radial = edges_of(column_ref, start, chunk, xyz, rows)
            for n in range(nbasis):
                spot = n * span + side * LANES
                edge_ref[part * chunk : (part + 1) * chunk, spot : spot + LANES] = radial[n]
                for k in range(1, NHARM):
                    row = k * TILE + part * chunk
                    edge_ref[row : row + chunk, spot : spot + LANES] = harmonic[k - 1] * radial[n]


def contract(edge_ref, weight_ref, tile, query_ref):
    channels = weight_ref.shape[1]
    agg = jnp.dot(edge_ref[...], weight_ref[...], preferred_element_type=F32) * (1.0 / TILE**0.5)
    part = [agg[k * TILE : (k + 1) * TILE] for k in range(NHARM)]
    square = [one * one for one in part]
    query = [part[0], square[0], square[1] + square[2] + square[3], square[4] + square[5] + square[6] + square[7] + square[8]]
    start = pl.multiple_of(tile * TILE, TILE)
    for spot, one in enumerate(query):
        query_ref[pl.ds(start, TILE), spot * channels : (spot + 1) * channels] = one.astype(BF16)


def run_layer(near_ref, pool_ref, column_ref, h_ref, radial_ref, update_ref, out_ref, edges, weights, query_ref):
    tiles = near_ref.shape[1]

    def make(tile, slot):
        make_edges(near_ref, pool_ref, column_ref, h_ref, radial_ref, tile, edges[slot], weights[slot])

    make(0, 0)

    def step(index, carry):
        tile = 2 * index
        make(tile + 1, 1)
        contract(edges[0], weights[0], tile, query_ref)
        make(jnp.minimum(tile + 2, tiles - 1), 0)
        contract(edges[1], weights[1], tile + 1, query_ref)
        return carry

    lax.fori_loop(0, tiles // 2, step, 0)
    block = 256
    for start in range(0, out_ref.shape[0], block):
        update = jnp.dot(query_ref[start : start + block, :], update_ref[...], preferred_element_type=F32)
        live = (column_ref[start : start + block, 3:4] > 0.5).astype(F32)
        fresh = h_ref[start : start + block, :].astype(F32) + update * (1.0 / (1.0 + jnp.exp(-update)))
        out_ref[start : start + block, :] = (fresh * live).astype(BF16)


def gather_rows(pick_ref, values, outs):
    rows = values.shape[0]
    ghost_rows = pick_ref.shape[1]
    picks = pick_ref[...].astype(F32)
    picks = jnp.concatenate([picks, jnp.zeros_like(picks)], axis=0)
    spots = [(ref, start) for ref in outs for start in range(0, ref.shape[0], ghost_rows)]
    for m in range(ghost_rows // LANES):
        columns = picks[:, m * LANES : (m + 1) * LANES].T.astype(jnp.int32)
        for face, (ref, start) in enumerate(spots):
            onehot = (columns[:, face : face + 1] == iota((LANES, rows), 1)).astype(F32).astype(BF16)
            found = jnp.dot(onehot, values, preferred_element_type=F32)
            ref[start + m * LANES : start + (m + 1) * LANES, :] = found.astype(BF16)


def first_kernel(n_dom, n_slab, cap, n_out, near_ref, recv_ref, emb_ref, radial_ref, update_ref, pick_ref, *rest):
    pool_ref, column_ref, out_ref = rest[:3]
    outs = rest[3 : 3 + n_out]
    edge_a, edge_b, weight_a, weight_b, query_ref, h_ref, kind_ref = rest[3 + n_out :]
    build_pool(n_dom, n_slab, cap, pick_ref.shape[1], recv_ref, emb_ref, pool_ref, column_ref, h_ref, kind_ref)
    run_layer(near_ref, pool_ref, column_ref, h_ref, radial_ref.at[0], update_ref.at[0], out_ref, (edge_a, edge_b), (weight_a, weight_b), query_ref)
    gather_rows(pick_ref, out_ref[...], outs)


def second_kernel(n_in, level, near_ref, pool_ref, column_ref, h_in_ref, *rest):
    ghosts = rest[:n_in]
    radial_ref, update_ref, force_ref, pick_ref, out_ref, g_ref = rest[n_in : n_in + 6]
    outs = rest[n_in + 6 : 2 * n_in + 6]
    edge_a, edge_b, weight_a, weight_b, query_ref, h_ref = rest[2 * n_in + 6 :]
    start = 0
    for ref in (h_in_ref,) + tuple(ghosts):
        h_ref[start : start + ref.shape[0], :] = ref[...]
        start += ref.shape[0]
    run_layer(near_ref, pool_ref, column_ref, h_ref, radial_ref.at[level], update_ref.at[level], out_ref, (edge_a, edge_b), (weight_a, weight_b), query_ref)
    projected = jnp.dot(out_ref[...], force_ref[...], preferred_element_type=F32).astype(BF16)
    g_ref[...] = projected
    gather_rows(pick_ref, projected, outs)


def layer_scratch(nbasis, near, channels, atom_rows, pool_rows):
    span = near * TILE
    return [
        pltpu.VMEM((NHARM * TILE, nbasis * span), BF16),
        pltpu.VMEM((NHARM * TILE, nbasis * span), BF16),
        pltpu.VMEM((nbasis * span, channels), BF16),
        pltpu.VMEM((nbasis * span, channels), BF16),
        pltpu.VMEM((atom_rows, 4 * channels), BF16),
        pltpu.VMEM((pool_rows, channels), BF16),
    ]


def force_kernel(n_in, near_ref, pool_ref, column_ref, g_in_ref, *rest):
    ghosts = rest[:n_in]
    local_ref = rest[n_in]
    outs = rest[n_in + 1 : 2 * n_in + 1]
    g_ref, total_ref, own_ref = rest[2 * n_in + 1 :]
    tiles = near_ref.shape[1]
    atom_rows, channels = g_in_ref.shape
    start = 0
    for ref in (g_in_ref,) + tuple(ghosts):
        g_ref[start : start + ref.shape[0], :] = ref[...]
        start += ref.shape[0]
    total_ref[...] = jnp.zeros_like(total_ref)
    scale = 1.0 / channels**0.5
    left = iota((8, LANES), 1) < TILE

    def step(tile, carry):
        start = pl.multiple_of(tile * TILE, TILE)
        mine = g_ref[pl.ds(start, TILE), :]
        own = [None] * 3
        for side in range(2):
            first, second, xyz, rows = half_rows(near_ref, pool_ref, tile, side)
            others = jnp.concatenate([g_ref[pl.ds(pl.multiple_of(one * TILE, TILE), TILE), :] for one in (first, second)], axis=0)
            inner = lax.dot_general(mine, others, (((1,), (1,)), ((), ())), preferred_element_type=F32)
            offset, inverse, _, envelope = geometry(column_ref, start, TILE, xyz, rows)
            strength = envelope * inverse * (inner * scale)
            for w in range(3):
                pair = strength * offset[w]
                own[w] = pair if own[w] is None else own[w] + pair
                against = sum(pair[8 * v : 8 * v + 8] for v in range(TILE // 8))
                total_ref[first, w] -= jnp.where(left, against, 0.0)
                total_ref[second, w] -= jnp.where(left, 0.0, against)
        for w in range(3):
            own_ref[w, pl.ds(start, TILE), :] = own[w]
        return carry

    lax.fori_loop(0, tiles, step, 0)
    local = jnp.zeros((8, atom_rows), F32)
    for w in range(3):
        ones = (iota((8, LANES), 0) == w).astype(F32).astype(BF16)
        for part in pieces(own_ref[w]):
            local = local + lax.dot_general(ones, part, (((1,), (1,)), ((), ())), preferred_element_type=F32)
    half = iota((1, LANES), 1) < TILE
    sums = []
    for w in range(3):
        folded = jnp.sum(total_ref[:, w], axis=1)
        sums.append(folded + pltpu.roll(folded, TILE, 1))
    local_ref[...] = local
    spots = [(ref, at) for ref in outs for at in range(0, ref.shape[1], LANES)]
    for pair in range(total_ref.shape[0] // 2):
        for w in range(3):
            row = jnp.where(half, sums[w][2 * pair : 2 * pair + 1], sums[w][2 * pair + 1 : 2 * pair + 2])
            if pair < atom_rows // LANES:
                local_ref[w : w + 1, pair * LANES : (pair + 1) * LANES] += row
            else:
                ref, at = spots[pair - atom_rows // LANES]
                ref[w : w + 1, at : at + LANES] = row


def add_kernel(local_ref, pick_ref, *rest):
    backs, out_ref = rest[:-1], rest[-1]
    atom_rows = local_ref.shape[1]
    ghost_rows = pick_ref.shape[1]
    blocks = atom_rows // LANES
    spots = [(ref, at) for ref in backs for at in range(0, ref.shape[1], ghost_rows)]
    shift = LANES.bit_length() - 1
    total = jnp.zeros((blocks * 8, LANES), F32)
    for face, (ref, at) in enumerate(spots):
        pick = pick_ref[face : face + 1, :]
        back = jnp.where(iota((8, ghost_rows), 0) < 3, ref[:, at : at + ghost_rows], 0.0)
        high = pick >> shift
        spread = jnp.concatenate([jnp.where(high == m, back, 0.0) for m in range(blocks)], axis=0)
        onehot = (iota((LANES, ghost_rows), 0) == (pick & (LANES - 1))).astype(F32).astype(BF16)
        for part in pieces(spread):
            total = total + lax.dot_general(part, onehot, (((1,), (1,)), ((), ())), preferred_element_type=F32)
    for m in range(blocks):
        spot = slice(m * LANES, (m + 1) * LANES)
        out_ref[:, spot] = local_ref[0:3, spot] + total[m * 8 : m * 8 + 3]


def passed_along(array, axis, by):
    count = lax.axis_size(axis)
    return lax.ppermute(array, axis, [(i, (i + by) % count) for i in range(count)])


def exchange(arrays, by):
    moved = [passed_along(arrays[0], "dom", by), passed_along(arrays[1], "dom", -by)]
    for one, way in zip(arrays[2:], (by, -by)):
        moved.append(passed_along(one, "slab", way))
    return moved


def body(n_dom, n_slab, positions, species, send_pick, ghost_pick, near_tiles, embedding, radial_weight, update_weight, force_weight):
    atom_rows = positions.shape[0]
    cap = send_pick.shape[1]
    ghost_rows = ghost_pick.shape[1]
    tiles, near = near_tiles.shape
    channels = embedding.shape[1]
    nbasis = radial_weight.shape[1]
    pool_rows = atom_rows + FACES * ghost_rows
    near_t = near_tiles.T
    face_rows = [ghost_rows, ghost_rows] + ([2 * ghost_rows] if n_slab == 2 else [ghost_rows, ghost_rows])
    n_out = len(face_rows)
    face_out = [jax.ShapeDtypeStruct((rows, channels), BF16) for rows in face_rows]
    scratch = layer_scratch(nbasis, near, channels, atom_rows, pool_rows)

    sent = send_states(n_dom, n_slab, positions, species, send_pick, ghost_pick)
    got = lax.all_to_all(sent, ("dom", "slab"), split_axis=0, concat_axis=0, tiled=True)

    pool, column, hidden, *faces = pl.pallas_call(
        functools.partial(first_kernel, n_dom, n_slab, cap, n_out),
        out_shape=[
            jax.ShapeDtypeStruct((pool_rows // TILE, 3, 8, LANES), F32),
            jax.ShapeDtypeStruct((atom_rows, 8), F32),
            jax.ShapeDtypeStruct((atom_rows, channels), BF16),
        ]
        + face_out,
        in_specs=[SMEM] + [VMEM] * 5,
        out_specs=[VMEM] * (3 + n_out),
        scratch_shapes=scratch + [pltpu.VMEM((8, pool_rows), F32)],
        compiler_params=params(),
        name="first_layer",
    )(near_t, got, embedding, radial_weight, update_weight, ghost_pick)

    faces = exchange(faces, 1)
    features, mine, *faces = pl.pallas_call(
        functools.partial(second_kernel, n_out, 1),
        out_shape=[jax.ShapeDtypeStruct((atom_rows, channels), BF16)] * 2 + face_out,
        in_specs=[SMEM] + [VMEM] * (7 + n_out),
        out_specs=[VMEM] * (2 + n_out),
        scratch_shapes=scratch,
        compiler_params=params(),
        name="second_layer",
    )(near_t, pool, column, hidden, *faces, radial_weight, update_weight, force_weight, ghost_pick)

    faces = exchange(faces, 1)
    local, *backs = pl.pallas_call(
        functools.partial(force_kernel, n_out),
        out_shape=[jax.ShapeDtypeStruct((8, atom_rows), F32)] + [jax.ShapeDtypeStruct((8, rows), F32) for rows in face_rows],
        in_specs=[SMEM] + [VMEM] * (3 + n_out),
        out_specs=[VMEM] * (1 + n_out),
        scratch_shapes=[
            pltpu.VMEM((pool_rows, channels), BF16),
            pltpu.VMEM((pool_rows // TILE, 3, 8, LANES), F32),
            pltpu.VMEM((3, atom_rows, LANES), F32),
        ],
        compiler_params=params(),
        name="pair_forces",
    )(near_t, pool, column, mine, *faces)

    backs = exchange(backs, -1)
    forces = pl.pallas_call(
        add_kernel,
        out_shape=jax.ShapeDtypeStruct((3, atom_rows), F32),
        in_specs=[VMEM] * (2 + n_out),
        out_specs=VMEM,
        compiler_params=params(),
        name="add_ghost_forces",
    )(local, ghost_pick, *backs)
    return features, forces


def solution(mesh):
    both = ("dom", "slab")
    return jax.shard_map(
        functools.partial(body, mesh.shape["dom"], mesh.shape["slab"]),
        mesh=mesh,
        in_specs=(P(both, None), P(both), P(both, None), P(both, None), P(both, None), P(), P(), P(), P()),
        out_specs=(P(both, None), P(None, both)),
        check_vma=False,
    )
```

```python
import functools

import jax
import jax.numpy as jnp
from jax import lax
from jax.experimental import pallas as pl
from jax.experimental.pallas import tpu as pltpu
from jax.sharding import PartitionSpec as P

LAYERS = 2
TILE = 64
LANES = 128
FACES = 4
NHARM = 9
AWAY = 1000.0
CUTOFF = 6.0
SOFTENING = 0.25
F32 = jnp.float32
BF16 = jnp.bfloat16

COS_TERMS = (1.0, -4.934802200544679, 4.058712126416768, -1.3352627688545893, 0.2353306303588935, -0.02580689139001406)
SIN_TERMS = (3.141592653589793, -5.16771278004997, 2.550164039877345, -0.5992645293207921, 0.08214588661112823, -0.00737043094571435)

VMEM = pl.BlockSpec(memory_space=pltpu.VMEM)
SMEM = pl.BlockSpec(memory_space=pltpu.SMEM)


def params(mib=40):
    return pltpu.CompilerParams(vmem_limit_bytes=mib * 1024 * 1024)


def pieces(value):
    top = value.astype(BF16)
    rest = value - top.astype(F32)
    middle = rest.astype(BF16)
    low = (rest - middle.astype(F32)).astype(BF16)
    return top, middle, low


def series(terms, square):
    total = jnp.full_like(square, terms[-1])
    for term in reversed(terms[:-1]):
        total = total * square + term
    return total


def iota(shape, dim):
    return lax.broadcasted_iota(jnp.int32, shape, dim)


def send_kernel(n_dom, n_slab, pos_in, kind_in, pick_in, ghost_in, near_in, embedding_in, radial_in, update_in, force_in, out_ref, weights_ref, numbers_ref,
                pos_ref, kind_ref, pick_ref, ghost_ref, near_ref, embedding_ref, radial_ref, picked_ref, sems):
    update_spot, force_spot = weight_spots(radial_in.shape, update_in.shape)
    pairs = [(pos_in, pos_ref), (kind_in, kind_ref), (pick_in, pick_ref), (ghost_in, ghost_ref), (near_in, near_ref), (embedding_in, embedding_ref), (radial_in, radial_ref)]
    pairs += [(update_in.at[m], weights_ref.at[spot : spot + update_in.shape[1]]) for m, spot in enumerate(update_spot)]
    pairs += [(force_in, weights_ref.at[force_spot : force_spot + force_in.shape[0]])]
    copies = []
    for spot, (source, target) in enumerate(pairs):
        copies.append(pltpu.make_async_copy(source, target, sems.at[spot]))
        copies[-1].start()
    for copy in copies:
        copy.wait()
    numbers_ref[...] = jnp.zeros_like(numbers_ref)
    numbers_ref[0:FACES, :] = ghost_ref[...]
    numbers_ref[FACES : FACES + near_ref.shape[0], 0 : near_ref.shape[1]] = near_ref[...]
    blank = jnp.zeros((16, embedding_ref.shape[1]), F32)
    for level in range(radial_ref.shape[0]):
        weights_ref[16 * level : 16 * level + 16, :] = jnp.concatenate([radial_ref[level].astype(F32), blank[radial_ref.shape[1] :]], axis=0).astype(BF16)
    spot = 16 * radial_ref.shape[0]
    weights_ref[spot : spot + 16, :] = jnp.concatenate([embedding_ref[...].astype(F32), blank[embedding_ref.shape[0] :]], axis=0).astype(BF16)
    rows = pos_ref.shape[1]
    cap = pick_ref.shape[1]
    blocks = rows // LANES
    state = jnp.concatenate([pos_ref[...], kind_ref[...].astype(F32) + 1.0], axis=0)
    top, middle, low = (part.astype(F32) for part in pieces(state))
    table = jnp.concatenate([top, middle, low, jnp.zeros_like(low)], axis=0).astype(BF16)
    table = jnp.concatenate([table[:, m * LANES : (m + 1) * LANES] for m in range(blocks)], axis=0)
    shift = LANES.bit_length() - 1
    for dest in range(n_dom):
        pick = pick_ref[dest : dest + 1, :]
        onehot = (iota((LANES, cap), 0) == (pick & (LANES - 1))).astype(F32).astype(BF16)
        found = jnp.dot(table, onehot, preferred_element_type=F32)
        high = pick >> shift
        total = jnp.zeros((16, cap), F32)
        for m in range(blocks):
            total = total + jnp.where(high == m, found[m * 16 : (m + 1) * 16], 0.0)
        total = total[:8] + total[8:]
        picked_ref[dest] = total + pltpu.roll(total, 4, 0)
    packs = []
    bits = rows.bit_length() - 1
    for face in range(FACES):
        picks = ghost_ref[face : face + 1, :]
        third = [picks[:, m * TILE : (m + 1) * TILE] for m in range(picks.shape[1] // TILE)]
        count = len(third) // 2
        lines = [(third[r] + (third[r + count] << bits)).astype(F32) for r in range(count)]
        near = near_ref[...].astype(F32)
        lines.append(jnp.concatenate([near[k : k + 1] for k in range(near.shape[0])], axis=1))
        packs.append(jnp.concatenate(lines, axis=0))
    upper = iota((8, cap), 0) < 4
    for dest in range(n_dom):
        left = jnp.where(upper, picked_ref[dest], picked_ref[(dest + 1) % n_dom])
        right = picked_ref[(dest - 1) % n_dom]
        if cap < TILE:
            gap = jnp.zeros((8, TILE - cap), F32)
            block = jnp.concatenate([left, gap, right, gap], axis=1)
        else:
            block = jnp.concatenate([left, right], axis=1)
        for slab in range(n_slab):
            out_ref[dest * n_slab + slab] = block
    me_dom, me_slab = lax.axis_index("dom"), lax.axis_index("slab")
    targets = (
        lax.rem(me_dom + 1, n_dom) * n_slab + me_slab,
        lax.rem(me_dom + n_dom - 1, n_dom) * n_slab + me_slab,
        me_dom * n_slab + lax.rem(me_slab + 1, n_slab),
        me_dom * n_slab + lax.rem(me_slab + n_slab - 1, n_slab),
    )
    for face, target in enumerate(targets):
        start = 0 if face == 3 else 4
        out_ref[target, start : start + 4, TILE:] = packs[face]


def weight_spots(radial_shape, update_shape):
    first = 16 * radial_shape[0] + 16
    spots = [first + m * update_shape[1] for m in range(update_shape[0])]
    return spots, first + update_shape[0] * update_shape[1]


def send_states(n_dom, n_slab, positions, species, send_pick, ghost_pick, near_tiles, embedding, radial, update, force):
    cap = send_pick.shape[1]
    inputs = (positions.T, species.reshape(1, -1), send_pick, ghost_pick, near_tiles.T, embedding, radial, update, force)
    count = weight_spots(radial.shape, update.shape)[1] + force.shape[0]
    return pl.pallas_call(
        functools.partial(send_kernel, n_dom, n_slab),
        out_shape=[
            jax.ShapeDtypeStruct((n_dom * n_slab, 8, LANES), F32),
            jax.ShapeDtypeStruct((count, force.shape[1]), BF16),
            jax.ShapeDtypeStruct((8, ghost_pick.shape[1]), jnp.int32),
        ],
        in_specs=[pl.BlockSpec(memory_space=pl.ANY)] * len(inputs),
        out_specs=[VMEM] * 3,
        scratch_shapes=[pltpu.VMEM(one.shape, one.dtype) for one in inputs[:7]]
        + [pltpu.VMEM((n_dom, 8, cap), F32), pltpu.SemaphoreType.DMA((8 + update.shape[0],))],
        compiler_params=params(63),
        name="send_states",
    )(*inputs)


def store_tile(doubled, tile, pool_ref):
    live = doubled[3:4] > 0.5
    for word in range(3):
        pool_ref[tile, word] = jnp.broadcast_to(jnp.where(live, doubled[word : word + 1], AWAY), (8, LANES))


def find_rows(tables, lane, group, groups):
    onehot = (iota((LANES, LANES), 0) == lane).astype(F32).astype(BF16)
    found = sum(jnp.dot(table, onehot, preferred_element_type=F32) for table in (tables[0], tables[2], tables[1]))
    total = jnp.zeros((8, LANES), F32)
    for one in range(groups):
        total = total + jnp.where(group == one, found[one * 8 : (one + 1) * 8], 0.0)
    return total


def build_pool(n_dom, n_slab, cap, ghost_rows, recv_ref, emb_ref, pool_ref, column_ref, around_ref, taken_ref, h_ref, kind_ref):
    me_dom, me_slab = lax.axis_index("dom"), lax.axis_index("slab")
    atom_rows = column_ref.shape[0]
    local_tiles = atom_rows // TILE
    before, after = lax.rem(me_slab + n_slab - 1, n_slab), lax.rem(me_slab + 1, n_slab)
    per = TILE // cap
    half = iota((1, LANES), 1) < TILE
    for pair in range(local_tiles // 2):
        kinds = []
        for tile in (2 * pair, 2 * pair + 1):
            parts = [recv_ref[(tile * per + p) * n_slab + me_slab, 0:8, :][:, :cap] for p in range(per)]
            doubled = jnp.concatenate(parts * 2, axis=1)
            store_tile(doubled, tile, pool_ref)
            column = doubled.T[:TILE]
            live = column[:, 3:4] > 0.5
            spot = iota((TILE, 8), 1)
            column_ref[tile * TILE : (tile + 1) * TILE, :] = jnp.where((spot >= 3) | live, column, -AWAY)
            kinds.append(doubled[3:4])
        kind_ref[0:1, pair * LANES : (pair + 1) * LANES] = jnp.where(half, kinds[0], kinds[1])

    def rows_of(slab):
        return jnp.concatenate([recv_ref[e * n_slab + slab, 0:8, :] for e in range(n_dom)], axis=0)

    own = pieces(rows_of(me_slab))
    below = pieces(rows_of(before))
    above = below if n_slab == 2 else pieces(rows_of(after))
    own_at = me_dom * n_slab
    width = ghost_rows // LANES
    sources = (
        (lax.rem(me_dom + n_dom - 1, n_dom) * n_slab + me_slab, 4, own, TILE, 0),
        (lax.rem(me_dom + 1, n_dom) * n_slab + me_slab, 4, own, 0, 4),
        (own_at + before, 4, below, 0, 0),
        (own_at + after, 0, above, 0, 0),
    )
    shift = cap.bit_length() - 1
    bits = atom_rows.bit_length() - 1
    for face, (origin, place, tables, lane_start, row_start) in enumerate(sources):
        packed = recv_ref[origin, place : place + 4, :][:, TILE:].astype(jnp.int32)
        around_ref[face : face + 1, :] = jnp.concatenate([packed[width : width + 1]] * 2, axis=1)
        lines = [packed[r : r + 1] for r in range(width)]
        thirds = [line & (atom_rows - 1) for line in lines] + [line >> bits for line in lines]
        for m in range(width):
            pick = jnp.concatenate(thirds[2 * m : 2 * m + 2], axis=1)
            taken_ref[face : face + 1, m * LANES : (m + 1) * LANES] = pick
            total = find_rows(tables, (pick & (cap - 1)) + lane_start, pick >> shift, n_dom)
            if row_start:
                total = pltpu.roll(total, 4, 0)
            swapped = pltpu.roll(total, TILE, 1)
            tile = local_tiles + (face * ghost_rows) // TILE + 2 * m
            store_tile(jnp.where(half, total, swapped), tile, pool_ref)
            store_tile(jnp.where(half, swapped, total), tile + 1, pool_ref)
            spot = tile * TILE
            kind_ref[0:1, spot : spot + LANES] = total[3:4]
    table = emb_ref[...]
    step = 512
    for start in range(0, h_ref.shape[0], step):
        kinds = kind_ref[0:1, start : start + step].astype(jnp.int32)
        onehot = (iota((16, step), 0) == kinds - 1).astype(F32).astype(BF16)
        h_ref[start : start + step, :] = lax.dot_general(onehot, table, (((0,), (0,)), ((), ())), preferred_element_type=F32).astype(BF16)


class Near:
    def __init__(self, table_ref, shape):
        self.table_ref, self.shape = table_ref, shape

    def __getitem__(self, at):
        return self.table_ref[FACES + at[0], at[1]]


def half_rows(near_ref, pool_ref, tile, side):
    first, second = near_ref[2 * side, tile], near_ref[2 * side + 1, tile]
    lane = iota((8, LANES), 1)
    left = lane < TILE
    xyz = [jnp.where(left, pool_ref[first, w], pool_ref[second, w]) for w in range(3)]
    rows = jnp.where(left, first * TILE, second * TILE) + (lane & (TILE - 1))
    return first, second, xyz, rows


def tall(value, count):
    return jnp.concatenate([value] * count, axis=0) if count > 1 else value


def geometry(column_ref, start, count, xyz, rows):
    column = column_ref[pl.ds(start, count), :]
    offset = [tall(xyz[w], count // 8) - column[:, w : w + 1] for w in range(3)]
    square = offset[0] * offset[0] + offset[1] * offset[1] + offset[2] * offset[2] + SOFTENING
    inverse = lax.rsqrt(square)
    ratio = jnp.minimum(square * inverse * (1.0 / CUTOFF), 1.0)
    same = tall(rows, count // 8) == iota((count, LANES), 0) + start
    ratio = jnp.where(same, 1.0, ratio)
    fade = 1.0 - ratio * ratio
    return offset, inverse, ratio, fade * fade


def edges_of(column_ref, start, count, xyz, rows):
    offset, inverse, ratio, envelope = geometry(column_ref, start, count, xyz, rows)
    x, y, z = (part * inverse for part in offset)
    harmonic = [x, y, z, x * y, y * z, z * x, (x - y) * (x + y), 3.0 * (z * z) - 1.0]
    shifted = ratio - 0.5
    square = shifted * shifted
    sine = series(COS_TERMS, square)
    cosine = -shifted * series(SIN_TERMS, square)
    twice = cosine + cosine
    radial = [sine * (envelope * inverse)]
    radial.append(twice * radial[0])
    while len(radial) < 8:
        radial.append(twice * radial[-1] - radial[-2])
    return harmonic, radial


def store_part(near_ref, pool_ref, column_ref, tile, side, part, harmonic_ref, radial_ref):
    chunk = 16
    _, _, xyz, rows = half_rows(near_ref, pool_ref, tile, side)
    spot = slice(part * chunk, (part + 1) * chunk)
    harmonic, radial = edges_of(column_ref, pl.multiple_of(tile * TILE + part * chunk, chunk), chunk, xyz, rows)
    for k, one in enumerate(harmonic):
        harmonic_ref[k, spot, :] = one.astype(BF16)
    for n, one in enumerate(radial):
        radial_ref[n, spot, :] = one.astype(BF16)
    return jnp.maximum(radial[-1][:8], radial[-1][8:])[:1]


def side_sum(near_ref, h_ref, weight_ref, tile, side, harmonic_ref, radial_ref, gates):
    nears = [near_ref[2 * side + place, tile] for place in range(2)]
    features = jnp.concatenate([h_ref[pl.ds(pl.multiple_of(other * TILE, TILE), TILE), :] for other in nears], axis=0)
    nbasis = weight_ref.shape[0]
    radial = [radial_ref[n] for n in range(nbasis)]
    rows = [jnp.concatenate(radial, axis=1)]
    for k in range(NHARM - 1):
        harmonic = harmonic_ref[k]
        rows.append(jnp.concatenate([harmonic * one for one in radial], axis=1))
    weight = weight_ref[...].astype(F32)
    steps = []
    for m in range(nbasis // 2):
        part = weight[2 * m : 2 * m + 2]
        for one in gates[m]:
            part = jnp.where(one < 1e30, part, 0.0)
        part = part.astype(BF16)
        steps += [features * part[n : n + 1] for n in range(2)]
    return jnp.dot(jnp.concatenate(rows, axis=0), jnp.concatenate(steps, axis=0), preferred_element_type=F32)


def store_query(agg_ref, tile, query_ref):
    channels = agg_ref.shape[1]
    part = [agg_ref[k * TILE : (k + 1) * TILE, :] * (1.0 / TILE**0.5) for k in range(NHARM)]
    square = [one * one for one in part]
    query = [part[0], square[0], square[1] + square[2] + square[3], square[4] + square[5] + square[6] + square[7] + square[8]]
    start = pl.multiple_of(tile * TILE, TILE)
    for spot, one in enumerate(query):
        query_ref[pl.ds(start, TILE), spot * channels : (spot + 1) * channels] = one.astype(BF16)
    return query[-1][:1]


def run_layer(near_ref, pool_ref, column_ref, h_ref, weight_ref, update_ref, out_ref, query_ref, agg_ref, harm_now, harm_next, radial_now, radial_next):
    tiles = near_ref.shape[1]

    harmonics, radials = (harm_now, harm_next), (radial_now, radial_next)

    def make(tile, unit, slot):
        side, part = divmod(unit, 4)
        return store_part(near_ref, pool_ref, column_ref, tile, side, part, harmonics[slot].at[side], radials[slot].at[side])

    for unit in range(8):
        make(0, unit, 0)
    agg_ref[...] = jnp.zeros_like(agg_ref)

    def step(index, carry):
        for turn in range(4):
            slot = turn % 2
            tile = 4 * index + turn
            later = jnp.minimum(tile + 1, tiles - 1)
            query = store_query(agg_ref, jnp.maximum(tile - 1, 0), query_ref)
            units = [make(later, unit, 1 - slot) for unit in range(8)]
            gates = ((), (), (), ())
            sides = [side_sum(near_ref, h_ref, weight_ref, tile, side, harmonics[slot].at[side], radials[slot].at[side], gates) for side in range(2)]
            agg_ref[...] = sides[0] + sides[1]
        return carry

    lax.fori_loop(0, tiles // 4, step, 0)
    store_query(agg_ref, tiles - 1, query_ref)
    block = 256
    for start in range(0, out_ref.shape[0], block):
        update = jnp.dot(query_ref[start : start + block, :], update_ref[...], preferred_element_type=F32)
        live = (column_ref[start : start + block, 3:4] > 0.5).astype(F32)
        fresh = h_ref[start : start + block, :].astype(F32) + update * (1.0 / (1.0 + jnp.exp(-update)))
        out_ref[start : start + block, :] = (fresh * live).astype(BF16)


def spread(refs, size):
    return [(ref, start) for ref in refs for start in range(0, ref.shape[0], size)]


def gather_rows(pick_ref, tasks):
    ghost_rows = pick_ref.shape[1]
    picks = pick_ref[...].astype(F32)
    if picks.shape[0] < 8:
        picks = jnp.concatenate([picks, jnp.zeros((8 - picks.shape[0], ghost_rows), F32)], axis=0)
    for m in range(ghost_rows // LANES):
        columns = picks[:, m * LANES : (m + 1) * LANES].T.astype(jnp.int32)
        for face, source, target, start in tasks:
            onehot = (columns[:, face : face + 1] == iota((LANES, source.shape[0]), 1)).astype(F32).astype(BF16)
            found = jnp.dot(onehot, source[...], preferred_element_type=F32)
            target[start + m * LANES : start + (m + 1) * LANES, :] = found.astype(BF16)


def views(weights_ref, spot):
    radial, nbasis, update, depth = spot
    return weights_ref.at[radial : radial + nbasis], weights_ref.at[update : update + depth]


def first_kernel(n_dom, n_slab, cap, n_out, spot, emb_spot, tiles, table_ref, recv_ref, weights_ref, numbers_ref, *rest):
    near_ref = Near(table_ref, tiles)
    pick_ref = numbers_ref
    emb_ref = weights_ref.at[emb_spot : emb_spot + 16]
    pool_ref, column_ref, around_ref, taken_ref, out_ref = rest[:5]
    outs = rest[5 : 5 + n_out]
    *scratch, h_ref, kind_ref = rest[5 + n_out :]
    build_pool(n_dom, n_slab, cap, pick_ref.shape[1], recv_ref, emb_ref, pool_ref, column_ref, around_ref, taken_ref, h_ref, kind_ref)
    run_layer(near_ref, pool_ref, column_ref, h_ref, *views(weights_ref, spot), out_ref, *scratch)
    gather_rows(pick_ref, [(face, out_ref, ref, start) for face, (ref, start) in enumerate(spread(outs, pick_ref.shape[1]))])


def second_kernel(n_in, spot, force_spot, tiles, table_ref, pool_ref, column_ref, h_in_ref, *rest):
    near_ref = Near(table_ref, tiles)
    ghosts = rest[:n_in]
    weights_ref, out_ref, g_ref = rest[n_in : n_in + 3]
    *scratch, h_ref = rest[n_in + 3 :]
    start = 0
    for ref in (h_in_ref,) + tuple(ghosts):
        h_ref[start : start + ref.shape[0], :] = ref[...]
        start += ref.shape[0]
    run_layer(near_ref, pool_ref, column_ref, h_ref, *views(weights_ref, spot), out_ref, *scratch)
    g_ref[...] = jnp.dot(out_ref[...], weights_ref[force_spot:, :], preferred_element_type=F32).astype(BF16)


def layer_scratch(nbasis, near, channels, atom_rows, pool_rows):
    half = near * TILE // 2
    return [
        pltpu.VMEM((atom_rows, 4 * channels), BF16),
        pltpu.VMEM((NHARM * TILE, channels), F32),
        *[pltpu.VMEM((2, NHARM - 1, TILE, half), BF16)] * 2,
        *[pltpu.VMEM((2, nbasis, TILE, half), BF16)] * 2,
        pltpu.VMEM((pool_rows, channels), BF16),
    ]


def list_blocks(near_ref, around_ref, atom_tiles, face_tiles, early_ref, late_ref):
    near = near_ref.shape[0]
    pool_tiles = atom_tiles + FACES * face_tiles
    spare = (5 * atom_tiles) * 128 + pool_tiles + FACES * face_tiles
    first_slab = atom_tiles + 2 * face_tiles

    def own(tile, counts):
        early, late = counts
        for k in range(near):
            other = near_ref[k, tile]
            entry = tile * 128 + other
            with_dom = ((other >= atom_tiles) & (other < first_slab)).astype(jnp.int32)
            early_ref[early] = entry
            late_ref[late] = entry
            early, late = early + 1 - with_dom, late + with_dom
        return early, late

    counts = lax.fori_loop(0, atom_tiles, own, (jnp.int32(0), jnp.int32(0)))

    def of_others(ref, pairs):
        def others(tile, count):
            for domain, face in pairs:
                start = atom_tiles + face * face_tiles
                for k in range(near):
                    other = around_ref[domain, k * atom_tiles + tile] - start
                    ref[count] = (atom_tiles * (domain + 1) + tile) * 128 + pool_tiles + face * face_tiles + other
                    count = count + ((other >= 0) & (other < face_tiles)).astype(jnp.int32)
            return count

        return others

    early = lax.fori_loop(0, atom_tiles, of_others(early_ref, ((2, 3), (3, 2))), counts[0])
    late = lax.fori_loop(0, atom_tiles, of_others(late_ref, ((0, 1), (1, 0))), counts[1])
    for extra in range(3):
        early_ref[early + extra] = spare
        late_ref[late + extra] = spare
    return early, late


def block_pair(first, second, atom_tiles, pool_ref, column_ref, gi_ref, gj_ref):
    scale = 1.0 / gi_ref.shape[1] ** 0.5
    lane = iota((8, LANES), 1)
    left = lane < TILE
    half = iota((TILE, LANES), 1) < TILE
    i_tiles = [pl.multiple_of((one >> 7) * TILE, TILE) for one in (first, second)]
    j_tiles = [one & 127 for one in (first, second)]
    same = [jnp.where((one >> 7 == one & 127) & (one >> 7 < atom_tiles), 0, 4096) for one in (first, second)]
    rows = jnp.where(left, same[0], same[1]) + (lane & (TILE - 1))
    columns = [column_ref[pl.ds(one, TILE), :] for one in i_tiles]
    mine = jnp.concatenate([gi_ref[pl.ds(one, TILE), :] for one in i_tiles], axis=0)
    others = jnp.concatenate([gj_ref[pl.ds(pl.multiple_of(one * TILE, TILE), TILE), :] for one in j_tiles], axis=0)
    inner = lax.dot_general(mine, others, (((1,), (1,)), ((), ())), preferred_element_type=F32)
    inner = jnp.where(half, inner[:TILE], inner[TILE:])
    offset = []
    for w in range(3):
        away = tall(jnp.where(left, pool_ref[j_tiles[0], w], pool_ref[j_tiles[1], w]), TILE // 8)
        offset.append(away - jnp.where(half, columns[0][:, w : w + 1], columns[1][:, w : w + 1]))
    square = offset[0] * offset[0] + offset[1] * offset[1] + offset[2] * offset[2] + SOFTENING
    inverse = lax.rsqrt(square)
    ratio = jnp.minimum(square * inverse * (1.0 / CUTOFF), 1.0)
    ratio = jnp.where(tall(rows, TILE // 8) == iota((TILE, LANES), 0), 1.0, ratio)
    fade = 1.0 - ratio * ratio
    strength = fade * fade * inverse * (inner * scale)
    return [strength * one for one in offset]


def sum_blocks(list_ref, count, atom_tiles, pool_ref, column_ref, gi_ref, gj_ref, own_ref, total_ref):
    own_ref[...] = jnp.zeros_like(own_ref)
    total_ref[...] = jnp.zeros_like(total_ref)
    left = iota((8, LANES), 1) < TILE
    half = iota((TILE, LANES), 1) < TILE

    def step(index, carry):
        entries = [list_ref[4 * index + spot] for spot in range(4)]
        found = [block_pair(entries[2 * p], entries[2 * p + 1], atom_tiles, pool_ref, column_ref, gi_ref, gj_ref) for p in range(2)]
        for p in range(2):
            for spot in range(2):
                entry = entries[2 * p + spot]
                i_tile, j_tile = jnp.minimum(entry >> 7, atom_tiles), entry & 127
                for w in range(3):
                    pair = found[p][w]
                    against = sum(pair[8 * v : 8 * v + 8] for v in range(TILE // 8))
                    total_ref[j_tile, w] -= jnp.where(left, against, 0.0) if spot == 0 else jnp.where(left, 0.0, against)
                    own_ref[i_tile, w] += jnp.where(half, pair, 0.0) if spot == 0 else jnp.where(half, 0.0, pair)
        return carry

    lax.fori_loop(0, (count + 3) // 4, step, 0)


def gather_forces(pick_ref, faces, atom_tiles, face_tiles, own_ref, total_ref):
    atom_rows = atom_tiles * TILE
    pool_tiles = atom_tiles + FACES * face_tiles
    half = iota((1, LANES), 1) < TILE
    sums = []
    for w in range(3):
        folded = jnp.sum(total_ref[:, w], axis=1)
        sums.append(folded + pltpu.roll(folded, TILE, 1))

    def row(tile):
        lines = [jnp.where(half, sums[w][tile : tile + 1], sums[w][tile + 1 : tile + 2]) for w in range(3)]
        return jnp.concatenate(lines + [jnp.zeros((5, LANES), F32)], axis=0)

    blocks = atom_rows // LANES
    shift = LANES.bit_length() - 1
    total = jnp.concatenate([row(2 * m) for m in range(blocks)], axis=0)
    for face in faces:
        for m in range(face_tiles // 2):
            pick = pick_ref[face : face + 1, m * LANES : (m + 1) * LANES]
            back = row(pool_tiles + face * face_tiles + 2 * m)
            high = pick >> shift
            wide = jnp.concatenate([jnp.where(high == one, back, 0.0) for one in range(blocks)], axis=0)
            onehot = (iota((LANES, LANES), 0) == (pick & (LANES - 1))).astype(F32).astype(BF16)
            for part in pieces(wide)[:2]:
                total = total + lax.dot_general(part, onehot, (((1,), (1,)), ((), ())), preferred_element_type=F32)
    total = jnp.concatenate([total[m * 8 : (m + 1) * 8] for m in range(blocks)], axis=1)
    for w in range(3):
        ones = (iota((8, LANES), 0) == w).astype(F32).astype(BF16)
        mine = jnp.concatenate([own_ref[tile, w] for tile in range(atom_tiles)], axis=0)
        for part in pieces(mine)[:2]:
            total = total + lax.dot_general(ones, part, (((1,), (1,)), ((), ())), preferred_element_type=F32)
    return total


def near_forces_kernel(n_dom, n_slab, cap, tiles, table_ref, around_ref, recv_ref, numbers_ref, taken_ref, pool_in, column_in, g_ref, *rest):
    near_ref = Near(table_ref, tiles)
    pick_ref = numbers_ref
    slabs = rest[: 1 if n_slab == 2 else 2]
    part_ref, pool_ref, column_ref, out_g_ref, late_ref, gi_ref, gj_ref, own_ref, total_ref, early_ref = rest[len(slabs) :]
    atom_rows, channels = g_ref.shape
    ghost_rows = pick_ref.shape[1]
    atom_tiles, face_tiles = atom_rows // TILE, ghost_rows // TILE
    pool_tiles = atom_tiles + FACES * face_tiles
    me_slab = lax.axis_index("slab")
    before, after = lax.rem(me_slab + n_slab - 1, n_slab), lax.rem(me_slab + 1, n_slab)
    early, late = list_blocks(near_ref, around_ref, atom_tiles, face_tiles, early_ref, late_ref.at[0])
    late_ref[1, 0] = late
    column_ref[0:atom_rows, :] = column_in[...]
    column_ref[5 * atom_rows :, :] = jnp.full((TILE, 8), -AWAY, F32)
    per = TILE // cap
    spot = iota((TILE, 8), 1)

    def put(domain, tile, column):
        live = column[:, 3:4] > 0.5
        start = atom_rows * (domain + 1) + tile * TILE
        column_ref[start : start + TILE, :] = jnp.where((spot >= 3) | live, column, -AWAY)

    def tile_of(slab, tile):
        parts = [recv_ref[(tile * per + p) * n_slab + slab] for p in range(per)]
        return jnp.concatenate([one[:, start : start + cap] for start in (0, TILE) for one in parts], axis=1)

    for tile in range(atom_tiles):
        block = tile_of(me_slab, tile)
        put(0, tile, block.T[TILE:])
        put(1, tile, pltpu.roll(block, 4, 0).T[:TILE])
        below = tile_of(before, tile).T[:TILE]
        put(2, tile, below)
        put(3, tile, below if n_slab == 2 else tile_of(after, tile).T[:TILE])
    pool_ref[0:pool_tiles] = pool_in[...]
    pool_ref[pool_tiles + FACES * face_tiles] = jnp.full((3, 8, LANES), AWAY, F32)
    own = pieces(jnp.concatenate([recv_ref[e * n_slab + me_slab] for e in range(n_dom)], axis=0))
    shift = cap.bit_length() - 1
    half = iota((1, LANES), 1) < TILE
    for face in range(FACES):
        for m in range(ghost_rows // LANES):
            pick = pick_ref[face : face + 1, m * LANES : (m + 1) * LANES]
            total = find_rows(own, pick & (cap - 1), pick >> shift, n_dom)
            swapped = pltpu.roll(total, TILE, 1)
            tile = pool_tiles + face * face_tiles + 2 * m
            store_tile(jnp.where(half, total, swapped), tile, pool_ref)
            store_tile(jnp.where(half, swapped, total), tile + 1, pool_ref)
    gi_ref[0:atom_rows, :] = g_ref[...]
    gj_ref[0:atom_rows, :] = g_ref[...]
    spare = jnp.zeros((TILE, channels), BF16)
    gi_ref[5 * atom_rows :, :] = spare
    gj_ref[(pool_tiles + FACES * face_tiles) * TILE :, :] = spare
    gi_ref[3 * atom_rows : 4 * atom_rows, :] = slabs[0][...]
    gi_ref[4 * atom_rows : 5 * atom_rows, :] = slabs[-1][...]
    gather_rows(pick_ref, [(face, g_ref, gj_ref, pool_tiles * TILE + face * ghost_rows) for face in range(FACES)])
    gather_rows(taken_ref, [(face, ref, gj_ref, atom_rows + face * ghost_rows) for face, ref in ((2, slabs[0]), (3, slabs[-1]))])
    out_g_ref[...] = gj_ref[pool_tiles * TILE : pool_tiles * TILE + 2 * ghost_rows, :]
    sum_blocks(early_ref, early, atom_tiles, pool_ref, column_ref, gi_ref, gj_ref, own_ref, total_ref)
    part_ref[...] = gather_forces(pick_ref, (2, 3), atom_tiles, face_tiles, own_ref, total_ref)


def far_forces_kernel(list_ref, numbers_ref, taken_ref, pool_ref, column_ref, g_ref, out_g_ref, below_ref, above_ref, part_ref, out_ref, gi_ref, gj_ref, own_ref, total_ref):
    pick_ref = numbers_ref
    atom_rows, channels = g_ref.shape
    ghost_rows = pick_ref.shape[1]
    atom_tiles, face_tiles = atom_rows // TILE, ghost_rows // TILE
    pool_tiles = atom_tiles + FACES * face_tiles
    spare = jnp.zeros((TILE, channels), BF16)
    gi_ref[0:atom_rows, :] = g_ref[...]
    gi_ref[atom_rows : 2 * atom_rows, :] = below_ref[...]
    gi_ref[2 * atom_rows : 3 * atom_rows, :] = above_ref[...]
    gi_ref[5 * atom_rows :, :] = spare
    gj_ref[pool_tiles * TILE : pool_tiles * TILE + 2 * ghost_rows, :] = out_g_ref[...]
    gj_ref[(pool_tiles + FACES * face_tiles) * TILE :, :] = spare
    gather_rows(taken_ref, [(face, ref, gj_ref, atom_rows + face * ghost_rows) for face, ref in ((0, below_ref), (1, above_ref))])
    sum_blocks(list_ref.at[0], list_ref[1, 0], atom_tiles, pool_ref, column_ref, gi_ref, gj_ref, own_ref, total_ref)
    total = gather_forces(pick_ref, (0, 1), atom_tiles, face_tiles, own_ref, total_ref) + part_ref[...]
    out_ref[...] = total[0:3]


def passed_along(array, axis, by):
    count = lax.axis_size(axis)
    return lax.ppermute(array, axis, [(i, (i + by) % count) for i in range(count)])


def exchange(arrays, by):
    moved = [passed_along(arrays[0], "dom", by), passed_along(arrays[1], "dom", -by)]
    for one, way in zip(arrays[2:], (by, -by)):
        moved.append(passed_along(one, "slab", way))
    return moved


def body(n_dom, n_slab, positions, species, send_pick, ghost_pick, near_tiles, embedding, radial_weight, update_weight, force_weight):
    atom_rows = positions.shape[0]
    cap = send_pick.shape[1]
    ghost_rows = ghost_pick.shape[1]
    tiles, near = near_tiles.shape
    channels = embedding.shape[1]
    nbasis = radial_weight.shape[1]
    pool_rows = atom_rows + FACES * ghost_rows
    face_rows = [ghost_rows, ghost_rows] + ([2 * ghost_rows] if n_slab == 2 else [ghost_rows, ghost_rows])
    n_out = len(face_rows)
    face_out = [jax.ShapeDtypeStruct((rows, channels), BF16) for rows in face_rows]
    scratch = layer_scratch(nbasis, near, channels, atom_rows, pool_rows)

    sent, weights, numbers = send_states(n_dom, n_slab, positions, species, send_pick, ghost_pick, near_tiles, embedding, radial_weight, update_weight, force_weight)
    update_spot, force_spot = weight_spots(radial_weight.shape, update_weight.shape)
    spots = [(16 * m, nbasis, at, update_weight.shape[1]) for m, at in enumerate(update_spot)]
    got = lax.all_to_all(sent, ("dom", "slab"), split_axis=0, concat_axis=0, tiled=True)

    pool, column, around, taken, hidden, *faces = pl.pallas_call(
        functools.partial(first_kernel, n_dom, n_slab, cap, n_out, spots[0], 16 * len(spots), (near, tiles)),
        out_shape=[
            jax.ShapeDtypeStruct((pool_rows // TILE, 3, 8, LANES), F32),
            jax.ShapeDtypeStruct((atom_rows, 8), F32),
            jax.ShapeDtypeStruct((8, LANES), jnp.int32),
            jax.ShapeDtypeStruct((8, ghost_rows), jnp.int32),
            jax.ShapeDtypeStruct((atom_rows, channels), BF16),
        ]
        + face_out,
        in_specs=[SMEM] + [VMEM] * 3,
        out_specs=[VMEM] * (5 + n_out),
        scratch_shapes=scratch + [pltpu.VMEM((8, pool_rows), F32)],
        compiler_params=params(),
        name="first_layer",
    )(numbers, got, weights, numbers)

    faces = exchange(faces, 1)
    features, mine = pl.pallas_call(
        functools.partial(second_kernel, n_out, spots[1], force_spot, (near, tiles)),
        out_shape=[jax.ShapeDtypeStruct((atom_rows, channels), BF16)] * 2,
        in_specs=[SMEM] + [VMEM] * (4 + n_out),
        out_specs=[VMEM] * 2,
        scratch_shapes=scratch,
        compiler_params=params(),
        name="second_layer",
    )(numbers, pool, column, hidden, *faces, weights)

    slabs = [passed_along(mine, "slab", 1)]
    if n_slab != 2:
        slabs.append(passed_along(mine, "slab", -1))
    below, above = passed_along(mine, "dom", 1), passed_along(mine, "dom", -1)
    face_tiles = ghost_rows // TILE
    i_rows = 5 * atom_rows + TILE
    j_tiles = pool_rows // TILE + FACES * face_tiles + 1
    longest = (near * tiles) * 5 + 4
    force_scratch = [
        pltpu.VMEM((i_rows, channels), BF16),
        pltpu.VMEM((j_tiles * TILE, channels), BF16),
        pltpu.VMEM((tiles + 1, 3, TILE, LANES), F32),
        pltpu.VMEM((j_tiles, 3, 8, LANES), F32),
    ]
    part, pool, column, out_g, late = pl.pallas_call(
        functools.partial(near_forces_kernel, n_dom, n_slab, cap, (near, tiles)),
        out_shape=[
            jax.ShapeDtypeStruct((8, atom_rows), F32),
            jax.ShapeDtypeStruct((j_tiles, 3, 8, LANES), F32),
            jax.ShapeDtypeStruct((i_rows, 8), F32),
            jax.ShapeDtypeStruct((2 * ghost_rows, channels), BF16),
            jax.ShapeDtypeStruct((2, longest), jnp.int32),
        ],
        in_specs=[SMEM] * 2 + [VMEM] * (6 + len(slabs)),
        out_specs=[VMEM] * 4 + [SMEM],
        scratch_shapes=force_scratch + [pltpu.SMEM((longest,), jnp.int32)],
        cost_estimate=pl.CostEstimate(flops=4_000_000_000, bytes_accessed=4_000_000, transcendentals=0),
        compiler_params=params(),
        name="near_forces",
    )(numbers, around, got, numbers, taken, pool, column, mine, *slabs)
    forces = pl.pallas_call(
        far_forces_kernel,
        out_shape=jax.ShapeDtypeStruct((3, atom_rows), F32),
        in_specs=[SMEM] + [VMEM] * 9,
        out_specs=VMEM,
        scratch_shapes=force_scratch,
        compiler_params=params(),
        name="far_forces",
    )(late, numbers, taken, pool, column, mine, out_g, below, above, part)
    return features, forces


def solution(mesh):
    both = ("dom", "slab")
    return jax.shard_map(
        functools.partial(body, mesh.shape["dom"], mesh.shape["slab"]),
        mesh=mesh,
        in_specs=(P(both, None), P(both), P(both, None), P(both, None), P(both, None), P(), P(), P(), P()),
        out_specs=(P(both, None), P(None, both)),
        check_vma=False,
    )
```

```python
import functools

import jax
import jax.numpy as jnp
from jax import lax
from jax.experimental import pallas as pl
from jax.experimental.pallas import tpu as pltpu
from jax.sharding import PartitionSpec as P

LAYERS = 2
TILE = 64
LANES = 128
FACES = 4
NHARM = 9
AWAY = 1000.0
CUTOFF = 6.0
SOFTENING = 0.25
F32 = jnp.float32
BF16 = jnp.bfloat16

COS_TERMS = (1.0, -4.934802200544679, 4.058712126416768, -1.3352627688545893, 0.2353306303588935, -0.02580689139001406)
SIN_TERMS = (3.141592653589793, -5.16771278004997, 2.550164039877345, -0.5992645293207921, 0.08214588661112823, -0.00737043094571435)

VMEM = pl.BlockSpec(memory_space=pltpu.VMEM)
SMEM = pl.BlockSpec(memory_space=pltpu.SMEM)


def params(mib=40):
    return pltpu.CompilerParams(vmem_limit_bytes=int(mib * 1024 * 1024))


def pieces(value):
    top = value.astype(BF16)
    rest = value - top.astype(F32)
    middle = rest.astype(BF16)
    low = (rest - middle.astype(F32)).astype(BF16)
    return top, middle, low


def series(terms, square):
    total = jnp.full_like(square, terms[-1])
    for term in reversed(terms[:-1]):
        total = total * square + term
    return total


def iota(shape, dim):
    return lax.broadcasted_iota(jnp.int32, shape, dim)


def send_kernel(n_dom, n_slab, pos_in, kind_in, pick_in, ghost_in, near_in, embedding_in, radial_in, update_in, force_in, out_ref, weights_ref, numbers_ref,
                pos_ref, kind_ref, pick_ref, ghost_ref, near_ref, embedding_ref, radial_ref, picked_ref, sems):
    update_spot, force_spot = weight_spots(radial_in.shape, update_in.shape)
    pairs = [(pos_in, pos_ref), (kind_in, kind_ref), (pick_in, pick_ref), (ghost_in, ghost_ref), (near_in, near_ref), (embedding_in, embedding_ref), (radial_in, radial_ref)]
    pairs += [(update_in.at[m], weights_ref.at[spot : spot + update_in.shape[1]]) for m, spot in enumerate(update_spot)]
    pairs += [(force_in, weights_ref.at[force_spot : force_spot + force_in.shape[0]])]
    copies = []
    for spot, (source, target) in enumerate(pairs):
        copies.append(pltpu.make_async_copy(source, target, sems.at[spot]))
        copies[-1].start()
    for copy in copies:
        copy.wait()
    numbers_ref[...] = jnp.zeros_like(numbers_ref)
    numbers_ref[0:FACES, :] = ghost_ref[...]
    numbers_ref[FACES : FACES + near_ref.shape[0], 0 : near_ref.shape[1]] = near_ref[...]
    blank = jnp.zeros((16, embedding_ref.shape[1]), F32)
    for level in range(radial_ref.shape[0]):
        weights_ref[16 * level : 16 * level + 16, :] = jnp.concatenate([radial_ref[level].astype(F32), blank[radial_ref.shape[1] :]], axis=0).astype(BF16)
    spot = 16 * radial_ref.shape[0]
    weights_ref[spot : spot + 16, :] = jnp.concatenate([embedding_ref[...].astype(F32), blank[embedding_ref.shape[0] :]], axis=0).astype(BF16)
    rows = pos_ref.shape[1]
    cap = pick_ref.shape[1]
    blocks = rows // LANES
    state = jnp.concatenate([pos_ref[...], kind_ref[...].astype(F32) + 1.0], axis=0)
    top, middle, low = (part.astype(F32) for part in pieces(state))
    table = jnp.concatenate([top, middle, low, jnp.zeros_like(low)], axis=0).astype(BF16)
    table = jnp.concatenate([table[:, m * LANES : (m + 1) * LANES] for m in range(blocks)], axis=0)
    shift = LANES.bit_length() - 1
    for dest in range(n_dom):
        pick = pick_ref[dest : dest + 1, :]
        onehot = (iota((LANES, cap), 0) == (pick & (LANES - 1))).astype(F32).astype(BF16)
        found = jnp.dot(table, onehot, preferred_element_type=F32)
        high = pick >> shift
        total = jnp.zeros((16, cap), F32)
        for m in range(blocks):
            total = total + jnp.where(high == m, found[m * 16 : (m + 1) * 16], 0.0)
        total = total[:8] + total[8:]
        picked_ref[dest] = total + pltpu.roll(total, 4, 0)
    packs = []
    bits = rows.bit_length() - 1
    for face in range(FACES):
        picks = ghost_ref[face : face + 1, :]
        third = [picks[:, m * TILE : (m + 1) * TILE] for m in range(picks.shape[1] // TILE)]
        count = len(third) // 2
        lines = [(third[r] + (third[r + count] << bits)).astype(F32) for r in range(count)]
        near = near_ref[...].astype(F32)
        lines.append(jnp.concatenate([near[k : k + 1] for k in range(near.shape[0])], axis=1))
        packs.append(jnp.concatenate(lines, axis=0))
    upper = iota((8, cap), 0) < 4
    for dest in range(n_dom):
        left = jnp.where(upper, picked_ref[dest], picked_ref[(dest + 1) % n_dom])
        right = picked_ref[(dest - 1) % n_dom]
        if cap < TILE:
            gap = jnp.zeros((8, TILE - cap), F32)
            block = jnp.concatenate([left, gap, right, gap], axis=1)
        else:
            block = jnp.concatenate([left, right], axis=1)
        for slab in range(n_slab):
            out_ref[dest * n_slab + slab] = block
    me_dom, me_slab = lax.axis_index("dom"), lax.axis_index("slab")
    targets = (
        lax.rem(me_dom + 1, n_dom) * n_slab + me_slab,
        lax.rem(me_dom + n_dom - 1, n_dom) * n_slab + me_slab,
        me_dom * n_slab + lax.rem(me_slab + 1, n_slab),
        me_dom * n_slab + lax.rem(me_slab + n_slab - 1, n_slab),
    )
    for face, target in enumerate(targets):
        start = 0 if face == 3 else 4
        out_ref[target, start : start + 4, TILE:] = packs[face]


def weight_spots(radial_shape, update_shape):
    first = 16 * radial_shape[0] + 16
    spots = [first + m * update_shape[1] for m in range(update_shape[0])]
    return spots, first + update_shape[0] * update_shape[1]


def send_states(n_dom, n_slab, positions, species, send_pick, ghost_pick, near_tiles, embedding, radial, update, force):
    cap = send_pick.shape[1]
    inputs = (positions.T, species.reshape(1, -1), send_pick, ghost_pick, near_tiles.T, embedding, radial, update, force)
    count = weight_spots(radial.shape, update.shape)[1] + force.shape[0]
    return pl.pallas_call(
        functools.partial(send_kernel, n_dom, n_slab),
        out_shape=[
            jax.ShapeDtypeStruct((n_dom * n_slab, 8, LANES), F32),
            jax.ShapeDtypeStruct((count, force.shape[1]), BF16),
            jax.ShapeDtypeStruct((8, ghost_pick.shape[1]), jnp.int32),
        ],
        in_specs=[pl.BlockSpec(memory_space=pl.ANY)] * len(inputs),
        out_specs=[VMEM] * 3,
        scratch_shapes=[pltpu.VMEM(one.shape, one.dtype) for one in inputs[:7]]
        + [pltpu.VMEM((n_dom, 8, cap), F32), pltpu.SemaphoreType.DMA((8 + update.shape[0],))],
        compiler_params=params(63),
        name="send_states",
    )(*inputs)


def store_tile(doubled, tile, pool_ref):
    live = doubled[3:4] > 0.5
    for word in range(3):
        pool_ref[tile, word] = jnp.broadcast_to(jnp.where(live, doubled[word : word + 1], AWAY), (8, LANES))


def find_rows(tables, lane, group, groups):
    onehot = (iota((LANES, LANES), 0) == lane).astype(F32).astype(BF16)
    found = sum(jnp.dot(table, onehot, preferred_element_type=F32) for table in (tables[0], tables[2], tables[1]))
    total = jnp.zeros((8, LANES), F32)
    for one in range(groups):
        total = total + jnp.where(group == one, found[one * 8 : (one + 1) * 8], 0.0)
    return total


def build_pool(n_dom, n_slab, cap, ghost_rows, recv_ref, emb_ref, pool_ref, column_ref, around_ref, taken_ref, h_ref, kind_ref):
    me_dom, me_slab = lax.axis_index("dom"), lax.axis_index("slab")
    atom_rows = column_ref.shape[0]
    local_tiles = atom_rows // TILE
    before, after = lax.rem(me_slab + n_slab - 1, n_slab), lax.rem(me_slab + 1, n_slab)
    per = TILE // cap
    half = iota((1, LANES), 1) < TILE
    for pair in range(local_tiles // 2):
        kinds = []
        for tile in (2 * pair, 2 * pair + 1):
            parts = [recv_ref[(tile * per + p) * n_slab + me_slab, 0:8, :][:, :cap] for p in range(per)]
            doubled = jnp.concatenate(parts * 2, axis=1)
            store_tile(doubled, tile, pool_ref)
            column = doubled.T[:TILE]
            live = column[:, 3:4] > 0.5
            spot = iota((TILE, 8), 1)
            column_ref[tile * TILE : (tile + 1) * TILE, :] = jnp.where((spot >= 3) | live, column, -AWAY)
            kinds.append(doubled[3:4])
        kind_ref[0:1, pair * LANES : (pair + 1) * LANES] = jnp.where(half, kinds[0], kinds[1])

    def rows_of(slab):
        return jnp.concatenate([recv_ref[e * n_slab + slab, 0:8, :] for e in range(n_dom)], axis=0)

    own = pieces(rows_of(me_slab))
    below = pieces(rows_of(before))
    above = below if n_slab == 2 else pieces(rows_of(after))
    own_at = me_dom * n_slab
    width = ghost_rows // LANES
    sources = (
        (lax.rem(me_dom + n_dom - 1, n_dom) * n_slab + me_slab, 4, own, TILE, 0),
        (lax.rem(me_dom + 1, n_dom) * n_slab + me_slab, 4, own, 0, 4),
        (own_at + before, 4, below, 0, 0),
        (own_at + after, 0, above, 0, 0),
    )
    shift = cap.bit_length() - 1
    bits = atom_rows.bit_length() - 1
    for face, (origin, place, tables, lane_start, row_start) in enumerate(sources):
        packed = recv_ref[origin, place : place + 4, :][:, TILE:].astype(jnp.int32)
        around_ref[face : face + 1, :] = jnp.concatenate([packed[width : width + 1]] * 2, axis=1)
        lines = [packed[r : r + 1] for r in range(width)]
        thirds = [line & (atom_rows - 1) for line in lines] + [line >> bits for line in lines]
        for m in range(width):
            pick = jnp.concatenate(thirds[2 * m : 2 * m + 2], axis=1)
            taken_ref[face : face + 1, m * LANES : (m + 1) * LANES] = pick
            total = find_rows(tables, (pick & (cap - 1)) + lane_start, pick >> shift, n_dom)
            if row_start:
                total = pltpu.roll(total, 4, 0)
            swapped = pltpu.roll(total, TILE, 1)
            tile = local_tiles + (face * ghost_rows) // TILE + 2 * m
            store_tile(jnp.where(half, total, swapped), tile, pool_ref)
            store_tile(jnp.where(half, swapped, total), tile + 1, pool_ref)
            spot = tile * TILE
            kind_ref[0:1, spot : spot + LANES] = total[3:4]
    table = emb_ref[...]
    step = 512
    for start in range(0, h_ref.shape[0], step):
        kinds = kind_ref[0:1, start : start + step].astype(jnp.int32)
        onehot = (iota((16, step), 0) == kinds - 1).astype(F32).astype(BF16)
        h_ref[start : start + step, :] = lax.dot_general(onehot, table, (((0,), (0,)), ((), ())), preferred_element_type=F32).astype(BF16)


class Near:
    def __init__(self, table_ref, shape):
        self.table_ref, self.shape = table_ref, shape

    def __getitem__(self, at):
        return self.table_ref[FACES + at[0], at[1]]


def half_rows(near_ref, pool_ref, tile, side):
    first, second = near_ref[2 * side, tile], near_ref[2 * side + 1, tile]
    lane = iota((8, LANES), 1)
    left = lane < TILE
    xyz = [jnp.where(left, pool_ref[first, w], pool_ref[second, w]) for w in range(3)]
    rows = jnp.where(left, first * TILE, second * TILE) + (lane & (TILE - 1))
    return first, second, xyz, rows


def tall(value, count):
    return jnp.concatenate([value] * count, axis=0) if count > 1 else value


def geometry(column_ref, start, count, xyz, rows):
    column = column_ref[pl.ds(start, count), :]
    offset = [tall(xyz[w], count // 8) - column[:, w : w + 1] for w in range(3)]
    square = offset[0] * offset[0] + offset[1] * offset[1] + offset[2] * offset[2] + SOFTENING
    inverse = lax.rsqrt(square)
    ratio = jnp.minimum(square * inverse * (1.0 / CUTOFF), 1.0)
    same = tall(rows, count // 8) == iota((count, LANES), 0) + start
    ratio = jnp.where(same, 1.0, ratio)
    fade = 1.0 - ratio * ratio
    return offset, inverse, ratio, fade * fade


def edges_of(column_ref, start, count, xyz, rows):
    offset, inverse, ratio, envelope = geometry(column_ref, start, count, xyz, rows)
    x, y, z = (part * inverse for part in offset)
    harmonic = [x, y, z, x * y, y * z, z * x, (x - y) * (x + y), 3.0 * (z * z) - 1.0]
    shifted = ratio - 0.5
    square = shifted * shifted
    sine = series(COS_TERMS, square)
    cosine = -shifted * series(SIN_TERMS, square)
    twice = cosine + cosine
    radial = [sine * (envelope * inverse)]
    radial.append(twice * radial[0])
    while len(radial) < 8:
        radial.append(twice * radial[-1] - radial[-2])
    return harmonic, radial


def store_part(near_ref, pool_ref, column_ref, tile, side, part, harmonic_ref, radial_ref):
    chunk = 16
    _, _, xyz, rows = half_rows(near_ref, pool_ref, tile, side)
    spot = slice(part * chunk, (part + 1) * chunk)
    harmonic, radial = edges_of(column_ref, pl.multiple_of(tile * TILE + part * chunk, chunk), chunk, xyz, rows)
    for k, one in enumerate(harmonic):
        harmonic_ref[k, spot, :] = one.astype(BF16)
    for n, one in enumerate(radial):
        radial_ref[n, spot, :] = one.astype(BF16)
    return jnp.maximum(radial[-1][:8], radial[-1][8:])[:1]


def side_sum(near_ref, h_ref, weight_ref, tile, side, harmonic_ref, radial_ref, gates):
    nears = [near_ref[2 * side + place, tile] for place in range(2)]
    features = jnp.concatenate([h_ref[pl.ds(pl.multiple_of(other * TILE, TILE), TILE), :] for other in nears], axis=0)
    nbasis = weight_ref.shape[0]
    radial = [radial_ref[n] for n in range(nbasis)]
    rows = [jnp.concatenate(radial, axis=1)]
    for k in range(NHARM - 1):
        harmonic = harmonic_ref[k]
        rows.append(jnp.concatenate([harmonic * one for one in radial], axis=1))
    weight = weight_ref[...].astype(F32)
    steps = []
    for m in range(nbasis // 2):
        part = weight[2 * m : 2 * m + 2]
        for one in gates[m]:
            part = jnp.where(one < 1e30, part, 0.0)
        part = part.astype(BF16)
        steps += [features * part[n : n + 1] for n in range(2)]
    return jnp.dot(jnp.concatenate(rows, axis=0), jnp.concatenate(steps, axis=0), preferred_element_type=F32)


def store_query(agg_ref, tile, query_ref):
    channels = agg_ref.shape[1]
    part = [agg_ref[k * TILE : (k + 1) * TILE, :] * (1.0 / TILE**0.5) for k in range(NHARM)]
    square = [one * one for one in part]
    query = [part[0], square[0], square[1] + square[2] + square[3], square[4] + square[5] + square[6] + square[7] + square[8]]
    start = pl.multiple_of(tile * TILE, TILE)
    for spot, one in enumerate(query):
        query_ref[pl.ds(start, TILE), spot * channels : (spot + 1) * channels] = one.astype(BF16)
    return query[-1][:1]


def run_layer(turns, near_ref, pool_ref, column_ref, h_ref, weight_ref, update_ref, out_ref, query_ref, agg_ref, harm_now, harm_next, radial_now, radial_next):
    tiles = near_ref.shape[1]

    harmonics, radials = (harm_now, harm_next), (radial_now, radial_next)

    def make(tile, unit, slot):
        side, part = divmod(unit, 4)
        return store_part(near_ref, pool_ref, column_ref, tile, side, part, harmonics[slot].at[side], radials[slot].at[side])

    for unit in range(8):
        make(0, unit, 0)
    agg_ref[...] = jnp.zeros_like(agg_ref)

    def step(index, carry):
        for turn in range(turns):
            slot = turn % 2
            tile = turns * index + turn
            later = jnp.minimum(tile + 1, tiles - 1)
            query = store_query(agg_ref, jnp.maximum(tile - 1, 0), query_ref)
            units = [make(later, unit, 1 - slot) for unit in range(8)]
            gates = ((), (), (), ())
            sides = [side_sum(near_ref, h_ref, weight_ref, tile, side, harmonics[slot].at[side], radials[slot].at[side], gates) for side in range(2)]
            agg_ref[...] = sides[0] + sides[1]
        return carry

    lax.fori_loop(0, tiles // turns, step, 0)
    store_query(agg_ref, tiles - 1, query_ref)
    changes = jnp.dot(query_ref[...], update_ref[...], preferred_element_type=F32)
    block = 256
    for start in range(0, out_ref.shape[0], block):
        update = changes[start : start + block]
        live = (column_ref[start : start + block, 3:4] > 0.5).astype(F32)
        fresh = h_ref[start : start + block, :].astype(F32) + update * (1.0 / (1.0 + jnp.exp(-update)))
        out_ref[start : start + block, :] = (fresh * live).astype(BF16)


def spread(refs, size):
    return [(ref, start) for ref in refs for start in range(0, ref.shape[0], size)]


def is_even():
    return lax.rem(lax.axis_index("dom"), 2) == 0


def gather_rows(pick_ref, tasks, keep=None):
    ghost_rows = pick_ref.shape[1]
    picks = pick_ref[...].astype(F32)
    if keep is not None:
        picks = jnp.concatenate([jnp.where(keep, picks[0:1], picks[1:2]), jnp.where(keep, picks[1:2], picks[0:1]), picks[2:]], axis=0)
    if picks.shape[0] < 8:
        picks = jnp.concatenate([picks, jnp.zeros((8 - picks.shape[0], ghost_rows), F32)], axis=0)
    columns = [picks[:, m * LANES : (m + 1) * LANES].T.astype(jnp.int32) for m in range(ghost_rows // LANES)]
    sources = []
    for _, source, _, _ in tasks:
        if not any(source is one for one in sources):
            sources.append(source)
    for source in sources:
        here = [task for task in tasks if task[1] is source]
        onehot = [(column[:, task[0] : task[0] + 1] == iota((LANES, source.shape[0]), 1)).astype(F32).astype(BF16) for task in here for column in columns]
        found = jnp.dot(jnp.concatenate(onehot, axis=0), source[...], preferred_element_type=F32).astype(BF16)
        for spot, (_, _, target, start) in enumerate(here):
            target[pl.ds(start if isinstance(start, int) else pl.multiple_of(start, LANES), ghost_rows), :] = found[spot * ghost_rows : (spot + 1) * ghost_rows]


def views(weights_ref, spot):
    radial, nbasis, update, depth = spot
    return weights_ref.at[radial : radial + nbasis], weights_ref.at[update : update + depth]


def first_kernel(n_dom, n_slab, cap, n_out, spot, emb_spot, tiles, table_ref, recv_ref, weights_ref, numbers_ref, *rest):
    near_ref = Near(table_ref, tiles)
    pick_ref = numbers_ref
    emb_ref = weights_ref.at[emb_spot : emb_spot + 16]
    pool_ref, column_ref, around_ref, taken_ref, kept_ref, out_ref = rest[:6]
    outs = rest[6 : 6 + n_out]
    *scratch, h_ref, kind_ref = rest[6 + n_out :]
    kept_ref[...] = weights_ref[...]
    build_pool(n_dom, n_slab, cap, pick_ref.shape[1], recv_ref, emb_ref, pool_ref, column_ref, around_ref, taken_ref, h_ref, kind_ref)
    run_layer(4, near_ref, pool_ref, column_ref, h_ref, *views(weights_ref, spot), out_ref, *scratch)
    gather_rows(pick_ref, [(face, out_ref, ref, start) for face, (ref, start) in enumerate(spread(outs, pick_ref.shape[1]))], is_even())


def second_kernel(n_in, spot, force_spot, tiles, table_ref, list_ref, pool_ref, column_ref, h_in_ref, *rest):
    near_ref = Near(table_ref, tiles)
    ghosts = rest[:n_in]
    weights_ref, out_ref, g_ref = rest[n_in : n_in + 3]
    *scratch, h_ref = rest[n_in + 3 :]
    atom_rows, ghost_rows = h_in_ref.shape[0], ghosts[0].shape[0]
    even = is_even().astype(jnp.int32)
    h_ref[0:atom_rows, :] = h_in_ref[...]
    for block, ref in zip((even, 1 - even), ghosts):
        h_ref[pl.ds(pl.multiple_of(atom_rows + block * ghost_rows, LANES), ghost_rows), :] = ref[...]
    start = atom_rows + 2 * ghost_rows
    for ref in ghosts[2:]:
        h_ref[start : start + ref.shape[0], :] = ref[...]
        start += ref.shape[0]
    run_layer(16, near_ref, pool_ref, column_ref, h_ref, *views(weights_ref, spot), out_ref, *scratch)
    g_ref[...] = jnp.dot(out_ref[...], weights_ref[force_spot:, :], preferred_element_type=F32).astype(BF16)


def layer_scratch(nbasis, near, channels, atom_rows, pool_rows):
    half = near * TILE // 2
    return [
        pltpu.VMEM((atom_rows, 4 * channels), BF16),
        pltpu.VMEM((NHARM * TILE, channels), F32),
        *[pltpu.VMEM((2, NHARM - 1, TILE, half), BF16)] * 2,
        *[pltpu.VMEM((2, nbasis, TILE, half), BF16)] * 2,
        pltpu.VMEM((pool_rows, channels), BF16),
    ]


def list_blocks(near_ref, around_ref, atom_tiles, face_tiles, early_ref, late_ref):
    near = near_ref.shape[0]
    pool_tiles = atom_tiles + FACES * face_tiles
    spare = (5 * atom_tiles) * 128 + pool_tiles + FACES * face_tiles
    first_slab = atom_tiles + 2 * face_tiles

    def own(tile, counts):
        early, late = counts
        for k in range(near):
            other = near_ref[k, tile]
            entry = tile * 128 + other
            with_dom = ((other >= atom_tiles) & (other < first_slab)).astype(jnp.int32)
            early_ref[early] = entry
            late_ref[late] = entry
            early, late = early + 1 - with_dom, late + with_dom
        return early, late

    counts = lax.fori_loop(0, atom_tiles, own, (jnp.int32(0), jnp.int32(0)))

    def of_others(ref, pairs):
        def others(tile, count):
            for domain, face in pairs:
                start = atom_tiles + face * face_tiles
                for k in range(near):
                    other = around_ref[domain, k * atom_tiles + tile] - start
                    ref[count] = (atom_tiles * (domain + 1) + tile) * 128 + pool_tiles + face * face_tiles + other
                    count = count + ((other >= 0) & (other < face_tiles)).astype(jnp.int32)
            return count

        return others

    early = lax.fori_loop(0, atom_tiles, of_others(early_ref, ((2, 3), (3, 2))), counts[0])
    late = lax.fori_loop(0, atom_tiles, of_others(late_ref, ((0, 1), (1, 0))), counts[1])
    for extra in range(7):
        early_ref[early + extra] = spare
        late_ref[late + extra] = spare
    return early, late


def block_pair(first, second, atom_tiles, pool_ref, column_ref, gi_ref, gj_ref):
    scale = 1.0 / gi_ref.shape[1] ** 0.5
    lane = iota((8, LANES), 1)
    left = lane < TILE
    half = iota((TILE, LANES), 1) < TILE
    i_tiles = [pl.multiple_of((one >> 7) * TILE, TILE) for one in (first, second)]
    j_tiles = [one & 127 for one in (first, second)]
    same = [jnp.where((one >> 7 == one & 127) & (one >> 7 < atom_tiles), 0, 4096) for one in (first, second)]
    rows = jnp.where(left, same[0], same[1]) + (lane & (TILE - 1))
    columns = [column_ref[pl.ds(one, TILE), :] for one in i_tiles]
    mine = jnp.concatenate([gi_ref[pl.ds(one, TILE), :] for one in i_tiles], axis=0)
    others = jnp.concatenate([gj_ref[pl.ds(pl.multiple_of(one * TILE, TILE), TILE), :] for one in j_tiles], axis=0)
    inner = lax.dot_general(mine, others, (((1,), (1,)), ((), ())), preferred_element_type=F32)
    inner = jnp.where(half, inner[:TILE], inner[TILE:])
    offset = []
    for w in range(3):
        away = tall(jnp.where(left, pool_ref[j_tiles[0], w], pool_ref[j_tiles[1], w]), TILE // 8)
        offset.append(away - jnp.where(half, columns[0][:, w : w + 1], columns[1][:, w : w + 1]))
    square = offset[0] * offset[0] + offset[1] * offset[1] + offset[2] * offset[2] + SOFTENING
    inverse = lax.rsqrt(square)
    ratio = jnp.minimum(square * inverse * (1.0 / CUTOFF), 1.0)
    ratio = jnp.where(tall(rows, TILE // 8) == iota((TILE, LANES), 0), 1.0, ratio)
    fade = 1.0 - ratio * ratio
    strength = fade * fade * inverse * (inner * scale)
    return [strength * one for one in offset]


def sum_blocks(list_ref, count, atom_tiles, pool_ref, column_ref, gi_ref, gj_ref, own_ref, total_ref):
    own_ref[...] = jnp.zeros_like(own_ref)
    total_ref[...] = jnp.zeros_like(total_ref)
    left = iota((8, LANES), 1) < TILE
    half = iota((TILE, LANES), 1) < TILE

    def step(index, carry):
        entries = [list_ref[8 * index + spot] for spot in range(8)]
        found = [block_pair(entries[2 * p], entries[2 * p + 1], atom_tiles, pool_ref, column_ref, gi_ref, gj_ref) for p in range(4)]
        for p in range(4):
            for spot in range(2):
                entry = entries[2 * p + spot]
                i_tile, j_tile = jnp.minimum(entry >> 7, atom_tiles), entry & 127
                for w in range(3):
                    pair = found[p][w]
                    against = sum(pair[8 * v : 8 * v + 8] for v in range(TILE // 8))
                    total_ref[j_tile, w] -= jnp.where(left, against, 0.0) if spot == 0 else jnp.where(left, 0.0, against)
                    own_ref[i_tile, w] += jnp.where(half, pair, 0.0) if spot == 0 else jnp.where(half, 0.0, pair)
        return carry

    lax.fori_loop(0, (count + 7) // 8, step, 0)


def gather_forces(pick_ref, faces, atom_tiles, face_tiles, own_ref, total_ref):
    atom_rows = atom_tiles * TILE
    pool_tiles = atom_tiles + FACES * face_tiles
    half = iota((1, LANES), 1) < TILE
    sums = []
    for w in range(3):
        folded = jnp.sum(total_ref[:, w], axis=1)
        sums.append(folded + pltpu.roll(folded, TILE, 1))

    def row(tile):
        lines = [jnp.where(half, sums[w][tile : tile + 1], sums[w][tile + 1 : tile + 2]) for w in range(3)]
        return jnp.concatenate(lines + [jnp.zeros((5, LANES), F32)], axis=0)

    blocks = atom_rows // LANES
    shift = LANES.bit_length() - 1
    total = jnp.concatenate([row(2 * m) for m in range(blocks)], axis=0)
    for face in faces:
        for m in range(face_tiles // 2):
            pick = pick_ref[face : face + 1, m * LANES : (m + 1) * LANES]
            back = row(pool_tiles + face * face_tiles + 2 * m)
            high = pick >> shift
            wide = jnp.concatenate([jnp.where(high == one, back, 0.0) for one in range(blocks)], axis=0)
            onehot = (iota((LANES, LANES), 0) == (pick & (LANES - 1))).astype(F32).astype(BF16)
            for part in pieces(wide)[:2]:
                total = total + lax.dot_general(part, onehot, (((1,), (1,)), ((), ())), preferred_element_type=F32)
    total = jnp.concatenate([total[m * 8 : (m + 1) * 8] for m in range(blocks)], axis=1)
    for w in range(3):
        ones = (iota((8, LANES), 0) == w).astype(F32).astype(BF16)
        mine = jnp.concatenate([own_ref[tile, w] for tile in range(atom_tiles)], axis=0)
        for part in pieces(mine)[:2]:
            total = total + lax.dot_general(ones, part, (((1,), (1,)), ((), ())), preferred_element_type=F32)
    return total


def neighbour_kernel(n_dom, n_slab, cap, tiles, table_ref, around_ref, recv_ref, numbers_ref, pool_in, column_in, early_ref, late_ref, pool_ref, column_ref):
    near_ref = Near(table_ref, tiles)
    pick_ref = numbers_ref
    atom_rows, ghost_rows = column_in.shape[0], pick_ref.shape[1]
    atom_tiles, face_tiles = atom_rows // TILE, ghost_rows // TILE
    pool_tiles = atom_tiles + FACES * face_tiles
    me_slab = lax.axis_index("slab")
    before, after = lax.rem(me_slab + n_slab - 1, n_slab), lax.rem(me_slab + 1, n_slab)
    early, late = list_blocks(near_ref, around_ref, atom_tiles, face_tiles, early_ref.at[0], late_ref.at[0])
    early_ref[1, 0] = early
    late_ref[1, 0] = late
    column_ref[0:atom_rows, :] = column_in[...]
    column_ref[5 * atom_rows :, :] = jnp.full((TILE, 8), -AWAY, F32)
    per = TILE // cap
    spot = iota((TILE, 8), 1)

    def put(domain, tile, column):
        live = column[:, 3:4] > 0.5
        start = atom_rows * (domain + 1) + tile * TILE
        column_ref[start : start + TILE, :] = jnp.where((spot >= 3) | live, column, -AWAY)

    def tile_of(slab, tile):
        parts = [recv_ref[(tile * per + p) * n_slab + slab] for p in range(per)]
        return jnp.concatenate([one[:, start : start + cap] for start in (0, TILE) for one in parts], axis=1)

    for tile in range(atom_tiles):
        block = tile_of(me_slab, tile)
        put(0, tile, block.T[TILE:])
        put(1, tile, pltpu.roll(block, 4, 0).T[:TILE])
        below = tile_of(before, tile).T[:TILE]
        put(2, tile, below)
        put(3, tile, below if n_slab == 2 else tile_of(after, tile).T[:TILE])
    pool_ref[0:pool_tiles] = pool_in[...]
    pool_ref[pool_tiles + FACES * face_tiles] = jnp.full((3, 8, LANES), AWAY, F32)
    own = pieces(jnp.concatenate([recv_ref[e * n_slab + me_slab] for e in range(n_dom)], axis=0))
    shift = cap.bit_length() - 1
    half = iota((1, LANES), 1) < TILE
    for face in range(FACES):
        for m in range(ghost_rows // LANES):
            pick = pick_ref[face : face + 1, m * LANES : (m + 1) * LANES]
            total = find_rows(own, pick & (cap - 1), pick >> shift, n_dom)
            swapped = pltpu.roll(total, TILE, 1)
            tile = pool_tiles + face * face_tiles + 2 * m
            store_tile(jnp.where(half, total, swapped), tile, pool_ref)
            store_tile(jnp.where(half, swapped, total), tile + 1, pool_ref)


def near_forces_kernel(n_slab, list_ref, numbers_ref, taken_ref, pool_ref, column_ref, g_ref, *rest):
    pick_ref = numbers_ref
    slabs = rest[: 1 if n_slab == 2 else 2]
    part_ref, out_g_ref, gi_ref, gj_ref, own_ref, total_ref = rest[len(slabs) :]
    atom_rows, channels = g_ref.shape
    ghost_rows = pick_ref.shape[1]
    atom_tiles, face_tiles = atom_rows // TILE, ghost_rows // TILE
    pool_tiles = atom_tiles + FACES * face_tiles
    gi_ref[0:atom_rows, :] = g_ref[...]
    gj_ref[0:atom_rows, :] = g_ref[...]
    spare = jnp.zeros((TILE, channels), BF16)
    gi_ref[5 * atom_rows :, :] = spare
    gj_ref[(pool_tiles + FACES * face_tiles) * TILE :, :] = spare
    gi_ref[3 * atom_rows : 4 * atom_rows, :] = slabs[0][...]
    gi_ref[4 * atom_rows : 5 * atom_rows, :] = slabs[-1][...]
    gather_rows(pick_ref, [(face, g_ref, gj_ref, pool_tiles * TILE + face * ghost_rows) for face in range(FACES)])
    gather_rows(taken_ref, [(face, ref, gj_ref, atom_rows + face * ghost_rows) for face, ref in ((2, slabs[0]), (3, slabs[-1]))])
    out_g_ref[...] = gj_ref[pool_tiles * TILE : pool_tiles * TILE + 2 * ghost_rows, :]
    sum_blocks(list_ref.at[0], list_ref[1, 0], atom_tiles, pool_ref, column_ref, gi_ref, gj_ref, own_ref, total_ref)
    part_ref[...] = gather_forces(pick_ref, (2, 3), atom_tiles, face_tiles, own_ref, total_ref)


def far_forces_kernel(list_ref, numbers_ref, taken_ref, pool_ref, column_ref, g_ref, out_g_ref, first_ref, second_ref, part_ref, out_ref, gi_ref, gj_ref, own_ref, total_ref):
    pick_ref = numbers_ref
    atom_rows, channels = g_ref.shape
    ghost_rows = pick_ref.shape[1]
    atom_tiles, face_tiles = atom_rows // TILE, ghost_rows // TILE
    pool_tiles = atom_tiles + FACES * face_tiles
    spare = jnp.zeros((TILE, channels), BF16)
    gi_ref[0:atom_rows, :] = g_ref[...]
    even = is_even().astype(jnp.int32)
    spots = (even, 1 - even)
    for spot, ref in zip(spots, (first_ref, second_ref)):
        gi_ref[pl.ds(pl.multiple_of((1 + spot) * atom_rows, LANES), atom_rows), :] = ref[...]
    gi_ref[5 * atom_rows :, :] = spare
    gj_ref[pool_tiles * TILE : pool_tiles * TILE + 2 * ghost_rows, :] = out_g_ref[...]
    gj_ref[(pool_tiles + FACES * face_tiles) * TILE :, :] = spare
    gather_rows(taken_ref, [(face, ref, gj_ref, atom_rows + spots[face] * ghost_rows) for face, ref in ((0, first_ref), (1, second_ref))], even == 0)
    sum_blocks(list_ref.at[0], list_ref[1, 0], atom_tiles, pool_ref, column_ref, gi_ref, gj_ref, own_ref, total_ref)
    total = gather_forces(pick_ref, (0, 1), atom_tiles, face_tiles, own_ref, total_ref) + part_ref[...]
    out_ref[...] = total[0:3]


def passed_along(array, axis, by):
    count = lax.axis_size(axis)
    return lax.ppermute(array, axis, [(i, (i + by) % count) for i in range(count)])


def swapped(first, second):
    count = lax.axis_size("dom")
    ends = lax.ppermute(second, "dom", [(i, (i - 1 if i % 2 == 0 else i + 1) % count) for i in range(count)])
    return lax.ppermute(first, "dom", [(i, i + 1 if i % 2 == 0 else i - 1) for i in range(count)]), ends


def body(n_dom, n_slab, positions, species, send_pick, ghost_pick, near_tiles, embedding, radial_weight, update_weight, force_weight):
    atom_rows = positions.shape[0]
    cap = send_pick.shape[1]
    ghost_rows = ghost_pick.shape[1]
    tiles, near = near_tiles.shape
    channels = embedding.shape[1]
    nbasis = radial_weight.shape[1]
    pool_rows = atom_rows + FACES * ghost_rows
    face_rows = [ghost_rows, ghost_rows] + ([2 * ghost_rows] if n_slab == 2 else [ghost_rows, ghost_rows])
    n_out = len(face_rows)
    face_out = [jax.ShapeDtypeStruct((rows, channels), BF16) for rows in face_rows]
    face_tiles = ghost_rows // TILE
    i_rows = 5 * atom_rows + TILE
    j_tiles = pool_rows // TILE + FACES * face_tiles + 1
    longest = (near * tiles) * 5 + 8
    scratch = layer_scratch(nbasis, near, channels, atom_rows, pool_rows)

    sent, weights, numbers = send_states(n_dom, n_slab, positions, species, send_pick, ghost_pick, near_tiles, embedding, radial_weight, update_weight, force_weight)
    update_spot, force_spot = weight_spots(radial_weight.shape, update_weight.shape)
    spots = [(16 * m, nbasis, at, update_weight.shape[1]) for m, at in enumerate(update_spot)]
    got = lax.all_to_all(sent, ("dom", "slab"), split_axis=0, concat_axis=0, tiled=True)

    pool, column, around, taken, kept, hidden, *faces = pl.pallas_call(
        functools.partial(first_kernel, n_dom, n_slab, cap, n_out, spots[0], 16 * len(spots), (near, tiles)),
        out_shape=[
            jax.ShapeDtypeStruct((pool_rows // TILE, 3, 8, LANES), F32),
            jax.ShapeDtypeStruct((atom_rows, 8), F32),
            jax.ShapeDtypeStruct((8, LANES), jnp.int32),
            jax.ShapeDtypeStruct((8, ghost_rows), jnp.int32),
            jax.ShapeDtypeStruct(weights.shape, BF16),
            jax.ShapeDtypeStruct((atom_rows, channels), BF16),
        ]
        + face_out,
        in_specs=[SMEM] + [VMEM] * 3,
        out_specs=[VMEM] * (6 + n_out),
        scratch_shapes=scratch + [pltpu.VMEM((8, pool_rows), F32)],
        compiler_params=params(),
        name="first_layer",
    )(numbers, got, weights, numbers)

    early, late, wide_pool, wide_column = pl.pallas_call(
        functools.partial(neighbour_kernel, n_dom, n_slab, cap, (near, tiles)),
        out_shape=[
            jax.ShapeDtypeStruct((2, longest), jnp.int32),
            jax.ShapeDtypeStruct((2, longest), jnp.int32),
            jax.ShapeDtypeStruct((j_tiles, 3, 8, LANES), F32),
            jax.ShapeDtypeStruct((i_rows, 8), F32),
        ],
        in_specs=[SMEM] * 2 + [VMEM] * 4,
        out_specs=[SMEM] * 2 + [VMEM] * 2,
        compiler_params=params(),
        name="neighbours",
    )(numbers, around, got, numbers, pool, column)
    faces = [*swapped(*faces[:2]), *(passed_along(one, "slab", way) for one, way in zip(faces[2:], (1, -1)))]
    features, mine = pl.pallas_call(
        functools.partial(second_kernel, n_out, spots[1], force_spot, (near, tiles)),
        out_shape=[jax.ShapeDtypeStruct((atom_rows, channels), BF16)] * 2,
        in_specs=[SMEM] * 2 + [VMEM] * (4 + n_out),
        out_specs=[VMEM] * 2,
        scratch_shapes=scratch,
        compiler_params=params(),
        name="second_layer",
    )(numbers, early, pool, column, hidden, *faces, kept)

    slabs = [passed_along(mine, "slab", 1)]
    if n_slab != 2:
        slabs.append(passed_along(mine, "slab", -1))
    first, second = swapped(mine, mine)
    force_scratch = [
        pltpu.VMEM((i_rows, channels), BF16),
        pltpu.VMEM((j_tiles * TILE, channels), BF16),
        pltpu.VMEM((tiles + 1, 3, TILE, LANES), F32),
        pltpu.VMEM((j_tiles, 3, 8, LANES), F32),
    ]
    part, out_g = pl.pallas_call(
        functools.partial(near_forces_kernel, n_slab),
        out_shape=[jax.ShapeDtypeStruct((8, atom_rows), F32), jax.ShapeDtypeStruct((2 * ghost_rows, channels), BF16)],
        in_specs=[SMEM] + [VMEM] * (5 + len(slabs)),
        out_specs=[VMEM] * 2,
        scratch_shapes=force_scratch,
        cost_estimate=pl.CostEstimate(flops=4_000_000_000, bytes_accessed=4_000_000, transcendentals=0),
        compiler_params=params(),
        name="near_forces",
    )(early, numbers, taken, wide_pool, wide_column, mine, *slabs)
    forces = pl.pallas_call(
        far_forces_kernel,
        out_shape=jax.ShapeDtypeStruct((3, atom_rows), F32),
        in_specs=[SMEM] + [VMEM] * 9,
        out_specs=VMEM,
        scratch_shapes=force_scratch,
        compiler_params=params(),
        name="far_forces",
    )(late, numbers, taken, wide_pool, wide_column, mine, out_g, first, second, part)
    return features, forces


def solution(mesh):
    both = ("dom", "slab")
    return jax.shard_map(
        functools.partial(body, mesh.shape["dom"], mesh.shape["slab"]),
        mesh=mesh,
        in_specs=(P(both, None), P(both), P(both, None), P(both, None), P(both, None), P(), P(), P(), P()),
        out_specs=(P(both, None), P(None, both)),
        check_vma=False,
    )
```

```python
import functools

import jax
import jax.numpy as jnp
from jax import lax
from jax.experimental import pallas as pl
from jax.experimental.pallas import tpu as pltpu
from jax.sharding import PartitionSpec as P

LAYERS = 2
TILE = 64
LANES = 128
FACES = 4
NHARM = 9
AWAY = 1000.0
CUTOFF = 6.0
SOFTENING = 0.25
F32 = jnp.float32
BF16 = jnp.bfloat16

COS_TERMS = (1.0, -4.934802200544679, 4.058712126416768, -1.3352627688545893, 0.2353306303588935, -0.02580689139001406)
SIN_TERMS = (3.141592653589793, -5.16771278004997, 2.550164039877345, -0.5992645293207921, 0.08214588661112823, -0.00737043094571435)

VMEM = pl.BlockSpec(memory_space=pltpu.VMEM)
SMEM = pl.BlockSpec(memory_space=pltpu.SMEM)


def params(mib=40):
    return pltpu.CompilerParams(vmem_limit_bytes=int(mib * 1024 * 1024))


def pieces(value):
    top = value.astype(BF16)
    rest = value - top.astype(F32)
    middle = rest.astype(BF16)
    low = (rest - middle.astype(F32)).astype(BF16)
    return top, middle, low


def series(terms, square):
    total = jnp.full_like(square, terms[-1])
    for term in reversed(terms[:-1]):
        total = total * square + term
    return total


def iota(shape, dim):
    return lax.broadcasted_iota(jnp.int32, shape, dim)


def send_kernel(n_dom, n_slab, pos_in, kind_in, pick_in, ghost_in, near_in, embedding_in, radial_in, update_in, force_in, out_ref, weights_ref,
                pos_ref, kind_ref, pick_ref, ghost_ref, near_ref, embedding_ref, radial_ref, picked_ref, sems):
    update_spot, force_spot = weight_spots(radial_in.shape, update_in.shape)
    pairs = [(pos_in, pos_ref), (kind_in, kind_ref), (pick_in, pick_ref), (ghost_in, ghost_ref), (near_in, near_ref), (embedding_in, embedding_ref), (radial_in, radial_ref)]
    pairs += [(update_in.at[m], weights_ref.at[spot : spot + update_in.shape[1]]) for m, spot in enumerate(update_spot)]
    pairs += [(force_in, weights_ref.at[force_spot : force_spot + force_in.shape[0]])]
    copies = []
    for spot, (source, target) in enumerate(pairs):
        copies.append(pltpu.make_async_copy(source, target, sems.at[spot]))
        copies[-1].start()
    for copy in copies:
        copy.wait()
    beside = jnp.zeros((near_ref.shape[0], ghost_ref.shape[1] - near_ref.shape[1]), jnp.int32)
    numbers = jnp.concatenate([ghost_ref[...], jnp.concatenate([near_ref[...], beside], axis=1)], axis=0)
    parts = [part[:, m * LANES : (m + 1) * LANES] for part in (numbers >> 5, numbers & 31) for m in range(numbers.shape[1] // LANES)]
    number_spot = force_spot + force_in.shape[0]
    weights_ref[number_spot:, :] = jnp.concatenate(parts, axis=0).astype(F32).astype(BF16)
    blank = jnp.zeros((16, embedding_ref.shape[1]), F32)
    for level in range(radial_ref.shape[0]):
        weights_ref[16 * level : 16 * level + 16, :] = jnp.concatenate([radial_ref[level].astype(F32), blank[radial_ref.shape[1] :]], axis=0).astype(BF16)
    spot = 16 * radial_ref.shape[0]
    weights_ref[spot : spot + 16, :] = jnp.concatenate([embedding_ref[...].astype(F32), blank[embedding_ref.shape[0] :]], axis=0).astype(BF16)
    rows = pos_ref.shape[1]
    cap = pick_ref.shape[1]
    blocks = rows // LANES
    state = jnp.concatenate([pos_ref[...], kind_ref[...].astype(F32) + 1.0], axis=0)
    top, middle, low = (part.astype(F32) for part in pieces(state))
    table = jnp.concatenate([top, middle, low, jnp.zeros_like(low)], axis=0).astype(BF16)
    table = jnp.concatenate([table[:, m * LANES : (m + 1) * LANES] for m in range(blocks)], axis=0)
    shift = LANES.bit_length() - 1
    for dest in range(n_dom):
        pick = pick_ref[dest : dest + 1, :]
        onehot = (iota((LANES, cap), 0) == (pick & (LANES - 1))).astype(F32).astype(BF16)
        found = jnp.dot(table, onehot, preferred_element_type=F32)
        high = pick >> shift
        total = jnp.zeros((16, cap), F32)
        for m in range(blocks):
            total = total + jnp.where(high == m, found[m * 16 : (m + 1) * 16], 0.0)
        total = total[:8] + total[8:]
        picked_ref[dest] = total + pltpu.roll(total, 4, 0)
    packs = []
    bits = rows.bit_length() - 1
    for face in range(FACES):
        picks = ghost_ref[face : face + 1, :]
        third = [picks[:, m * TILE : (m + 1) * TILE] for m in range(picks.shape[1] // TILE)]
        count = len(third) // 2
        lines = [(third[r] + (third[r + count] << bits)).astype(F32) for r in range(count)]
        near = near_ref[...].astype(F32)
        lines.append(jnp.concatenate([near[k : k + 1] for k in range(near.shape[0])], axis=1))
        packs.append(jnp.concatenate(lines, axis=0))
    upper = iota((8, cap), 0) < 4
    for dest in range(n_dom):
        left = jnp.where(upper, picked_ref[dest], picked_ref[(dest + 1) % n_dom])
        right = picked_ref[(dest - 1) % n_dom]
        if cap < TILE:
            gap = jnp.zeros((8, TILE - cap), F32)
            block = jnp.concatenate([left, gap, right, gap], axis=1)
        else:
            block = jnp.concatenate([left, right], axis=1)
        for slab in range(n_slab):
            out_ref[dest * n_slab + slab] = block
    me_dom, me_slab = lax.axis_index("dom"), lax.axis_index("slab")
    targets = (
        lax.rem(me_dom + 1, n_dom) * n_slab + me_slab,
        lax.rem(me_dom + n_dom - 1, n_dom) * n_slab + me_slab,
        me_dom * n_slab + lax.rem(me_slab + 1, n_slab),
        me_dom * n_slab + lax.rem(me_slab + n_slab - 1, n_slab),
    )
    for face, target in enumerate(targets):
        start = 0 if face == 3 else 4
        out_ref[target, start : start + 4, TILE:] = packs[face]


def weight_spots(radial_shape, update_shape):
    first = 16 * radial_shape[0] + 16
    spots = [first + m * update_shape[1] for m in range(update_shape[0])]
    return spots, first + update_shape[0] * update_shape[1]


def send_states(n_dom, n_slab, positions, species, send_pick, ghost_pick, near_tiles, embedding, radial, update, force):
    cap = send_pick.shape[1]
    inputs = (positions.T, species.reshape(1, -1), send_pick, ghost_pick, near_tiles.T, embedding, radial, update, force)
    count = weight_spots(radial.shape, update.shape)[1] + force.shape[0] + 16 * (ghost_pick.shape[1] // LANES)
    return pl.pallas_call(
        functools.partial(send_kernel, n_dom, n_slab),
        out_shape=[
            jax.ShapeDtypeStruct((n_dom * n_slab, 8, LANES), F32),
            jax.ShapeDtypeStruct((count, force.shape[1]), BF16),
        ],
        in_specs=[pl.BlockSpec(memory_space=pl.ANY)] * len(inputs),
        out_specs=[VMEM] * 2,
        scratch_shapes=[pltpu.VMEM(one.shape, one.dtype) for one in inputs[:7]]
        + [pltpu.VMEM((n_dom, 8, cap), F32), pltpu.SemaphoreType.DMA((8 + update.shape[0],))],
        compiler_params=params(63),
        name="send_states",
    )(*inputs)


def store_tile(doubled, tile, pool_ref):
    live = doubled[3:4] > 0.5
    for word in range(3):
        pool_ref[tile, word] = jnp.broadcast_to(jnp.where(live, doubled[word : word + 1], AWAY), (8, LANES))


def find_rows(tables, lane, group, groups):
    onehot = (iota((LANES, LANES), 0) == lane).astype(F32).astype(BF16)
    found = sum(jnp.dot(table, onehot, preferred_element_type=F32) for table in (tables[0], tables[2], tables[1]))
    total = jnp.zeros((8, LANES), F32)
    for one in range(groups):
        total = total + jnp.where(group == one, found[one * 8 : (one + 1) * 8], 0.0)
    return total


def build_pool(n_dom, n_slab, cap, ghost_rows, recv_ref, emb_ref, pool_ref, column_ref, around_ref, taken_ref, h_ref, kind_ref):
    me_dom, me_slab = lax.axis_index("dom"), lax.axis_index("slab")
    atom_rows = column_ref.shape[0]
    local_tiles = atom_rows // TILE
    before, after = lax.rem(me_slab + n_slab - 1, n_slab), lax.rem(me_slab + 1, n_slab)
    per = TILE // cap
    half = iota((1, LANES), 1) < TILE
    for pair in range(local_tiles // 2):
        kinds = []
        for tile in (2 * pair, 2 * pair + 1):
            parts = [recv_ref[(tile * per + p) * n_slab + me_slab, 0:8, :][:, :cap] for p in range(per)]
            doubled = jnp.concatenate(parts * 2, axis=1)
            store_tile(doubled, tile, pool_ref)
            column = doubled.T[:TILE]
            live = column[:, 3:4] > 0.5
            spot = iota((TILE, 8), 1)
            column_ref[tile * TILE : (tile + 1) * TILE, :] = jnp.where((spot >= 3) | live, column, -AWAY)
            kinds.append(doubled[3:4])
        kind_ref[0:1, pair * LANES : (pair + 1) * LANES] = jnp.where(half, kinds[0], kinds[1])

    def rows_of(slab):
        return jnp.concatenate([recv_ref[e * n_slab + slab, 0:8, :] for e in range(n_dom)], axis=0)

    own = pieces(rows_of(me_slab))
    below = pieces(rows_of(before))
    above = below if n_slab == 2 else pieces(rows_of(after))
    own_at = me_dom * n_slab
    width = ghost_rows // LANES
    sources = (
        (lax.rem(me_dom + n_dom - 1, n_dom) * n_slab + me_slab, 4, own, TILE, 0),
        (lax.rem(me_dom + 1, n_dom) * n_slab + me_slab, 4, own, 0, 4),
        (own_at + before, 4, below, 0, 0),
        (own_at + after, 0, above, 0, 0),
    )
    shift = cap.bit_length() - 1
    bits = atom_rows.bit_length() - 1
    for face, (origin, place, tables, lane_start, row_start) in enumerate(sources):
        packed = recv_ref[origin, place : place + 4, :][:, TILE:].astype(jnp.int32)
        around_ref[face : face + 1, :] = jnp.concatenate([packed[width : width + 1]] * 2, axis=1)
        lines = [packed[r : r + 1] for r in range(width)]
        thirds = [line & (atom_rows - 1) for line in lines] + [line >> bits for line in lines]
        for m in range(width):
            pick = jnp.concatenate(thirds[2 * m : 2 * m + 2], axis=1)
            taken_ref[face : face + 1, m * LANES : (m + 1) * LANES] = pick
            total = find_rows(tables, (pick & (cap - 1)) + lane_start, pick >> shift, n_dom)
            if row_start:
                total = pltpu.roll(total, 4, 0)
            swapped = pltpu.roll(total, TILE, 1)
            tile = local_tiles + (face * ghost_rows) // TILE + 2 * m
            store_tile(jnp.where(half, total, swapped), tile, pool_ref)
            store_tile(jnp.where(half, swapped, total), tile + 1, pool_ref)
            spot = tile * TILE
            kind_ref[0:1, spot : spot + LANES] = total[3:4]
    table = emb_ref[...]
    step = 512
    for start in range(0, h_ref.shape[0], step):
        kinds = kind_ref[0:1, start : start + step].astype(jnp.int32)
        onehot = (iota((16, step), 0) == kinds - 1).astype(F32).astype(BF16)
        h_ref[start : start + step, :] = lax.dot_general(onehot, table, (((0,), (0,)), ((), ())), preferred_element_type=F32).astype(BF16)


class Near:
    def __init__(self, table_ref, shape):
        self.table_ref, self.shape = table_ref, shape

    def __getitem__(self, at):
        return self.table_ref[FACES + at[0], at[1]]


def half_rows(near_ref, pool_ref, tile, side):
    first, second = near_ref[2 * side, tile], near_ref[2 * side + 1, tile]
    lane = iota((8, LANES), 1)
    left = lane < TILE
    xyz = [jnp.where(left, pool_ref[first, w], pool_ref[second, w]) for w in range(3)]
    rows = jnp.where(left, first * TILE, second * TILE) + (lane & (TILE - 1))
    return first, second, xyz, rows


def tall(value, count):
    return jnp.concatenate([value] * count, axis=0) if count > 1 else value


def geometry(column_ref, start, count, xyz, rows):
    column = column_ref[pl.ds(start, count), :]
    offset = [tall(xyz[w], count // 8) - column[:, w : w + 1] for w in range(3)]
    square = offset[0] * offset[0] + offset[1] * offset[1] + offset[2] * offset[2] + SOFTENING
    inverse = lax.rsqrt(square)
    ratio = jnp.minimum(square * inverse * (1.0 / CUTOFF), 1.0)
    same = tall(rows, count // 8) == iota((count, LANES), 0) + start
    ratio = jnp.where(same, 1.0, ratio)
    fade = 1.0 - ratio * ratio
    return offset, inverse, ratio, fade * fade


def edges_of(column_ref, start, count, xyz, rows):
    offset, inverse, ratio, envelope = geometry(column_ref, start, count, xyz, rows)
    x, y, z = (part * inverse for part in offset)
    harmonic = [x, y, z, x * y, y * z, z * x, (x - y) * (x + y), 3.0 * (z * z) - 1.0]
    shifted = ratio - 0.5
    square = shifted * shifted
    sine = series(COS_TERMS, square)
    cosine = -shifted * series(SIN_TERMS, square)
    twice = cosine + cosine
    radial = [sine * (envelope * inverse)]
    radial.append(twice * radial[0])
    while len(radial) < 8:
        radial.append(twice * radial[-1] - radial[-2])
    return harmonic, radial


def store_part(near_ref, pool_ref, column_ref, tile, side, part, harmonic_ref, radial_ref):
    chunk = 16
    _, _, xyz, rows = half_rows(near_ref, pool_ref, tile, side)
    spot = slice(part * chunk, (part + 1) * chunk)
    harmonic, radial = edges_of(column_ref, pl.multiple_of(tile * TILE + part * chunk, chunk), chunk, xyz, rows)
    for k, one in enumerate(harmonic):
        harmonic_ref[k, spot, :] = one.astype(BF16)
    for n, one in enumerate(radial):
        radial_ref[n, spot, :] = one.astype(BF16)
    return jnp.maximum(radial[-1][:8], radial[-1][8:])[:1]


def side_sum(near_ref, h_ref, weight_ref, tile, side, harmonic_ref, radial_ref, gates):
    nears = [near_ref[2 * side + place, tile] for place in range(2)]
    features = jnp.concatenate([h_ref[pl.ds(pl.multiple_of(other * TILE, TILE), TILE), :] for other in nears], axis=0)
    nbasis = weight_ref.shape[0]
    radial = [radial_ref[n] for n in range(nbasis)]
    rows = [jnp.concatenate(radial, axis=1)]
    for k in range(NHARM - 1):
        harmonic = harmonic_ref[k]
        rows.append(jnp.concatenate([harmonic * one for one in radial], axis=1))
    weight = weight_ref[...].astype(F32)
    steps = []
    for m in range(nbasis // 2):
        part = weight[2 * m : 2 * m + 2]
        for one in gates[m]:
            part = jnp.where(one < 1e30, part, 0.0)
        part = part.astype(BF16)
        steps += [features * part[n : n + 1] for n in range(2)]
    return jnp.dot(jnp.concatenate(rows, axis=0), jnp.concatenate(steps, axis=0), preferred_element_type=F32)


def store_query(agg_ref, tile, query_ref):
    channels = agg_ref.shape[1]
    part = [agg_ref[k * TILE : (k + 1) * TILE, :] * (1.0 / TILE**0.5) for k in range(NHARM)]
    square = [one * one for one in part]
    query = [part[0], square[0], square[1] + square[2] + square[3], square[4] + square[5] + square[6] + square[7] + square[8]]
    start = pl.multiple_of(tile * TILE, TILE)
    for spot, one in enumerate(query):
        query_ref[pl.ds(start, TILE), spot * channels : (spot + 1) * channels] = one.astype(BF16)
    return query[-1][:1]


def run_layer(turns, near_ref, pool_ref, column_ref, h_ref, weight_ref, update_ref, out_ref, query_ref, agg_ref, harm_now, harm_next, radial_now, radial_next):
    tiles = near_ref.shape[1]

    harmonics, radials = (harm_now, harm_next), (radial_now, radial_next)

    def make(tile, unit, slot):
        side, part = divmod(unit, 4)
        return store_part(near_ref, pool_ref, column_ref, tile, side, part, harmonics[slot].at[side], radials[slot].at[side])

    for unit in range(8):
        make(0, unit, 0)
    agg_ref[...] = jnp.zeros_like(agg_ref)

    def step(index, carry):
        for turn in range(turns):
            slot = turn % 2
            tile = turns * index + turn
            later = jnp.minimum(tile + 1, tiles - 1)
            query = store_query(agg_ref, jnp.maximum(tile - 1, 0), query_ref)
            units = [make(later, unit, 1 - slot) for unit in range(8)]
            gates = ((), (), (), ())
            sides = [side_sum(near_ref, h_ref, weight_ref, tile, side, harmonics[slot].at[side], radials[slot].at[side], gates) for side in range(2)]
            agg_ref[...] = sides[0] + sides[1]
        return carry

    lax.fori_loop(0, tiles // turns, step, 0)
    store_query(agg_ref, tiles - 1, query_ref)
    changes = jnp.dot(query_ref[...], update_ref[...], preferred_element_type=F32)
    block = 256
    for start in range(0, out_ref.shape[0], block):
        update = changes[start : start + block]
        live = (column_ref[start : start + block, 3:4] > 0.5).astype(F32)
        fresh = h_ref[start : start + block, :].astype(F32) + update * (1.0 / (1.0 + jnp.exp(-update)))
        out_ref[start : start + block, :] = (fresh * live).astype(BF16)


def spread(refs, size):
    return [(ref, start) for ref in refs for start in range(0, ref.shape[0], size)]


def is_even():
    return lax.rem(lax.axis_index("dom"), 2) == 0


def gather_rows(pick_ref, tasks, keep=None):
    ghost_rows = pick_ref.shape[1]
    picks = pick_ref[...].astype(F32)
    if keep is not None:
        picks = jnp.concatenate([jnp.where(keep, picks[0:1], picks[1:2]), jnp.where(keep, picks[1:2], picks[0:1]), picks[2:]], axis=0)
    if picks.shape[0] < 8:
        picks = jnp.concatenate([picks, jnp.zeros((8 - picks.shape[0], ghost_rows), F32)], axis=0)
    columns = [picks[:, m * LANES : (m + 1) * LANES].T.astype(jnp.int32) for m in range(ghost_rows // LANES)]
    sources = []
    for _, source, _, _ in tasks:
        if not any(source is one for one in sources):
            sources.append(source)
    for source in sources:
        here = [task for task in tasks if task[1] is source]
        onehot = [(column[:, task[0] : task[0] + 1] == iota((LANES, source.shape[0]), 1)).astype(F32).astype(BF16) for task in here for column in columns]
        found = jnp.dot(jnp.concatenate(onehot, axis=0), source[...], preferred_element_type=F32).astype(BF16)
        for spot, (_, _, target, start) in enumerate(here):
            target[pl.ds(start if isinstance(start, int) else pl.multiple_of(start, LANES), ghost_rows), :] = found[spot * ghost_rows : (spot + 1) * ghost_rows]


def views(weights_ref, spot):
    radial, nbasis, update, depth = spot
    return weights_ref.at[radial : radial + nbasis], weights_ref.at[update : update + depth]


def first_kernel(n_dom, n_slab, cap, n_out, spot, emb_spot, number_spot, tiles, recv_ref, weights_ref, numbers_ref, *rest):
    *rest, table_ref, sem = rest
    parts = weights_ref[number_spot:, :].astype(F32).astype(jnp.int32)
    blocks = parts.shape[0] // 16
    for m in range(blocks):
        top, low = parts[8 * m : 8 * m + 8], parts[8 * (m + blocks) : 8 * (m + blocks) + 8]
        numbers_ref[:, m * LANES : (m + 1) * LANES] = (top << 5) + low
    copy = pltpu.make_async_copy(numbers_ref, table_ref, sem)
    copy.start()
    near_ref = Near(table_ref, tiles)
    pick_ref = numbers_ref
    emb_ref = weights_ref.at[emb_spot : emb_spot + 16]
    pool_ref, column_ref, around_ref, taken_ref, kept_ref, out_ref = rest[:6]
    outs = rest[6 : 6 + n_out]
    *scratch, h_ref, kind_ref = rest[6 + n_out :]
    kept_ref[...] = weights_ref[:number_spot, :]
    build_pool(n_dom, n_slab, cap, pick_ref.shape[1], recv_ref, emb_ref, pool_ref, column_ref, around_ref, taken_ref, h_ref, kind_ref)
    copy.wait()
    run_layer(4, near_ref, pool_ref, column_ref, h_ref, *views(weights_ref, spot), out_ref, *scratch)
    gather_rows(pick_ref, [(face, out_ref, ref, start) for face, (ref, start) in enumerate(spread(outs, pick_ref.shape[1]))], is_even())


def second_kernel(n_in, spot, force_spot, tiles, table_ref, list_ref, pool_ref, column_ref, h_in_ref, *rest):
    near_ref = Near(table_ref, tiles)
    ghosts = rest[:n_in]
    weights_ref, out_ref, g_ref = rest[n_in : n_in + 3]
    *scratch, h_ref = rest[n_in + 3 :]
    atom_rows, ghost_rows = h_in_ref.shape[0], ghosts[0].shape[0]
    even = is_even().astype(jnp.int32)
    h_ref[0:atom_rows, :] = h_in_ref[...]
    for block, ref in zip((even, 1 - even), ghosts):
        h_ref[pl.ds(pl.multiple_of(atom_rows + block * ghost_rows, LANES), ghost_rows), :] = ref[...]
    start = atom_rows + 2 * ghost_rows
    for ref in ghosts[2:]:
        h_ref[start : start + ref.shape[0], :] = ref[...]
        start += ref.shape[0]
    run_layer(16, near_ref, pool_ref, column_ref, h_ref, *views(weights_ref, spot), out_ref, *scratch)
    g_ref[...] = jnp.dot(out_ref[...], weights_ref[force_spot:, :], preferred_element_type=F32).astype(BF16)


def layer_scratch(nbasis, near, channels, atom_rows, pool_rows):
    half = near * TILE // 2
    return [
        pltpu.VMEM((atom_rows, 4 * channels), BF16),
        pltpu.VMEM((NHARM * TILE, channels), F32),
        *[pltpu.VMEM((2, NHARM - 1, TILE, half), BF16)] * 2,
        *[pltpu.VMEM((2, nbasis, TILE, half), BF16)] * 2,
        pltpu.VMEM((pool_rows, channels), BF16),
    ]


def list_blocks(near_ref, around_ref, atom_tiles, face_tiles, early_ref, late_ref):
    near = near_ref.shape[0]
    pool_tiles = atom_tiles + FACES * face_tiles
    spare = (5 * atom_tiles) * 128 + pool_tiles + FACES * face_tiles
    first_slab = atom_tiles + 2 * face_tiles

    def own(tile, counts):
        early, late = counts
        for k in range(near):
            other = near_ref[k, tile]
            entry = tile * 128 + other
            with_dom = ((other >= atom_tiles) & (other < first_slab)).astype(jnp.int32)
            early_ref[early] = entry
            late_ref[late] = entry
            early, late = early + 1 - with_dom, late + with_dom
        return early, late

    counts = lax.fori_loop(0, atom_tiles, own, (jnp.int32(0), jnp.int32(0)))

    def of_others(ref, pairs):
        def others(tile, count):
            for domain, face in pairs:
                start = atom_tiles + face * face_tiles
                for k in range(near):
                    other = around_ref[domain, k * atom_tiles + tile] - start
                    ref[count] = (atom_tiles * (domain + 1) + tile) * 128 + pool_tiles + face * face_tiles + other
                    count = count + ((other >= 0) & (other < face_tiles)).astype(jnp.int32)
            return count

        return others

    early = lax.fori_loop(0, atom_tiles, of_others(early_ref, ((2, 3), (3, 2))), counts[0])
    late = lax.fori_loop(0, atom_tiles, of_others(late_ref, ((0, 1), (1, 0))), counts[1])
    for extra in range(7):
        early_ref[early + extra] = spare
        late_ref[late + extra] = spare
    return early, late


def block_pair(first, second, atom_tiles, pool_ref, column_ref, gi_ref, gj_ref):
    scale = 1.0 / gi_ref.shape[1] ** 0.5
    lane = iota((8, LANES), 1)
    left = lane < TILE
    half = iota((TILE, LANES), 1) < TILE
    i_tiles = [pl.multiple_of((one >> 7) * TILE, TILE) for one in (first, second)]
    j_tiles = [one & 127 for one in (first, second)]
    same = [jnp.where((one >> 7 == one & 127) & (one >> 7 < atom_tiles), 0, 4096) for one in (first, second)]
    rows = jnp.where(left, same[0], same[1]) + (lane & (TILE - 1))
    columns = [column_ref[pl.ds(one, TILE), :] for one in i_tiles]
    mine = jnp.concatenate([gi_ref[pl.ds(one, TILE), :] for one in i_tiles], axis=0)
    others = jnp.concatenate([gj_ref[pl.ds(pl.multiple_of(one * TILE, TILE), TILE), :] for one in j_tiles], axis=0)
    inner = lax.dot_general(mine, others, (((1,), (1,)), ((), ())), preferred_element_type=F32)
    inner = jnp.where(half, inner[:TILE], inner[TILE:])
    offset = []
    for w in range(3):
        away = tall(jnp.where(left, pool_ref[j_tiles[0], w], pool_ref[j_tiles[1], w]), TILE // 8)
        offset.append(away - jnp.where(half, columns[0][:, w : w + 1], columns[1][:, w : w + 1]))
    square = offset[0] * offset[0] + offset[1] * offset[1] + offset[2] * offset[2] + SOFTENING
    inverse = lax.rsqrt(square)
    ratio = jnp.minimum(square * inverse * (1.0 / CUTOFF), 1.0)
    ratio = jnp.where(tall(rows, TILE // 8) == iota((TILE, LANES), 0), 1.0, ratio)
    fade = 1.0 - ratio * ratio
    strength = fade * fade * inverse * (inner * scale)
    return [strength * one for one in offset]


def sum_blocks(list_ref, count, atom_tiles, pool_ref, column_ref, gi_ref, gj_ref, own_ref, total_ref):
    own_ref[...] = jnp.zeros_like(own_ref)
    total_ref[...] = jnp.zeros_like(total_ref)
    left = iota((8, LANES), 1) < TILE
    half = iota((TILE, LANES), 1) < TILE

    def step(index, carry):
        entries = [list_ref[8 * index + spot] for spot in range(8)]
        found = [block_pair(entries[2 * p], entries[2 * p + 1], atom_tiles, pool_ref, column_ref, gi_ref, gj_ref) for p in range(4)]
        for p in range(4):
            for spot in range(2):
                entry = entries[2 * p + spot]
                i_tile, j_tile = jnp.minimum(entry >> 7, atom_tiles), entry & 127
                for w in range(3):
                    pair = found[p][w]
                    against = sum(pair[8 * v : 8 * v + 8] for v in range(TILE // 8))
                    total_ref[j_tile, w] -= jnp.where(left, against, 0.0) if spot == 0 else jnp.where(left, 0.0, against)
                    own_ref[i_tile, w] += jnp.where(half, pair, 0.0) if spot == 0 else jnp.where(half, 0.0, pair)
        return carry

    lax.fori_loop(0, (count + 7) // 8, step, 0)


def gather_forces(pick_ref, faces, atom_tiles, face_tiles, own_ref, total_ref):
    atom_rows = atom_tiles * TILE
    pool_tiles = atom_tiles + FACES * face_tiles
    half = iota((1, LANES), 1) < TILE
    sums = []
    for w in range(3):
        folded = jnp.sum(total_ref[:, w], axis=1)
        sums.append(folded + pltpu.roll(folded, TILE, 1))

    def row(tile):
        lines = [jnp.where(half, sums[w][tile : tile + 1], sums[w][tile + 1 : tile + 2]) for w in range(3)]
        return jnp.concatenate(lines + [jnp.zeros((5, LANES), F32)], axis=0)

    blocks = atom_rows // LANES
    shift = LANES.bit_length() - 1
    total = jnp.concatenate([row(2 * m) for m in range(blocks)], axis=0)
    for face in faces:
        for m in range(face_tiles // 2):
            pick = pick_ref[face : face + 1, m * LANES : (m + 1) * LANES]
            back = row(pool_tiles + face * face_tiles + 2 * m)
            high = pick >> shift
            wide = jnp.concatenate([jnp.where(high == one, back, 0.0) for one in range(blocks)], axis=0)
            onehot = (iota((LANES, LANES), 0) == (pick & (LANES - 1))).astype(F32).astype(BF16)
            for part in pieces(wide)[:2]:
                total = total + lax.dot_general(part, onehot, (((1,), (1,)), ((), ())), preferred_element_type=F32)
    total = jnp.concatenate([total[m * 8 : (m + 1) * 8] for m in range(blocks)], axis=1)
    for w in range(3):
        ones = (iota((8, LANES), 0) == w).astype(F32).astype(BF16)
        mine = jnp.concatenate([own_ref[tile, w] for tile in range(atom_tiles)], axis=0)
        for part in pieces(mine)[:2]:
            total = total + lax.dot_general(ones, part, (((1,), (1,)), ((), ())), preferred_element_type=F32)
    return total


def neighbour_kernel(n_dom, n_slab, cap, tiles, table_ref, around_ref, recv_ref, numbers_ref, pool_in, column_in, early_ref, late_ref, pool_ref, column_ref):
    near_ref = Near(table_ref, tiles)
    pick_ref = numbers_ref
    atom_rows, ghost_rows = column_in.shape[0], pick_ref.shape[1]
    atom_tiles, face_tiles = atom_rows // TILE, ghost_rows // TILE
    pool_tiles = atom_tiles + FACES * face_tiles
    me_slab = lax.axis_index("slab")
    before, after = lax.rem(me_slab + n_slab - 1, n_slab), lax.rem(me_slab + 1, n_slab)
    early, late = list_blocks(near_ref, around_ref, atom_tiles, face_tiles, early_ref.at[0], late_ref.at[0])
    early_ref[1, 0] = early
    late_ref[1, 0] = late
    column_ref[0:atom_rows, :] = column_in[...]
    column_ref[5 * atom_rows :, :] = jnp.full((TILE, 8), -AWAY, F32)
    per = TILE // cap
    spot = iota((TILE, 8), 1)

    def put(domain, tile, column):
        live = column[:, 3:4] > 0.5
        start = atom_rows * (domain + 1) + tile * TILE
        column_ref[start : start + TILE, :] = jnp.where((spot >= 3) | live, column, -AWAY)

    def tile_of(slab, tile):
        parts = [recv_ref[(tile * per + p) * n_slab + slab] for p in range(per)]
        return jnp.concatenate([one[:, start : start + cap] for start in (0, TILE) for one in parts], axis=1)

    for tile in range(atom_tiles):
        block = tile_of(me_slab, tile)
        put(0, tile, block.T[TILE:])
        put(1, tile, pltpu.roll(block, 4, 0).T[:TILE])
        below = tile_of(before, tile).T[:TILE]
        put(2, tile, below)
        put(3, tile, below if n_slab == 2 else tile_of(after, tile).T[:TILE])
    pool_ref[0:pool_tiles] = pool_in[...]
    pool_ref[pool_tiles + FACES * face_tiles] = jnp.full((3, 8, LANES), AWAY, F32)
    own = pieces(jnp.concatenate([recv_ref[e * n_slab + me_slab] for e in range(n_dom)], axis=0))
    shift = cap.bit_length() - 1
    half = iota((1, LANES), 1) < TILE
    for face in range(FACES):
        for m in range(ghost_rows // LANES):
            pick = pick_ref[face : face + 1, m * LANES : (m + 1) * LANES]
            total = find_rows(own, pick & (cap - 1), pick >> shift, n_dom)
            swapped = pltpu.roll(total, TILE, 1)
            tile = pool_tiles + face * face_tiles + 2 * m
            store_tile(jnp.where(half, total, swapped), tile, pool_ref)
            store_tile(jnp.where(half, swapped, total), tile + 1, pool_ref)


def near_forces_kernel(n_slab, list_ref, numbers_ref, taken_ref, pool_ref, column_ref, g_ref, *rest):
    pick_ref = numbers_ref
    slabs = rest[: 1 if n_slab == 2 else 2]
    part_ref, out_g_ref, gi_ref, gj_ref, own_ref, total_ref = rest[len(slabs) :]
    atom_rows, channels = g_ref.shape
    ghost_rows = pick_ref.shape[1]
    atom_tiles, face_tiles = atom_rows // TILE, ghost_rows // TILE
    pool_tiles = atom_tiles + FACES * face_tiles
    gi_ref[0:atom_rows, :] = g_ref[...]
    gj_ref[0:atom_rows, :] = g_ref[...]
    spare = jnp.zeros((TILE, channels), BF16)
    gi_ref[5 * atom_rows :, :] = spare
    gj_ref[(pool_tiles + FACES * face_tiles) * TILE :, :] = spare
    gi_ref[3 * atom_rows : 4 * atom_rows, :] = slabs[0][...]
    gi_ref[4 * atom_rows : 5 * atom_rows, :] = slabs[-1][...]
    gather_rows(pick_ref, [(face, g_ref, gj_ref, pool_tiles * TILE + face * ghost_rows) for face in range(FACES)])
    gather_rows(taken_ref, [(face, ref, gj_ref, atom_rows + face * ghost_rows) for face, ref in ((2, slabs[0]), (3, slabs[-1]))])
    out_g_ref[...] = gj_ref[pool_tiles * TILE : pool_tiles * TILE + 2 * ghost_rows, :]
    sum_blocks(list_ref.at[0], list_ref[1, 0], atom_tiles, pool_ref, column_ref, gi_ref, gj_ref, own_ref, total_ref)
    part_ref[...] = gather_forces(pick_ref, (2, 3), atom_tiles, face_tiles, own_ref, total_ref)


def far_forces_kernel(list_ref, numbers_ref, taken_ref, pool_ref, column_ref, g_ref, out_g_ref, first_ref, second_ref, part_ref, out_ref, gi_ref, gj_ref, own_ref, total_ref):
    pick_ref = numbers_ref
    atom_rows, channels = g_ref.shape
    ghost_rows = pick_ref.shape[1]
    atom_tiles, face_tiles = atom_rows // TILE, ghost_rows // TILE
    pool_tiles = atom_tiles + FACES * face_tiles
    spare = jnp.zeros((TILE, channels), BF16)
    gi_ref[0:atom_rows, :] = g_ref[...]
    even = is_even().astype(jnp.int32)
    spots = (even, 1 - even)
    for spot, ref in zip(spots, (first_ref, second_ref)):
        gi_ref[pl.ds(pl.multiple_of((1 + spot) * atom_rows, LANES), atom_rows), :] = ref[...]
    gi_ref[5 * atom_rows :, :] = spare
    gj_ref[pool_tiles * TILE : pool_tiles * TILE + 2 * ghost_rows, :] = out_g_ref[...]
    gj_ref[(pool_tiles + FACES * face_tiles) * TILE :, :] = spare
    gather_rows(taken_ref, [(face, ref, gj_ref, atom_rows + spots[face] * ghost_rows) for face, ref in ((0, first_ref), (1, second_ref))], even == 0)
    sum_blocks(list_ref.at[0], list_ref[1, 0], atom_tiles, pool_ref, column_ref, gi_ref, gj_ref, own_ref, total_ref)
    total = gather_forces(pick_ref, (0, 1), atom_tiles, face_tiles, own_ref, total_ref) + part_ref[...]
    out_ref[...] = total[0:3]


def passed_along(array, axis, by):
    count = lax.axis_size(axis)
    return lax.ppermute(array, axis, [(i, (i + by) % count) for i in range(count)])


def swapped(first, second):
    count = lax.axis_size("dom")
    ends = lax.ppermute(second, "dom", [(i, (i - 1 if i % 2 == 0 else i + 1) % count) for i in range(count)])
    return lax.ppermute(first, "dom", [(i, i + 1 if i % 2 == 0 else i - 1) for i in range(count)]), ends


def body(n_dom, n_slab, positions, species, send_pick, ghost_pick, near_tiles, embedding, radial_weight, update_weight, force_weight):
    atom_rows = positions.shape[0]
    cap = send_pick.shape[1]
    ghost_rows = ghost_pick.shape[1]
    tiles, near = near_tiles.shape
    channels = embedding.shape[1]
    nbasis = radial_weight.shape[1]
    pool_rows = atom_rows + FACES * ghost_rows
    face_rows = [ghost_rows, ghost_rows] + ([2 * ghost_rows] if n_slab == 2 else [ghost_rows, ghost_rows])
    n_out = len(face_rows)
    face_out = [jax.ShapeDtypeStruct((rows, channels), BF16) for rows in face_rows]
    face_tiles = ghost_rows // TILE
    i_rows = 5 * atom_rows + TILE
    j_tiles = pool_rows // TILE + FACES * face_tiles + 1
    longest = (near * tiles) * 5 + 8
    scratch = layer_scratch(nbasis, near, channels, atom_rows, pool_rows)

    sent, weights = send_states(n_dom, n_slab, positions, species, send_pick, ghost_pick, near_tiles, embedding, radial_weight, update_weight, force_weight)
    update_spot, force_spot = weight_spots(radial_weight.shape, update_weight.shape)
    spots = [(16 * m, nbasis, at, update_weight.shape[1]) for m, at in enumerate(update_spot)]
    got = lax.all_to_all(sent, ("dom", "slab"), split_axis=0, concat_axis=0, tiled=True)

    numbers, pool, column, around, taken, kept, hidden, *faces = pl.pallas_call(
        functools.partial(first_kernel, n_dom, n_slab, cap, n_out, spots[0], 16 * len(spots), force_spot + channels, (near, tiles)),
        out_shape=[
            jax.ShapeDtypeStruct((8, ghost_rows), jnp.int32),
            jax.ShapeDtypeStruct((pool_rows // TILE, 3, 8, LANES), F32),
            jax.ShapeDtypeStruct((atom_rows, 8), F32),
            jax.ShapeDtypeStruct((8, LANES), jnp.int32),
            jax.ShapeDtypeStruct((8, ghost_rows), jnp.int32),
            jax.ShapeDtypeStruct((force_spot + channels, channels), BF16),
            jax.ShapeDtypeStruct((atom_rows, channels), BF16),
        ]
        + face_out,
        in_specs=[VMEM] * 2,
        out_specs=[VMEM] * (7 + n_out),
        scratch_shapes=scratch + [pltpu.VMEM((8, pool_rows), F32), pltpu.SMEM((8, ghost_rows), jnp.int32), pltpu.SemaphoreType.DMA],
        compiler_params=params(),
        name="first_layer",
    )(got, weights)

    early, late, wide_pool, wide_column = pl.pallas_call(
        functools.partial(neighbour_kernel, n_dom, n_slab, cap, (near, tiles)),
        out_shape=[
            jax.ShapeDtypeStruct((2, longest), jnp.int32),
            jax.ShapeDtypeStruct((2, longest), jnp.int32),
            jax.ShapeDtypeStruct((j_tiles, 3, 8, LANES), F32),
            jax.ShapeDtypeStruct((i_rows, 8), F32),
        ],
        in_specs=[SMEM] * 2 + [VMEM] * 4,
        out_specs=[SMEM] * 2 + [VMEM] * 2,
        compiler_params=params(),
        name="neighbours",
    )(numbers, around, got, numbers, pool, column)
    faces = [*swapped(*faces[:2]), *(passed_along(one, "slab", way) for one, way in zip(faces[2:], (1, -1)))]
    features, mine = pl.pallas_call(
        functools.partial(second_kernel, n_out, spots[1], force_spot, (near, tiles)),
        out_shape=[jax.ShapeDtypeStruct((atom_rows, channels), BF16)] * 2,
        in_specs=[SMEM] * 2 + [VMEM] * (4 + n_out),
        out_specs=[VMEM] * 2,
        scratch_shapes=scratch,
        compiler_params=params(),
        name="second_layer",
    )(numbers, early, pool, column, hidden, *faces, kept)

    slabs = [passed_along(mine, "slab", 1)]
    if n_slab != 2:
        slabs.append(passed_along(mine, "slab", -1))
    first, second = swapped(mine, mine)
    force_scratch = [
        pltpu.VMEM((i_rows, channels), BF16),
        pltpu.VMEM((j_tiles * TILE, channels), BF16),
        pltpu.VMEM((tiles + 1, 3, TILE, LANES), F32),
        pltpu.VMEM((j_tiles, 3, 8, LANES), F32),
    ]
    part, out_g = pl.pallas_call(
        functools.partial(near_forces_kernel, n_slab),
        out_shape=[jax.ShapeDtypeStruct((8, atom_rows), F32), jax.ShapeDtypeStruct((2 * ghost_rows, channels), BF16)],
        in_specs=[SMEM] + [VMEM] * (5 + len(slabs)),
        out_specs=[VMEM] * 2,
        scratch_shapes=force_scratch,
        cost_estimate=pl.CostEstimate(flops=4_000_000_000, bytes_accessed=4_000_000, transcendentals=0),
        compiler_params=params(),
        name="near_forces",
    )(early, numbers, taken, wide_pool, wide_column, mine, *slabs)
    forces = pl.pallas_call(
        far_forces_kernel,
        out_shape=jax.ShapeDtypeStruct((3, atom_rows), F32),
        in_specs=[SMEM] + [VMEM] * 9,
        out_specs=VMEM,
        scratch_shapes=force_scratch,
        compiler_params=params(),
        name="far_forces",
    )(late, numbers, taken, wide_pool, wide_column, mine, out_g, first, second, part)
    return features, forces


def solution(mesh):
    both = ("dom", "slab")
    return jax.shard_map(
        functools.partial(body, mesh.shape["dom"], mesh.shape["slab"]),
        mesh=mesh,
        in_specs=(P(both, None), P(both), P(both, None), P(both, None), P(both, None), P(), P(), P(), P()),
        out_specs=(P(both, None), P(None, both)),
        check_vma=False,
    )
```

```python
import functools

import jax
import jax.numpy as jnp
from jax import lax
from jax.experimental import pallas as pl
from jax.experimental.pallas import tpu as pltpu
from jax.sharding import PartitionSpec as P

LAYERS = 2
TILE = 64
LANES = 128
FACES = 4
NHARM = 9
AWAY = 1000.0
CUTOFF = 6.0
SOFTENING = 0.25
F32 = jnp.float32
BF16 = jnp.bfloat16

COS_TERMS = (1.0, -4.934802200544679, 4.058712126416768, -1.3352627688545893, 0.2353306303588935, -0.02580689139001406)
SIN_TERMS = (3.141592653589793, -5.16771278004997, 2.550164039877345, -0.5992645293207921, 0.08214588661112823, -0.00737043094571435)

VMEM = pl.BlockSpec(memory_space=pltpu.VMEM)
SMEM = pl.BlockSpec(memory_space=pltpu.SMEM)


def params(mib=40):
    return pltpu.CompilerParams(vmem_limit_bytes=int(mib * 1024 * 1024))


def pieces(value):
    top = value.astype(BF16)
    rest = value - top.astype(F32)
    middle = rest.astype(BF16)
    low = (rest - middle.astype(F32)).astype(BF16)
    return top, middle, low


def series(terms, square):
    total = jnp.full_like(square, terms[-1])
    for term in reversed(terms[:-1]):
        total = total * square + term
    return total


def iota(shape, dim):
    return lax.broadcasted_iota(jnp.int32, shape, dim)


def send_kernel(n_dom, n_slab, pos_in, kind_in, pick_in, ghost_in, near_in, embedding_in, radial_in, update_in, force_in, out_ref, weights_ref,
                pos_ref, kind_ref, pick_ref, ghost_ref, near_ref, embedding_ref, radial_ref, picked_ref, sems):
    update_spot, force_spot = weight_spots(radial_in.shape, update_in.shape)
    pairs = [(pos_in, pos_ref), (kind_in, kind_ref), (pick_in, pick_ref), (ghost_in, ghost_ref), (near_in, near_ref), (embedding_in, embedding_ref), (radial_in, radial_ref)]
    pairs += [(update_in.at[m], weights_ref.at[spot : spot + update_in.shape[1]]) for m, spot in enumerate(update_spot)]
    pairs += [(force_in, weights_ref.at[force_spot : force_spot + force_in.shape[0]])]
    copies = []
    for spot, (source, target) in enumerate(pairs):
        copies.append(pltpu.make_async_copy(source, target, sems.at[spot]))
        copies[-1].start()
    for copy in copies[:5]:
        copy.wait()
    rows = pos_ref.shape[1]
    cap = pick_ref.shape[1]
    blocks = rows // LANES
    state = jnp.concatenate([pos_ref[...], kind_ref[...].astype(F32) + 1.0], axis=0)
    top, middle, low = (part.astype(F32) for part in pieces(state))
    table = jnp.concatenate([top, middle, low, jnp.zeros_like(low)], axis=0).astype(BF16)
    table = jnp.concatenate([table[:, m * LANES : (m + 1) * LANES] for m in range(blocks)], axis=0)
    shift = LANES.bit_length() - 1
    for dest in range(n_dom):
        pick = pick_ref[dest : dest + 1, :]
        onehot = (iota((LANES, cap), 0) == (pick & (LANES - 1))).astype(F32).astype(BF16)
        found = jnp.dot(table, onehot, preferred_element_type=F32)
        high = pick >> shift
        total = jnp.zeros((16, cap), F32)
        for m in range(blocks):
            total = total + jnp.where(high == m, found[m * 16 : (m + 1) * 16], 0.0)
        total = total[:8] + total[8:]
        picked_ref[dest] = total + pltpu.roll(total, 4, 0)
    packs = []
    bits = rows.bit_length() - 1
    for face in range(FACES):
        picks = ghost_ref[face : face + 1, :]
        third = [picks[:, m * TILE : (m + 1) * TILE] for m in range(picks.shape[1] // TILE)]
        count = len(third) // 2
        lines = [(third[r] + (third[r + count] << bits)).astype(F32) for r in range(count)]
        near = near_ref[...].astype(F32)
        lines.append(jnp.concatenate([near[k : k + 1] for k in range(near.shape[0])], axis=1))
        packs.append(jnp.concatenate(lines, axis=0))
    upper = iota((8, cap), 0) < 4
    for dest in range(n_dom):
        left = jnp.where(upper, picked_ref[dest], picked_ref[(dest + 1) % n_dom])
        right = picked_ref[(dest - 1) % n_dom]
        if cap < TILE:
            gap = jnp.zeros((8, TILE - cap), F32)
            block = jnp.concatenate([left, gap, right, gap], axis=1)
        else:
            block = jnp.concatenate([left, right], axis=1)
        for slab in range(n_slab):
            out_ref[dest * n_slab + slab] = block
    me_dom, me_slab = lax.axis_index("dom"), lax.axis_index("slab")
    targets = (
        lax.rem(me_dom + 1, n_dom) * n_slab + me_slab,
        lax.rem(me_dom + n_dom - 1, n_dom) * n_slab + me_slab,
        me_dom * n_slab + lax.rem(me_slab + 1, n_slab),
        me_dom * n_slab + lax.rem(me_slab + n_slab - 1, n_slab),
    )
    for face, target in enumerate(targets):
        start = 0 if face == 3 else 4
        out_ref[target, start : start + 4, TILE:] = packs[face]
    for copy in copies[5:]:
        copy.wait()
    beside = jnp.zeros((near_ref.shape[0], ghost_ref.shape[1] - near_ref.shape[1]), jnp.int32)
    numbers = jnp.concatenate([ghost_ref[...], jnp.concatenate([near_ref[...], beside], axis=1)], axis=0)
    parts = [part[:, m * LANES : (m + 1) * LANES] for part in (numbers >> 5, numbers & 31) for m in range(numbers.shape[1] // LANES)]
    number_spot = force_spot + force_in.shape[0]
    weights_ref[number_spot:, :] = jnp.concatenate(parts, axis=0).astype(F32).astype(BF16)
    blank = jnp.zeros((16, embedding_ref.shape[1]), F32)
    for level in range(radial_ref.shape[0]):
        weights_ref[16 * level : 16 * level + 16, :] = jnp.concatenate([radial_ref[level].astype(F32), blank[radial_ref.shape[1] :]], axis=0).astype(BF16)
    spot = 16 * radial_ref.shape[0]
    weights_ref[spot : spot + 16, :] = jnp.concatenate([embedding_ref[...].astype(F32), blank[embedding_ref.shape[0] :]], axis=0).astype(BF16)


def weight_spots(radial_shape, update_shape):
    first = 16 * radial_shape[0] + 16
    spots = [first + m * update_shape[1] for m in range(update_shape[0])]
    return spots, first + update_shape[0] * update_shape[1]


def send_states(n_dom, n_slab, positions, species, send_pick, ghost_pick, near_tiles, embedding, radial, update, force):
    cap = send_pick.shape[1]
    inputs = (positions.T, species.reshape(1, -1), send_pick, ghost_pick, near_tiles.T, embedding, radial, update, force)
    count = weight_spots(radial.shape, update.shape)[1] + force.shape[0] + 16 * (ghost_pick.shape[1] // LANES)
    return pl.pallas_call(
        functools.partial(send_kernel, n_dom, n_slab),
        out_shape=[
            jax.ShapeDtypeStruct((n_dom * n_slab, 8, LANES), F32),
            jax.ShapeDtypeStruct((count, force.shape[1]), BF16),
        ],
        in_specs=[pl.BlockSpec(memory_space=pl.ANY)] * len(inputs),
        out_specs=[VMEM] * 2,
        scratch_shapes=[pltpu.VMEM(one.shape, one.dtype) for one in inputs[:7]]
        + [pltpu.VMEM((n_dom, 8, cap), F32), pltpu.SemaphoreType.DMA((8 + update.shape[0],))],
        compiler_params=params(63),
        name="send_states",
    )(*inputs)


def store_tile(doubled, tile, pool_ref):
    live = doubled[3:4] > 0.5
    for word in range(3):
        pool_ref[tile, word] = jnp.broadcast_to(jnp.where(live, doubled[word : word + 1], AWAY), (8, LANES))


def find_rows(tables, lane, group, groups):
    onehot = (iota((LANES, LANES), 0) == lane).astype(F32).astype(BF16)
    found = sum(jnp.dot(table, onehot, preferred_element_type=F32) for table in (tables[0], tables[2], tables[1]))
    total = jnp.zeros((8, LANES), F32)
    for one in range(groups):
        total = total + jnp.where(group == one, found[one * 8 : (one + 1) * 8], 0.0)
    return total


def build_pool(n_dom, n_slab, cap, ghost_rows, recv_ref, emb_ref, pool_ref, column_ref, around_ref, taken_ref, h_ref, kind_ref):
    me_dom, me_slab = lax.axis_index("dom"), lax.axis_index("slab")
    atom_rows = column_ref.shape[0]
    local_tiles = atom_rows // TILE
    before, after = lax.rem(me_slab + n_slab - 1, n_slab), lax.rem(me_slab + 1, n_slab)
    per = TILE // cap
    half = iota((1, LANES), 1) < TILE
    for pair in range(local_tiles // 2):
        kinds = []
        for tile in (2 * pair, 2 * pair + 1):
            parts = [recv_ref[(tile * per + p) * n_slab + me_slab, 0:8, :][:, :cap] for p in range(per)]
            doubled = jnp.concatenate(parts * 2, axis=1)
            store_tile(doubled, tile, pool_ref)
            column = doubled.T[:TILE]
            live = column[:, 3:4] > 0.5
            spot = iota((TILE, 8), 1)
            column_ref[tile * TILE : (tile + 1) * TILE, :] = jnp.where((spot >= 3) | live, column, -AWAY)
            kinds.append(doubled[3:4])
        kind_ref[0:1, pair * LANES : (pair + 1) * LANES] = jnp.where(half, kinds[0], kinds[1])

    def rows_of(slab):
        return jnp.concatenate([recv_ref[e * n_slab + slab, 0:8, :] for e in range(n_dom)], axis=0)

    own = pieces(rows_of(me_slab))
    below = pieces(rows_of(before))
    above = below if n_slab == 2 else pieces(rows_of(after))
    own_at = me_dom * n_slab
    width = ghost_rows // LANES
    sources = (
        (lax.rem(me_dom + n_dom - 1, n_dom) * n_slab + me_slab, 4, own, TILE, 0),
        (lax.rem(me_dom + 1, n_dom) * n_slab + me_slab, 4, own, 0, 4),
        (own_at + before, 4, below, 0, 0),
        (own_at + after, 0, above, 0, 0),
    )
    shift = cap.bit_length() - 1
    bits = atom_rows.bit_length() - 1
    for face, (origin, place, tables, lane_start, row_start) in enumerate(sources):
        packed = recv_ref[origin, place : place + 4, :][:, TILE:].astype(jnp.int32)
        around_ref[face : face + 1, :] = jnp.concatenate([packed[width : width + 1]] * 2, axis=1)
        lines = [packed[r : r + 1] for r in range(width)]
        thirds = [line & (atom_rows - 1) for line in lines] + [line >> bits for line in lines]
        for m in range(width):
            pick = jnp.concatenate(thirds[2 * m : 2 * m + 2], axis=1)
            taken_ref[face : face + 1, m * LANES : (m + 1) * LANES] = pick
            total = find_rows(tables, (pick & (cap - 1)) + lane_start, pick >> shift, n_dom)
            if row_start:
                total = pltpu.roll(total, 4, 0)
            swapped = pltpu.roll(total, TILE, 1)
            tile = local_tiles + (face * ghost_rows) // TILE + 2 * m
            store_tile(jnp.where(half, total, swapped), tile, pool_ref)
            store_tile(jnp.where(half, swapped, total), tile + 1, pool_ref)
            spot = tile * TILE
            kind_ref[0:1, spot : spot + LANES] = total[3:4]
    table = emb_ref[...]
    step = 512
    for start in range(0, h_ref.shape[0], step):
        kinds = kind_ref[0:1, start : start + step].astype(jnp.int32)
        onehot = (iota((16, step), 0) == kinds - 1).astype(F32).astype(BF16)
        h_ref[start : start + step, :] = lax.dot_general(onehot, table, (((0,), (0,)), ((), ())), preferred_element_type=F32).astype(BF16)


class Near:
    def __init__(self, table_ref, shape):
        self.table_ref, self.shape = table_ref, shape

    def __getitem__(self, at):
        return self.table_ref[FACES + at[0], at[1]]


def half_rows(near_ref, pool_ref, tile, side):
    first, second = near_ref[2 * side, tile], near_ref[2 * side + 1, tile]
    lane = iota((8, LANES), 1)
    left = lane < TILE
    xyz = [jnp.where(left, pool_ref[first, w], pool_ref[second, w]) for w in range(3)]
    rows = jnp.where(left, first * TILE, second * TILE) + (lane & (TILE - 1))
    return first, second, xyz, rows


def tall(value, count):
    return jnp.concatenate([value] * count, axis=0) if count > 1 else value


def geometry(column_ref, start, count, xyz, rows):
    column = column_ref[pl.ds(start, count), :]
    offset = [tall(xyz[w], count // 8) - column[:, w : w + 1] for w in range(3)]
    square = offset[0] * offset[0] + offset[1] * offset[1] + offset[2] * offset[2] + SOFTENING
    inverse = lax.rsqrt(square)
    ratio = jnp.minimum(square * inverse * (1.0 / CUTOFF), 1.0)
    same = tall(rows, count // 8) == iota((count, LANES), 0) + start
    ratio = jnp.where(same, 1.0, ratio)
    fade = 1.0 - ratio * ratio
    return offset, inverse, ratio, fade * fade


def edges_of(column_ref, start, count, xyz, rows):
    offset, inverse, ratio, envelope = geometry(column_ref, start, count, xyz, rows)
    x, y, z = (part * inverse for part in offset)
    harmonic = [x, y, z, x * y, y * z, z * x, (x - y) * (x + y), 3.0 * (z * z) - 1.0]
    shifted = ratio - 0.5
    square = shifted * shifted
    sine = series(COS_TERMS, square)
    cosine = -shifted * series(SIN_TERMS, square)
    twice = cosine + cosine
    radial = [sine * (envelope * inverse)]
    radial.append(twice * radial[0])
    while len(radial) < 8:
        radial.append(twice * radial[-1] - radial[-2])
    return harmonic, radial


def store_part(near_ref, pool_ref, column_ref, tile, side, part, harmonic_ref, radial_ref):
    chunk = 16
    _, _, xyz, rows = half_rows(near_ref, pool_ref, tile, side)
    spot = slice(part * chunk, (part + 1) * chunk)
    harmonic, radial = edges_of(column_ref, pl.multiple_of(tile * TILE + part * chunk, chunk), chunk, xyz, rows)
    for k, one in enumerate(harmonic):
        harmonic_ref[k, spot, :] = one.astype(BF16)
    for n, one in enumerate(radial):
        radial_ref[n, spot, :] = one.astype(BF16)
    return jnp.maximum(radial[-1][:8], radial[-1][8:])[:1]


def side_sum(near_ref, h_ref, weight_ref, tile, side, harmonic_ref, radial_ref, gates):
    nears = [near_ref[2 * side + place, tile] for place in range(2)]
    features = jnp.concatenate([h_ref[pl.ds(pl.multiple_of(other * TILE, TILE), TILE), :] for other in nears], axis=0)
    nbasis = weight_ref.shape[0]
    radial = [radial_ref[n] for n in range(nbasis)]
    rows = [jnp.concatenate(radial, axis=1)]
    for k in range(NHARM - 1):
        harmonic = harmonic_ref[k]
        rows.append(jnp.concatenate([harmonic * one for one in radial], axis=1))
    weight = weight_ref[...].astype(F32)
    steps = []
    for m in range(nbasis // 2):
        part = weight[2 * m : 2 * m + 2]
        for one in gates[m]:
            part = jnp.where(one < 1e30, part, 0.0)
        part = part.astype(BF16)
        steps += [features * part[n : n + 1] for n in range(2)]
    return jnp.dot(jnp.concatenate(rows, axis=0), jnp.concatenate(steps, axis=0), preferred_element_type=F32)


def store_query(agg_ref, tile, query_ref):
    channels = agg_ref.shape[1]
    part = [agg_ref[k * TILE : (k + 1) * TILE, :] * (1.0 / TILE**0.5) for k in range(NHARM)]
    square = [one * one for one in part]
    query = [part[0], square[0], square[1] + square[2] + square[3], square[4] + square[5] + square[6] + square[7] + square[8]]
    start = pl.multiple_of(tile * TILE, TILE)
    for spot, one in enumerate(query):
        query_ref[pl.ds(start, TILE), spot * channels : (spot + 1) * channels] = one.astype(BF16)
    return query[-1][:1]


def run_layer(turns, near_ref, pool_ref, column_ref, h_ref, weight_ref, update_ref, out_ref, query_ref, agg_ref, harm_now, harm_next, radial_now, radial_next):
    tiles = near_ref.shape[1]

    harmonics, radials = (harm_now, harm_next), (radial_now, radial_next)

    def make(tile, unit, slot):
        side, part = divmod(unit, 4)
        return store_part(near_ref, pool_ref, column_ref, tile, side, part, harmonics[slot].at[side], radials[slot].at[side])

    for unit in range(8):
        make(0, unit, 0)
    agg_ref[...] = jnp.zeros_like(agg_ref)

    def step(index, carry):
        for turn in range(turns):
            slot = turn % 2
            tile = turns * index + turn
            later = jnp.minimum(tile + 1, tiles - 1)
            query = store_query(agg_ref, jnp.maximum(tile - 1, 0), query_ref)
            units = [make(later, unit, 1 - slot) for unit in range(8)]
            gates = ((), (), (), ())
            sides = [side_sum(near_ref, h_ref, weight_ref, tile, side, harmonics[slot].at[side], radials[slot].at[side], gates) for side in range(2)]
            agg_ref[...] = sides[0] + sides[1]
        return carry

    lax.fori_loop(0, tiles // turns, step, 0)
    store_query(agg_ref, tiles - 1, query_ref)
    changes = jnp.dot(query_ref[...], update_ref[...], preferred_element_type=F32)
    block = 256
    for start in range(0, out_ref.shape[0], block):
        update = changes[start : start + block]
        live = (column_ref[start : start + block, 3:4] > 0.5).astype(F32)
        fresh = h_ref[start : start + block, :].astype(F32) + update * (1.0 / (1.0 + jnp.exp(-update)))
        out_ref[start : start + block, :] = (fresh * live).astype(BF16)


def spread(refs, size):
    return [(ref, start) for ref in refs for start in range(0, ref.shape[0], size)]


def is_even():
    return lax.rem(lax.axis_index("dom"), 2) == 0


def gather_rows(pick_ref, tasks, keep=None):
    ghost_rows = pick_ref.shape[1]
    picks = pick_ref[...].astype(F32)
    if keep is not None:
        picks = jnp.concatenate([jnp.where(keep, picks[0:1], picks[1:2]), jnp.where(keep, picks[1:2], picks[0:1]), picks[2:]], axis=0)
    if picks.shape[0] < 8:
        picks = jnp.concatenate([picks, jnp.zeros((8 - picks.shape[0], ghost_rows), F32)], axis=0)
    columns = [picks[:, m * LANES : (m + 1) * LANES].T.astype(jnp.int32) for m in range(ghost_rows // LANES)]
    sources = []
    for _, source, _, _ in tasks:
        if not any(source is one for one in sources):
            sources.append(source)
    for source in sources:
        here = [task for task in tasks if task[1] is source]
        onehot = [(column[:, task[0] : task[0] + 1] == iota((LANES, source.shape[0]), 1)).astype(F32).astype(BF16) for task in here for column in columns]
        found = jnp.dot(jnp.concatenate(onehot, axis=0), source[...], preferred_element_type=F32).astype(BF16)
        for spot, (_, _, target, start) in enumerate(here):
            target[pl.ds(start if isinstance(start, int) else pl.multiple_of(start, LANES), ghost_rows), :] = found[spot * ghost_rows : (spot + 1) * ghost_rows]


def views(weights_ref, spot):
    radial, nbasis, update, depth = spot
    return weights_ref.at[radial : radial + nbasis], weights_ref.at[update : update + depth]


def first_kernel(n_dom, n_slab, cap, n_out, spot, emb_spot, number_spot, tiles, recv_ref, weights_ref, numbers_ref, *rest):
    *rest, table_ref, sem = rest
    parts = weights_ref[number_spot:, :].astype(F32).astype(jnp.int32)
    blocks = parts.shape[0] // 16
    for m in range(blocks):
        top, low = parts[8 * m : 8 * m + 8], parts[8 * (m + blocks) : 8 * (m + blocks) + 8]
        numbers_ref[:, m * LANES : (m + 1) * LANES] = (top << 5) + low
    copy = pltpu.make_async_copy(numbers_ref, table_ref, sem)
    copy.start()
    near_ref = Near(table_ref, tiles)
    pick_ref = numbers_ref
    emb_ref = weights_ref.at[emb_spot : emb_spot + 16]
    pool_ref, column_ref, around_ref, taken_ref, kept_ref, out_ref = rest[:6]
    outs = rest[6 : 6 + n_out]
    *scratch, h_ref, kind_ref = rest[6 + n_out :]
    kept_ref[...] = weights_ref[:number_spot, :]
    build_pool(n_dom, n_slab, cap, pick_ref.shape[1], recv_ref, emb_ref, pool_ref, column_ref, around_ref, taken_ref, h_ref, kind_ref)
    copy.wait()
    run_layer(4, near_ref, pool_ref, column_ref, h_ref, *views(weights_ref, spot), out_ref, *scratch)
    gather_rows(pick_ref, [(face, out_ref, ref, start) for face, (ref, start) in enumerate(spread(outs, pick_ref.shape[1]))], is_even())


def second_kernel(n_in, spot, force_spot, tiles, table_ref, list_ref, pool_ref, column_ref, h_in_ref, *rest):
    near_ref = Near(table_ref, tiles)
    ghosts = rest[:n_in]
    weights_ref, out_ref, g_ref = rest[n_in : n_in + 3]
    *scratch, h_ref = rest[n_in + 3 :]
    atom_rows, ghost_rows = h_in_ref.shape[0], ghosts[0].shape[0]
    even = is_even().astype(jnp.int32)
    h_ref[0:atom_rows, :] = h_in_ref[...]
    for block, ref in zip((1 - even, even), ghosts):
        h_ref[pl.ds(pl.multiple_of(atom_rows + block * ghost_rows, LANES), ghost_rows), :] = ref[...]
    start = atom_rows + 2 * ghost_rows
    for ref in ghosts[2:]:
        h_ref[start : start + ref.shape[0], :] = ref[...]
        start += ref.shape[0]
    run_layer(16, near_ref, pool_ref, column_ref, h_ref, *views(weights_ref, spot), out_ref, *scratch)
    g_ref[...] = jnp.dot(out_ref[...], weights_ref[force_spot:, :], preferred_element_type=F32).astype(BF16)


def layer_scratch(nbasis, near, channels, atom_rows, pool_rows):
    half = near * TILE // 2
    return [
        pltpu.VMEM((atom_rows, 4 * channels), BF16),
        pltpu.VMEM((NHARM * TILE, channels), F32),
        *[pltpu.VMEM((2, NHARM - 1, TILE, half), BF16)] * 2,
        *[pltpu.VMEM((2, nbasis, TILE, half), BF16)] * 2,
        pltpu.VMEM((pool_rows, channels), BF16),
    ]


def list_blocks(near_ref, around_ref, atom_tiles, face_tiles, early_ref, late_ref):
    near = near_ref.shape[0]
    pool_tiles = atom_tiles + FACES * face_tiles
    spare = (5 * atom_tiles) * 128 + pool_tiles + FACES * face_tiles
    first_slab = atom_tiles + 2 * face_tiles

    def own(tile, counts):
        early, late = counts
        for k in range(near):
            other = near_ref[k, tile]
            entry = tile * 128 + other
            with_dom = ((other >= atom_tiles) & (other < first_slab)).astype(jnp.int32)
            early_ref[early] = entry
            late_ref[late] = entry
            early, late = early + 1 - with_dom, late + with_dom
        return early, late

    counts = lax.fori_loop(0, atom_tiles, own, (jnp.int32(0), jnp.int32(0)))

    def of_others(ref, pairs):
        def others(tile, count):
            for domain, face in pairs:
                start = atom_tiles + face * face_tiles
                for k in range(near):
                    other = around_ref[domain, k * atom_tiles + tile] - start
                    ref[count] = (atom_tiles * (domain + 1) + tile) * 128 + pool_tiles + face * face_tiles + other
                    count = count + ((other >= 0) & (other < face_tiles)).astype(jnp.int32)
            return count

        return others

    early = lax.fori_loop(0, atom_tiles, of_others(early_ref, ((2, 3), (3, 2))), counts[0])
    late = lax.fori_loop(0, atom_tiles, of_others(late_ref, ((0, 1), (1, 0))), counts[1])
    for extra in range(7):
        early_ref[early + extra] = spare
        late_ref[late + extra] = spare
    return early, late


def block_pair(first, second, atom_tiles, pool_ref, column_ref, gi_ref, gj_ref):
    scale = 1.0 / gi_ref.shape[1] ** 0.5
    lane = iota((8, LANES), 1)
    left = lane < TILE
    half = iota((TILE, LANES), 1) < TILE
    i_tiles = [pl.multiple_of((one >> 7) * TILE, TILE) for one in (first, second)]
    j_tiles = [one & 127 for one in (first, second)]
    same = [jnp.where((one >> 7 == one & 127) & (one >> 7 < atom_tiles), 0, 4096) for one in (first, second)]
    rows = jnp.where(left, same[0], same[1]) + (lane & (TILE - 1))
    columns = [column_ref[pl.ds(one, TILE), :] for one in i_tiles]
    mine = jnp.concatenate([gi_ref[pl.ds(one, TILE), :] for one in i_tiles], axis=0)
    others = jnp.concatenate([gj_ref[pl.ds(pl.multiple_of(one * TILE, TILE), TILE), :] for one in j_tiles], axis=0)
    inner = lax.dot_general(mine, others, (((1,), (1,)), ((), ())), preferred_element_type=F32)
    inner = jnp.where(half, inner[:TILE], inner[TILE:])
    offset = []
    for w in range(3):
        away = tall(jnp.where(left, pool_ref[j_tiles[0], w], pool_ref[j_tiles[1], w]), TILE // 8)
        offset.append(away - jnp.where(half, columns[0][:, w : w + 1], columns[1][:, w : w + 1]))
    square = offset[0] * offset[0] + offset[1] * offset[1] + offset[2] * offset[2] + SOFTENING
    inverse = lax.rsqrt(square)
    ratio = jnp.minimum(square * inverse * (1.0 / CUTOFF), 1.0)
    ratio = jnp.where(tall(rows, TILE // 8) == iota((TILE, LANES), 0), 1.0, ratio)
    fade = 1.0 - ratio * ratio
    strength = fade * fade * inverse * (inner * scale)
    return [strength * one for one in offset]


def sum_blocks(list_ref, count, atom_tiles, pool_ref, column_ref, gi_ref, gj_ref, own_ref, total_ref):
    own_ref[...] = jnp.zeros_like(own_ref)
    total_ref[...] = jnp.zeros_like(total_ref)
    left = iota((8, LANES), 1) < TILE
    half = iota((TILE, LANES), 1) < TILE

    def step(index, carry):
        entries = [list_ref[8 * index + spot] for spot in range(8)]
        found = [block_pair(entries[2 * p], entries[2 * p + 1], atom_tiles, pool_ref, column_ref, gi_ref, gj_ref) for p in range(4)]
        for p in range(4):
            for spot in range(2):
                entry = entries[2 * p + spot]
                i_tile, j_tile = jnp.minimum(entry >> 7, atom_tiles), entry & 127
                for w in range(3):
                    pair = found[p][w]
                    against = sum(pair[8 * v : 8 * v + 8] for v in range(TILE // 8))
                    total_ref[j_tile, w] -= jnp.where(left, against, 0.0) if spot == 0 else jnp.where(left, 0.0, against)
                    own_ref[i_tile, w] += jnp.where(half, pair, 0.0) if spot == 0 else jnp.where(half, 0.0, pair)
        return carry

    lax.fori_loop(0, (count + 7) // 8, step, 0)


def gather_forces(pick_ref, faces, atom_tiles, face_tiles, own_ref, total_ref):
    atom_rows = atom_tiles * TILE
    pool_tiles = atom_tiles + FACES * face_tiles
    half = iota((1, LANES), 1) < TILE
    sums = []
    for w in range(3):
        folded = jnp.sum(total_ref[:, w], axis=1)
        sums.append(folded + pltpu.roll(folded, TILE, 1))

    def row(tile):
        lines = [jnp.where(half, sums[w][tile : tile + 1], sums[w][tile + 1 : tile + 2]) for w in range(3)]
        return jnp.concatenate(lines + [jnp.zeros((5, LANES), F32)], axis=0)

    blocks = atom_rows // LANES
    shift = LANES.bit_length() - 1
    total = jnp.concatenate([row(2 * m) for m in range(blocks)], axis=0)
    for face in faces:
        for m in range(face_tiles // 2):
            pick = pick_ref[face : face + 1, m * LANES : (m + 1) * LANES]
            back = row(pool_tiles + face * face_tiles + 2 * m)
            high = pick >> shift
            wide = jnp.concatenate([jnp.where(high == one, back, 0.0) for one in range(blocks)], axis=0)
            onehot = (iota((LANES, LANES), 0) == (pick & (LANES - 1))).astype(F32).astype(BF16)
            for part in pieces(wide)[:2]:
                total = total + lax.dot_general(part, onehot, (((1,), (1,)), ((), ())), preferred_element_type=F32)
    total = jnp.concatenate([total[m * 8 : (m + 1) * 8] for m in range(blocks)], axis=1)
    for w in range(3):
        ones = (iota((8, LANES), 0) == w).astype(F32).astype(BF16)
        mine = jnp.concatenate([own_ref[tile, w] for tile in range(atom_tiles)], axis=0)
        for part in pieces(mine)[:2]:
            total = total + lax.dot_general(ones, part, (((1,), (1,)), ((), ())), preferred_element_type=F32)
    return total


def neighbour_kernel(n_dom, n_slab, cap, tiles, table_ref, around_ref, recv_ref, numbers_ref, pool_in, column_in, early_ref, late_ref, pool_ref, column_ref):
    near_ref = Near(table_ref, tiles)
    pick_ref = numbers_ref
    atom_rows, ghost_rows = column_in.shape[0], pick_ref.shape[1]
    atom_tiles, face_tiles = atom_rows // TILE, ghost_rows // TILE
    pool_tiles = atom_tiles + FACES * face_tiles
    me_slab = lax.axis_index("slab")
    before, after = lax.rem(me_slab + n_slab - 1, n_slab), lax.rem(me_slab + 1, n_slab)
    early, late = list_blocks(near_ref, around_ref, atom_tiles, face_tiles, early_ref.at[0], late_ref.at[0])
    early_ref[1, 0] = early
    late_ref[1, 0] = late
    column_ref[0:atom_rows, :] = column_in[...]
    column_ref[5 * atom_rows :, :] = jnp.full((TILE, 8), -AWAY, F32)
    per = TILE // cap
    spot = iota((TILE, 8), 1)

    def put(domain, tile, column):
        live = column[:, 3:4] > 0.5
        start = atom_rows * (domain + 1) + tile * TILE
        column_ref[start : start + TILE, :] = jnp.where((spot >= 3) | live, column, -AWAY)

    def tile_of(slab, tile):
        parts = [recv_ref[(tile * per + p) * n_slab + slab] for p in range(per)]
        return jnp.concatenate([one[:, start : start + cap] for start in (0, TILE) for one in parts], axis=1)

    for tile in range(atom_tiles):
        block = tile_of(me_slab, tile)
        put(0, tile, block.T[TILE:])
        put(1, tile, pltpu.roll(block, 4, 0).T[:TILE])
        below = tile_of(before, tile).T[:TILE]
        put(2, tile, below)
        put(3, tile, below if n_slab == 2 else tile_of(after, tile).T[:TILE])
    pool_ref[0:pool_tiles] = pool_in[...]
    pool_ref[pool_tiles + FACES * face_tiles] = jnp.full((3, 8, LANES), AWAY, F32)
    own = pieces(jnp.concatenate([recv_ref[e * n_slab + me_slab] for e in range(n_dom)], axis=0))
    shift = cap.bit_length() - 1
    half = iota((1, LANES), 1) < TILE
    for face in range(FACES):
        for m in range(ghost_rows // LANES):
            pick = pick_ref[face : face + 1, m * LANES : (m + 1) * LANES]
            total = find_rows(own, pick & (cap - 1), pick >> shift, n_dom)
            swapped = pltpu.roll(total, TILE, 1)
            tile = pool_tiles + face * face_tiles + 2 * m
            store_tile(jnp.where(half, total, swapped), tile, pool_ref)
            store_tile(jnp.where(half, swapped, total), tile + 1, pool_ref)


def near_forces_kernel(n_slab, list_ref, numbers_ref, taken_ref, pool_ref, column_ref, g_ref, *rest):
    pick_ref = numbers_ref
    slabs = rest[: 1 if n_slab == 2 else 2]
    part_ref, out_g_ref, gi_ref, gj_ref, own_ref, total_ref = rest[len(slabs) :]
    atom_rows, channels = g_ref.shape
    ghost_rows = pick_ref.shape[1]
    atom_tiles, face_tiles = atom_rows // TILE, ghost_rows // TILE
    pool_tiles = atom_tiles + FACES * face_tiles
    gi_ref[0:atom_rows, :] = g_ref[...]
    gj_ref[0:atom_rows, :] = g_ref[...]
    spare = jnp.zeros((TILE, channels), BF16)
    gi_ref[5 * atom_rows :, :] = spare
    gj_ref[(pool_tiles + FACES * face_tiles) * TILE :, :] = spare
    gi_ref[3 * atom_rows : 4 * atom_rows, :] = slabs[0][...]
    gi_ref[4 * atom_rows : 5 * atom_rows, :] = slabs[-1][...]
    gather_rows(pick_ref, [(face, g_ref, gj_ref, pool_tiles * TILE + face * ghost_rows) for face in range(FACES)])
    gather_rows(taken_ref, [(face, ref, gj_ref, atom_rows + face * ghost_rows) for face, ref in ((2, slabs[0]), (3, slabs[-1]))])
    out_g_ref[...] = gj_ref[pool_tiles * TILE : pool_tiles * TILE + 2 * ghost_rows, :]
    sum_blocks(list_ref.at[0], list_ref[1, 0], atom_tiles, pool_ref, column_ref, gi_ref, gj_ref, own_ref, total_ref)
    part_ref[...] = gather_forces(pick_ref, (2, 3), atom_tiles, face_tiles, own_ref, total_ref)


def far_forces_kernel(list_ref, numbers_ref, taken_ref, pool_ref, column_ref, g_ref, out_g_ref, first_ref, second_ref, part_ref, out_ref, gi_ref, gj_ref, own_ref, total_ref):
    pick_ref = numbers_ref
    atom_rows, channels = g_ref.shape
    ghost_rows = pick_ref.shape[1]
    atom_tiles, face_tiles = atom_rows // TILE, ghost_rows // TILE
    pool_tiles = atom_tiles + FACES * face_tiles
    spare = jnp.zeros((TILE, channels), BF16)
    gi_ref[0:atom_rows, :] = g_ref[...]
    even = is_even().astype(jnp.int32)
    spots = (even, 1 - even)
    for spot, ref in zip(spots, (first_ref, second_ref)):
        gi_ref[pl.ds(pl.multiple_of((1 + spot) * atom_rows, LANES), atom_rows), :] = ref[...]
    gi_ref[5 * atom_rows :, :] = spare
    gj_ref[pool_tiles * TILE : pool_tiles * TILE + 2 * ghost_rows, :] = out_g_ref[...]
    gj_ref[(pool_tiles + FACES * face_tiles) * TILE :, :] = spare
    gather_rows(taken_ref, [(face, ref, gj_ref, atom_rows + spots[face] * ghost_rows) for face, ref in ((0, first_ref), (1, second_ref))], even == 0)
    sum_blocks(list_ref.at[0], list_ref[1, 0], atom_tiles, pool_ref, column_ref, gi_ref, gj_ref, own_ref, total_ref)
    total = gather_forces(pick_ref, (0, 1), atom_tiles, face_tiles, own_ref, total_ref) + part_ref[...]
    out_ref[...] = total[0:3]


def passed_along(array, axis, by):
    count = lax.axis_size(axis)
    return lax.ppermute(array, axis, [(i, (i + by) % count) for i in range(count)])


def swapped(first, second):
    count = lax.axis_size("dom")
    ends = lax.ppermute(second, "dom", [(i, (i - 1 if i % 2 == 0 else i + 1) % count) for i in range(count)])
    return lax.ppermute(first, "dom", [(i, i + 1 if i % 2 == 0 else i - 1) for i in range(count)]), ends


def body(n_dom, n_slab, positions, species, send_pick, ghost_pick, near_tiles, embedding, radial_weight, update_weight, force_weight):
    atom_rows = positions.shape[0]
    cap = send_pick.shape[1]
    ghost_rows = ghost_pick.shape[1]
    tiles, near = near_tiles.shape
    channels = embedding.shape[1]
    nbasis = radial_weight.shape[1]
    pool_rows = atom_rows + FACES * ghost_rows
    face_rows = [ghost_rows, ghost_rows] + ([2 * ghost_rows] if n_slab == 2 else [ghost_rows, ghost_rows])
    n_out = len(face_rows)
    face_out = [jax.ShapeDtypeStruct((rows, channels), BF16) for rows in face_rows]
    face_tiles = ghost_rows // TILE
    i_rows = 5 * atom_rows + TILE
    j_tiles = pool_rows // TILE + FACES * face_tiles + 1
    longest = (near * tiles) * 5 + 8
    scratch = layer_scratch(nbasis, near, channels, atom_rows, pool_rows)

    sent, weights = send_states(n_dom, n_slab, positions, species, send_pick, ghost_pick, near_tiles, embedding, radial_weight, update_weight, force_weight)
    update_spot, force_spot = weight_spots(radial_weight.shape, update_weight.shape)
    spots = [(16 * m, nbasis, at, update_weight.shape[1]) for m, at in enumerate(update_spot)]
    got = lax.all_to_all(sent, ("dom", "slab"), split_axis=0, concat_axis=0, tiled=True)

    numbers, pool, column, around, taken, kept, hidden, *faces = pl.pallas_call(
        functools.partial(first_kernel, n_dom, n_slab, cap, n_out, spots[0], 16 * len(spots), force_spot + channels, (near, tiles)),
        out_shape=[
            jax.ShapeDtypeStruct((8, ghost_rows), jnp.int32),
            jax.ShapeDtypeStruct((pool_rows // TILE, 3, 8, LANES), F32),
            jax.ShapeDtypeStruct((atom_rows, 8), F32),
            jax.ShapeDtypeStruct((8, LANES), jnp.int32),
            jax.ShapeDtypeStruct((8, ghost_rows), jnp.int32),
            jax.ShapeDtypeStruct((force_spot + channels, channels), BF16),
            jax.ShapeDtypeStruct((atom_rows, channels), BF16),
        ]
        + face_out,
        in_specs=[VMEM] * 2,
        out_specs=[VMEM] * (7 + n_out),
        scratch_shapes=scratch + [pltpu.VMEM((8, pool_rows), F32), pltpu.SMEM((8, ghost_rows), jnp.int32), pltpu.SemaphoreType.DMA],
        compiler_params=params(),
        name="first_layer",
    )(got, weights)

    early, late, wide_pool, wide_column = pl.pallas_call(
        functools.partial(neighbour_kernel, n_dom, n_slab, cap, (near, tiles)),
        out_shape=[
            jax.ShapeDtypeStruct((2, longest), jnp.int32),
            jax.ShapeDtypeStruct((2, longest), jnp.int32),
            jax.ShapeDtypeStruct((j_tiles, 3, 8, LANES), F32),
            jax.ShapeDtypeStruct((i_rows, 8), F32),
        ],
        in_specs=[SMEM] * 2 + [VMEM] * 4,
        out_specs=[SMEM] * 2 + [VMEM] * 2,
        compiler_params=params(),
        name="neighbours",
    )(numbers, around, got, numbers, pool, column)
    faces = [*swapped(*faces[:2]), *(passed_along(one, "slab", way) for one, way in zip(faces[2:], (1, -1)))]
    features, mine = pl.pallas_call(
        functools.partial(second_kernel, n_out, spots[1], force_spot, (near, tiles)),
        out_shape=[jax.ShapeDtypeStruct((atom_rows, channels), BF16)] * 2,
        in_specs=[SMEM] * 2 + [VMEM] * (4 + n_out),
        out_specs=[VMEM] * 2,
        scratch_shapes=scratch,
        compiler_params=params(),
        name="second_layer",
    )(numbers, early, pool, column, hidden, faces[1], faces[0], *faces[2:], kept)

    slabs = [passed_along(mine, "slab", 1)]
    if n_slab != 2:
        slabs.append(passed_along(mine, "slab", -1))
    first, second = swapped(mine, mine)
    force_scratch = [
        pltpu.VMEM((i_rows, channels), BF16),
        pltpu.VMEM((j_tiles * TILE, channels), BF16),
        pltpu.VMEM((tiles + 1, 3, TILE, LANES), F32),
        pltpu.VMEM((j_tiles, 3, 8, LANES), F32),
    ]
    part, out_g = pl.pallas_call(
        functools.partial(near_forces_kernel, n_slab),
        out_shape=[jax.ShapeDtypeStruct((8, atom_rows), F32), jax.ShapeDtypeStruct((2 * ghost_rows, channels), BF16)],
        in_specs=[SMEM] + [VMEM] * (5 + len(slabs)),
        out_specs=[VMEM] * 2,
        scratch_shapes=force_scratch,
        cost_estimate=pl.CostEstimate(flops=4_000_000_000, bytes_accessed=4_000_000, transcendentals=0),
        compiler_params=params(),
        name="near_forces",
    )(early, numbers, taken, wide_pool, wide_column, mine, *slabs)
    forces = pl.pallas_call(
        far_forces_kernel,
        out_shape=jax.ShapeDtypeStruct((3, atom_rows), F32),
        in_specs=[SMEM] + [VMEM] * 9,
        out_specs=VMEM,
        scratch_shapes=force_scratch,
        compiler_params=params(),
        name="far_forces",
    )(late, numbers, taken, wide_pool, wide_column, mine, out_g, first, second, part)
    return features, forces


def solution(mesh):
    both = ("dom", "slab")
    return jax.shard_map(
        functools.partial(body, mesh.shape["dom"], mesh.shape["slab"]),
        mesh=mesh,
        in_specs=(P(both, None), P(both), P(both, None), P(both, None), P(both, None), P(), P(), P(), P()),
        out_specs=(P(both, None), P(None, both)),
        check_vma=False,
    )
```
